32 devices in a mesh: dp: 8 (over z, x), mp: 4 (over y, core).
Axes of the slice: x: 2, y: 2, z: 4, core: 2. Of those that a mesh axis runs over, the one named last changes fastest.
Arguments:
- token_owner: int32 [8192, 1], P('dp'), may hold values from 0 to 31; in each aligned block of 256 rows (0 to 255, 256 to 511, ...) at most 16 rows name the same one
- token_row: int32 [8192], P('dp'), may hold values from 0 to 2047
- long_len: int32 [8, 4], P('dp'), may hold values from 1 to 128, 384 in all within a row
- short_len: int32 [8, 16], P('dp'), may hold values from 1 to 32, 384 in all within a row
- pairing: int32 [160], replicated, may hold values from 0 to 159, each once
- embed_table: float32 [65536, 768], P(('dp', 'mp')), may hold values from -6 to 6
- first_moment: float32 [65536, 768], P(('dp', 'mp')), may hold values from -4 to 4
- second_moment: float32 [65536, 768], P(('dp', 'mp')), may hold values from 0.05 to 2
- heads_weight: bfloat16 [768, 3, 768], P(None, None, 'mp'), may hold values from -0.21875 to 0.21875
- mix_weight: bfloat16 [768, 768], P('mp'), may hold values from -0.625 to 0.625
- up_weight: bfloat16 [768, 3072], P(None, 'mp'), may hold values from -0.21875 to 0.21875
- down_weight: bfloat16 [3072, 768], P('mp'), may hold values from -0.109375 to 0.109375
- first_gain: float32 [768], replicated, may hold values from 0.1 to 1.9
- first_shift: float32 [768], replicated, may hold values from -4 to 4
- second_gain: float32 [768], replicated, may hold values from 0.1 to 1.9
- second_shift: float32 [768], replicated, may hold values from -4 to 4
- upper_grad: bfloat16 [8192, 768], P(('dp', 'mp')), may hold values from -6 to 6
Outputs:
- loss: float32 [], replicated
- block_out: bfloat16 [8192, 768], P(('dp', 'mp'))
- heads_grad: float32 [768, 3, 768], P(None, None, 'mp')
- mix_grad: float32 [768, 768], P('mp')
- up_grad: float32 [768, 3072], P(None, 'mp')
- down_grad: float32 [3072, 768], P('mp')
- first_gain_grad: float32 [768], replicated
- first_shift_grad: float32 [768], replicated
- second_gain_grad: float32 [768], replicated
- second_shift_grad: float32 [768], replicated
- table_step: float32 [65536, 768], P(('dp', 'mp'))
- first_new: float32 [65536, 768], P(('dp', 'mp'))
- second_new: float32 [65536, 768], P(('dp', 'mp'))
The draws below stay inside these ranges and needn't reach their ends.
Inputs may be any that keep to these rules, and one draw needn't show every extreme that they name: `token_owner`: in each aligned block of 256 tokens no owner is named by more than 16 tokens, and in some blocks one owner is named by exactly 16; every owner is named by some token.
All inputs are finite; a program needn't handle non-finite values.
Results may differ from the reference program's by a relative error of at most 0.012.
The reference program's roundings to bfloat16 on the way count: a program that leaves them out, or rounds other values in their place, can miss the bound.
Values may be sent and summed in bfloat16 or wider, within the bound.
A program may use at most 128 MiB of HBM per device.

```python
import math
import jax
import jax.numpy as jnp
import numpy as np
from jax import lax

D = 768
HEADS = 12
HEAD = 64
FF = 3072
ROWS_DEV = 2048
TOK_DEV = 256
LONG_LEN = 128
SHORT_LEN = 32
GROUP = 1024
TOKENS = 8192
LONG_G = 4
SHORT_G = 16
NSENT = 160
PAIRS = 80
VOCAB = 65536
CAP = 16
N_DP = 8
DEVICES = 32


def place_ends(drawn, own_key, smallest, largest):
    shape = drawn.shape
    index_at = [jax.random.randint(jax.random.fold_in(own_key, axis), (), 0, shape[axis]) for axis in range(len(shape))]
    drawn = drawn.at[tuple(index_at)].set(smallest)
    longest = shape.index(max(shape))
    index_at[longest] = (index_at[longest] + 1) % shape[longest]
    return drawn.at[tuple(index_at)].set(largest)


def block_scale(stream_key, extent, cuts, smallest, largest):
    def one(axis_at, parts):
        steps = jax.random.uniform(jax.random.fold_in(jax.random.fold_in(stream_key, 6), axis_at), (parts,), jnp.float32, smallest / len(cuts), largest / len(cuts))
        return jnp.repeat(jnp.exp(steps), extent[axis_at] // parts).reshape((-1,) + (1,) * (len(extent) - axis_at - 1))

    level = one(*cuts[0])
    for cut in cuts[1:]:
        level = level * one(*cut)
    return level


def profile(number_of, total, reach, skew):
    loads = [(1 << 20) // math.isqrt(grade ** skew) + 1 for grade in range(2, number_of + 1)]
    spare, given = total - reach - (number_of - 1), [1] * (number_of - 1)
    while spare > 0:
        free = [i for i in range(number_of - 1) if given[i] < reach]
        whole, budget = sum([loads[i] for i in free]), spare
        for i in free:
            addition = min(reach - given[i], max(1, budget * loads[i] // whole), spare)
            given[i] = given[i] + addition
            spare = spare - addition
    return np.array([reach] + given)


def uneven_parts(stream_key, number_of, total, bound, skew):
    if number_of == 2:
        one = jax.random.randint(stream_key, (), max(1, total - bound), min(bound, total - 1) + 1)
        return jnp.stack([one, total - one])
    tallies = jnp.asarray(profile(number_of, total, bound, skew), jnp.int32)
    pairs = (number_of - 1) // 2
    source_of, taker = tallies[1:1 + 2 * pairs:2], tallies[2:2 + 2 * pairs:2]
    margin = jnp.minimum(source_of - 1, bound - taker)
    moved = jax.random.randint(jax.random.fold_in(stream_key, 1), (pairs,), 0, 1 << 20) % (margin + 1)
    tallies = tallies.at[1:1 + 2 * pairs:2].set(source_of - moved).at[2:2 + 2 * pairs:2].set(taker + moved)
    return tallies[jax.random.permutation(jax.random.fold_in(stream_key, 2), number_of)]


def assign_block(rng, own, number, rows, count, top, reach, lean):
    sequence = jax.random.permutation(rng, count)
    packed, usual = shares(count, rows * top, reach, lean, True), shares(count, rows * top, reach, lean, False)
    places = jnp.arange(count)

    def named(sizes, offset_by):
        used = int((sizes > 0).sum())
        fixed = max(1, used // 4)
        shifted = fixed + (places - fixed + offset_by * (used - fixed)) % max(1, count - fixed)
        return jnp.zeros((count,), jnp.int32).at[sequence[jnp.where(places < fixed, places, shifted)]].set(jnp.asarray(sizes, jnp.int32))

    sizes = jnp.where(number % 4 == 0, named(packed, number // 4), named(usual, number - number // 4 - 1))
    mixed = jax.random.permutation(jax.random.fold_in(own, 3), count)
    donor, taker = mixed[0:count // 2 * 2:2], mixed[1:count // 2 * 2:2]
    room = jnp.minimum(sizes[donor] - 1, reach - sizes[taker]) // 2
    room = jnp.where((donor == sequence[0]) | (taker == sequence[0]) | (sizes[taker] == 0), 0, jnp.maximum(room, 0))
    shifted = jax.random.randint(jax.random.fold_in(own, 4), (count // 2,), 0, 1 << 20) % (room + 1)
    sizes = sizes.at[donor].add(-shifted).at[taker].add(shifted)
    labels = jnp.searchsorted(jnp.cumsum(sizes), jnp.arange(rows * top), side="right").astype(jnp.int32)
    grid = labels.reshape(top, rows).T
    grid = grid[jax.random.permutation(jax.random.fold_in(own, 1), rows)]
    offset_by = jax.random.randint(jax.random.fold_in(own, 2), (rows, 1), 0, top)
    return jnp.take_along_axis(grid, (jnp.arange(top)[None, :] + offset_by) % top, axis=1)


def shares(number_of, total, reach, slope, full):
    weights = [(1 << 20) // math.isqrt(grade ** slope) + 1 for grade in range(1, number_of + 1)]
    largest = reach if full else min(reach, max(-(-total // number_of), total * weights[0] // sum(weights)))
    least = 1 if total - largest >= number_of - 1 else 0
    given, spare = [largest] + [least] * (number_of - 1), total - largest - least * (number_of - 1)
    while spare > 0:
        candidates = [i for i in range(1, number_of) if given[i] < largest] or [i for i in range(1, number_of) if given[i] < reach]
        whole, remaining = sum([weights[i] for i in candidates]), spare
        for i in candidates:
            more = min(reach - given[i], max(1, remaining * weights[i] // whole), spare)
            given[i] = given[i] + more
            spare = spare - more
    return np.array(given)


def scatter_about(own_key, shape, deviation, most, shards=(), kind=jnp.bfloat16):
    level = block_scale(own_key, shape, shards, -0.22, 0.18) if shards else 1.0
    drawn = jax.random.normal(own_key, shape, jnp.float32) * deviation * level
    return jnp.minimum(jnp.maximum(drawn, -most), most).astype(kind)


def setup_inputs(seed: int = 0) -> dict:
    streams_of = jax.random.split(jax.random.key(seed), 18)
    token_owner_keys = jax.random.split(jax.random.fold_in(streams_of[0], 1), TOKENS // TOK_DEV)
    token_owner_turns = jax.random.permutation(jax.random.fold_in(streams_of[0], 3), TOKENS // TOK_DEV)
    token_owner = jax.vmap(lambda own, number: assign_block(jax.random.fold_in(streams_of[0], 2), own, number, TOK_DEV, DEVICES, 1, CAP, 2))(token_owner_keys, token_owner_turns).reshape((TOKENS, 1))
    token_row = place_ends(jax.random.randint(streams_of[1], (TOKENS,), 0, ROWS_DEV), jax.random.fold_in(streams_of[1], 1), 0, ROWS_DEV - 1).astype(jnp.int32)
    long_len = jax.vmap(lambda own: uneven_parts(own, LONG_G, LONG_G * LONG_LEN * 3 // 4, LONG_LEN, 1))(jax.random.split(streams_of[2], N_DP)).reshape((N_DP, LONG_G)).astype(jnp.int32)
    short_len = jax.vmap(lambda own: uneven_parts(own, SHORT_G, SHORT_G * SHORT_LEN * 3 // 4, SHORT_LEN, 1))(jax.random.split(streams_of[3], N_DP)).reshape((N_DP, SHORT_G)).astype(jnp.int32)
    pairing = jax.random.permutation(streams_of[4], NSENT).astype(jnp.int32)
    embed_table = scatter_about(streams_of[5], (VOCAB, D), 1.0, 6.0, ((0, 32),), jnp.float32)
    first_moment = scatter_about(streams_of[6], (VOCAB, D), 0.3, 4.0, ((0, 32),), jnp.float32)
    second_moment = jnp.clip(jnp.exp(math.log(2.0) - 3.6888794 * jax.random.uniform(streams_of[7], (VOCAB, D), jnp.float32) ** block_scale(streams_of[7], (VOCAB, D), ((0, 32),), -0.2, 0.2)), 0.05, 2.0)
    heads_weight = scatter_about(streams_of[8], (D, 3, D), D ** -0.5, 0.21875, ((2, 4),))
    mix_weight = scatter_about(streams_of[9], (D, D), (D // 8) ** -0.5, 0.625, ((0, 4),))
    up_weight = scatter_about(streams_of[10], (D, FF), D ** -0.5, 0.21875, ((1, 4),))
    down_weight = scatter_about(streams_of[11], (FF, D), FF ** -0.5, 0.109375, ((0, 4),))
    first_gain = jnp.clip(1.0 + 0.18 * jax.random.normal(streams_of[12], (D,), jnp.float32), 0.1, 1.9)
    first_shift = scatter_about(streams_of[13], (D,), 0.3, 4.0, (), jnp.float32)
    second_gain = jnp.clip(1.0 + 0.18 * jax.random.normal(streams_of[14], (D,), jnp.float32), 0.1, 1.9)
    second_shift = scatter_about(streams_of[15], (D,), 0.3, 4.0, (), jnp.float32)
    upper_grad = scatter_about(streams_of[16], (TOKENS, D), 1.0, 6.0, ((0, 32),))
    return {"token_owner": token_owner, "token_row": token_row, "long_len": long_len, "short_len": short_len, "pairing": pairing, "embed_table": embed_table, "first_moment": first_moment, "second_moment": second_moment, "heads_weight": heads_weight, "mix_weight": mix_weight, "up_weight": up_weight, "down_weight": down_weight, "first_gain": first_gain, "first_shift": first_shift, "second_gain": second_gain, "second_shift": second_shift, "upper_grad": upper_grad}


highest = lax.Precision.HIGHEST
first_fix = 1.0 - 0.9 ** 10
second_fix = 1.0 - 0.95 ** 10

@jax.custom_vjp
def low(v):
    return lax.optimization_barrier(v.astype(jnp.bfloat16)).astype(jnp.float32)

@jax.custom_vjp
def low_back(v):
    return v

def low_keep(v):
    return (low(v), None)

def low_pass(kept, grad):
    return (grad,)

def back_keep(v):
    return (v, None)

def back_low(kept, grad):
    return (low(grad),)
low.defvjp(low_keep, low_pass)
low_back.defvjp(back_keep, back_low)

def layer_norm(hidden, gain, shift):
    mean_value = lax.optimization_barrier(jnp.mean(hidden, axis=-1, keepdims=True))
    centered = hidden - mean_value
    variance = lax.optimization_barrier(jnp.mean(centered * centered, axis=-1, keepdims=True))
    return centered * lax.rsqrt(variance + 1e-12) * gain + shift

def ranking_loss(sentences, pairing):
    unit = sentences * lax.rsqrt(lax.optimization_barrier(jnp.sum(sentences * sentences, axis=1, keepdims=True)) + 1e-06)
    source = unit[pairing[0::2]]
    target = unit[pairing[1::2]]
    cosine = jnp.dot(source, target.T, precision=highest)
    count = cosine.shape[0]
    logits = 40.0 * (cosine - 0.3 * jnp.eye(count, dtype=jnp.float32))
    matched = jnp.diagonal(logits)
    forward_term = jnp.mean(jax.nn.logsumexp(logits, axis=1) - matched)
    backward_term = jnp.mean(jax.nn.logsumexp(logits, axis=0) - matched)
    return forward_term + backward_term

def attend_exact(query, key_part, value, lengths):
    size = query.shape[1]
    scores = low_back(jnp.einsum('sqhe,skhe->shqk', query, key_part, precision=highest) * 0.125)
    valid = jnp.arange(size, dtype=jnp.int32)[None, None, None, :] < lengths[:, None, None, None]
    probs = jax.nn.softmax(jnp.where(valid, scores, -jnp.inf), axis=-1)
    return jnp.einsum('shqk,skhe->sqhe', low(probs), value, precision=highest)

def group_forward(params, inputs, long_lengths, short_lengths):
    heads_w, mix_w, up_w, down_w, gain_one, shift_one, gain_two, shift_two = params
    half = GROUP // 2
    projected = low_back(low(jnp.dot(inputs, heads_w.reshape(D, 3 * D), precision=highest)))

    def long_kind(matrix):
        return matrix[:half].reshape(half // LONG_LEN, LONG_LEN, HEADS, HEAD)

    def short_kind(matrix):
        return matrix[half:].reshape(half // SHORT_LEN, SHORT_LEN, HEADS, HEAD)
    query = projected[:, :D]
    key_part = projected[:, D:2 * D]
    value = projected[:, 2 * D:]
    out_long = attend_exact(long_kind(query), long_kind(key_part), long_kind(value), long_lengths)
    out_short = attend_exact(short_kind(query), short_kind(key_part), short_kind(value), short_lengths)
    attended = low_back(low(jnp.concatenate([out_long.reshape(half, D), out_short.reshape(half, D)], axis=0)))
    first_hidden = inputs + low_back(jnp.dot(attended, mix_w, precision=highest))
    normed = layer_norm(first_hidden, gain_one, shift_one)
    up_pre = low_back(jnp.dot(low(normed), up_w, precision=highest))
    activated = low(jax.nn.gelu(up_pre, approximate=False))
    second_hidden = normed + low_back(jnp.dot(activated, down_w, precision=highest))
    block_rows = layer_norm(second_hidden, gain_two, shift_two)
    pooled = jnp.concatenate([block_rows[:half:LONG_LEN], block_rows[half::SHORT_LEN]], axis=0)
    return (block_rows, pooled)

def reference(token_owner, token_row, long_len, short_len, pairing, embed_table, first_moment, second_moment, heads_weight, mix_weight, up_weight, down_weight, first_gain, first_shift, second_gain, second_shift, upper_grad):
    token_ids = (token_owner[:, 0] * ROWS_DEV + token_row).astype(jnp.int32)
    params = tuple((item.astype(jnp.float32) for item in (heads_weight, mix_weight, up_weight, down_weight, first_gain, first_shift, second_gain, second_shift)))

    def forward(table, weights):
        inputs = low(table[token_ids]).reshape(N_DP, GROUP, D)

        def one_group(carry, pieces):
            return (carry, group_forward(weights, pieces[0], pieces[1], pieces[2]))
        carry, outs = lax.scan(jax.checkpoint(one_group), jnp.zeros((), jnp.float32), (inputs, long_len, short_len))
        block_rows, pooled = outs
        return (block_rows.reshape(TOKENS, D), ranking_loss(pooled.reshape(NSENT, D), pairing))
    results, backward = jax.vjp(forward, embed_table, params)
    block_rows, loss = results
    table_grad, weight_grads = backward((upper_grad.astype(jnp.float32), jnp.asarray(PAIRS, jnp.float32)))
    counts = jnp.zeros((VOCAB,), jnp.float32).at[token_ids].add(1.0)
    row_grad = table_grad / jnp.maximum(counts, 1.0)[:, None]
    first_new = 0.9 * first_moment + 0.1 * row_grad
    second_new = 0.95 * second_moment + 0.05 * row_grad * row_grad
    table_step = first_new / first_fix / (jnp.sqrt(second_new / second_fix) + 1e-08) + 0.01 * embed_table
    return (loss, block_rows.astype(jnp.bfloat16), weight_grads[0], weight_grads[1], weight_grads[2], weight_grads[3], weight_grads[4], weight_grads[5], weight_grads[6], weight_grads[7], table_step, first_new, second_new)
```

```python
import functools
from types import SimpleNamespace

import jax
import jax.numpy as jnp
from jax import lax
from jax.experimental import pallas as pl
from jax.experimental.pallas import tpu as pltpu
from jax.sharding import PartitionSpec as P

HEAD = 64
LONG_LEN = 128
SHORT_LEN = 32
BLOCK = 128
SLOTS = 16
MESH = pl.DeviceIdType.MESH
bf16 = jnp.bfloat16
f32 = jnp.float32
i32 = jnp.int32

first_fix = 1.0 - 0.9**10
second_fix = 1.0 - 0.95**10


def nn(left, right):
    return lax.dot_general(left, right, (((1,), (0,)), ((), ())), preferred_element_type=f32)


def nt(left, right):
    return lax.dot_general(left, right, (((1,), (1,)), ((), ())), preferred_element_type=f32)


def tn(left, right):
    return lax.dot_general(left, right, (((0,), (0,)), ((), ())), preferred_element_type=f32)


def iota(shape, axis):
    return lax.broadcasted_iota(i32, shape, axis)


def column_of(row):
    count = row.shape[1]
    eye = iota((count, count), 0) == iota((count, count), 1)
    return jnp.sum(jnp.where(eye, row, 0.0), axis=1, keepdims=True)


def mean_of(values):
    return jnp.mean(values, axis=-1, keepdims=True)


def norm_forward(hidden):
    centered = hidden - mean_of(hidden)
    scale = lax.rsqrt(mean_of(centered * centered) + 1e-12)
    return centered * scale, scale


def norm_back(grad, normal, scale, gain):
    scaled = grad * gain
    return scale * (scaled - mean_of(scaled) - normal * mean_of(scaled * normal))


class Net:
    def __init__(self, send_sems, recv_sems):
        self.send_sems, self.recv_sems = send_sems, recv_sems
        self.count = 0
        self.open = []

    def send(self, src, dst, device):
        at = self.count
        self.count += 1
        copy = pltpu.make_async_remote_copy(
            src_ref=src,
            dst_ref=dst,
            send_sem=self.send_sems.at[at],
            recv_sem=self.recv_sems.at[at],
            device_id=device,
            device_id_type=MESH,
        )
        copy.start()
        self.open.append(copy)
        return copy

    def sent(self, copy):
        copy.wait_send()
        self.open = [item for item in self.open if item is not copy]

    def drain(self):
        for copy in self.open:
            copy.wait_send()
        self.open = []


class Reduce:
    def __init__(self, net, part, whole, land, place, bits):
        self.net, self.part, self.whole, self.land = net, part, whole, land
        self.data_pos, self.model_pos = place
        self.bits = bits
        rows, width = part.shape
        self.half = width // 2
        self.row, self.len = 0, rows
        self.offset = 0
        self.stage = 0
        self.halved = []
        grows = sum(1 for stage in range(len(bits)) if self.halves(stage))
        self.todo = [self.add] * len(bits) + [self.grow] * grows

    def step(self):
        self.todo.pop(0)()

    def halves(self, stage):
        return stage == 0 or (self.part.shape[0] >> (stage - 1)) % 32 == 0

    def partner(self, bit):
        mine = lax.rem(lax.div(self.data_pos, 1 << bit), 2)
        return mine, (self.data_pos + (1 - 2 * mine) * (1 << bit), self.model_pos)

    def start(self):
        mine, device = self.partner(self.bits[self.stage])
        halved = self.halves(self.stage)
        count = self.len
        if self.stage == 0:
            away = pl.multiple_of((1 - mine) * self.half, 128)
            self.col = pl.multiple_of(mine * self.half, 128)
            src = self.part.at[:, pl.ds(away, self.half)]
        else:
            away = self.row
            if halved:
                count = self.len // 2
                away = pl.multiple_of(self.row + (1 - mine) * count, 16)
                self.row = pl.multiple_of(self.row + mine * count, 16)
                self.len = count
            src = self.part.at[pl.ds(away, count), pl.ds(self.col, self.half)]
        self.halved.append(halved)
        self.now = self.land.at[pl.ds(self.offset, count)]
        self.offset += count
        self.copy = self.net.send(src, self.now, device)

    def add(self):
        self.copy.wait_recv()
        last = self.stage == len(self.bits) - 1
        if not self.halved[-1]:
            self.net.sent(self.copy)
        target = self.whole if last else self.part
        cols = pl.ds(self.col, self.half)
        step = 48
        now, row, part = self.now, self.row, self.part

        def tile(at, carry):
            here = pl.multiple_of(at * step, 16)
            there = pl.ds(pl.multiple_of(row + here, 16), step)
            total = part[there, cols].astype(f32) + now[pl.ds(here, step), :].astype(f32)
            target[there, cols] = total.astype(bf16)
            return carry

        lax.fori_loop(0, self.len // step, tile, 0)
        if last:
            self.spread()
        else:
            self.stage += 1
            self.start()

    def spread(self):
        while self.stage and not self.halved[self.stage]:
            self.stage -= 1
        _, device = self.partner(self.bits[self.stage])
        rows = pl.ds(self.row, self.len) if self.stage else slice(None)
        here = self.whole.at[rows, pl.ds(self.col, self.half)]
        self.copy = self.net.send(here, here, device)

    def grow(self):
        self.copy.wait_recv()
        if self.stage == 0:
            return
        mine, _ = self.partner(self.bits[self.stage])
        self.row = pl.multiple_of(self.row - mine * self.len, 16)
        self.len *= 2
        self.stage -= 1
        self.spread()


def layer_kernel(
    dims,
    owner_ref,
    rowid_ref,
    long_ref,
    short_ref,
    pairing_ref,
    gain_one_ref,
    shift_one_ref,
    gain_two_ref,
    shift_two_ref,
    table_hbm,
    heads_hbm,
    mix_hbm,
    up_hbm,
    down_hbm,
    upper_hbm,
    block_out,
    weight_out,
    norm_out,
    loss_out,
    incoming_out,
    ids_out,
    *scratch,
):
    n_data, n_model = dims.n_data, dims.n_model
    s = SimpleNamespace(**dict(zip(dims.names, scratch, strict=True)))
    group_rows = dims.tok * n_model
    s.partial = s.stage
    s.gproj = s.table.at[pl.ds(0, group_rows)]
    s.gp = s.table.at[pl.ds(group_rows, group_rows)]
    s.outgoing = s.found
    s.incoming = s.returned
    tok, width, cols, pad, ff = dims.tok, dims.width, dims.cols, dims.pad, dims.ff
    devices = n_data * n_model
    group = tok * n_model
    chunks = tok // BLOCK
    span = BLOCK * n_model
    slots = devices * SLOTS
    table_rows = table_hbm.shape[0]
    d = lax.axis_index("dp")
    m = lax.axis_index("mp")
    me = d * n_model + m
    core = lax.rem(m, 2)
    side = lax.div(m, 2)
    m1 = m + 1 - 2 * core
    m2 = m + 2 - 4 * side
    m3 = m1 + m2 - m
    by_core = (d, m1)
    by_side = (d, m2)
    net = Net(s.send_sems, s.recv_sems)

    def at_device(place):
        return (lax.div(place, n_model), lax.rem(place, n_model))

    def other(j):
        return lax.rem(me + j, devices)

    barrier = pltpu.get_barrier_semaphore()

    def greet(j, carry):
        pl.semaphore_signal(barrier, inc=1, device_id=at_device(other(j)), device_id_type=MESH)
        return carry

    lax.fori_loop(1, devices, greet, 0)

    stage_rows = s.stage.shape[1]
    table_parts = table_rows // stage_rows

    def table_copy(at):
        return pltpu.make_async_copy(
            table_hbm.at[pl.ds(at * stage_rows, stage_rows)],
            s.stage.at[at % 2],
            s.load_sems.at[at % 2],
        )

    table_copy(0).start()
    table_copy(1).start()
    loads = []

    def load(src, dst):
        copy = pltpu.make_async_copy(src, dst, s.load_sems.at[2 + len(loads)])
        copy.start()
        loads.append(copy)

    wt, mixw, upw, downw = s.wt, s.mixw, s.upw, s.downw
    for part in range(3):
        load(heads_hbm.at[pl.ds(part * cols, cols)], wt.at[pl.ds(part * pad, cols)])
        wt[pl.ds(part * pad + cols, pad - cols), :] = jnp.zeros((pad - cols, width), bf16)
    load(mix_hbm, mixw.at[pl.ds(0, cols)])
    mixw[pl.ds(cols, pad - cols), :] = jnp.zeros((pad - cols, width), bf16)
    load(up_hbm, upw)
    load(down_hbm, downw)
    load(upper_hbm, s.upper)

    own_at = pl.multiple_of(m * tok, 128)
    owner_row = owner_ref[:, pl.ds(own_at, tok)]
    rowid_row = rowid_ref[:, pl.ds(own_at, tok)]
    owned = iota((devices, tok), 0) == owner_row
    before = (iota((tok, tok), 0) < iota((tok, tok), 1)).astype(f32).astype(bf16)
    counted = nn(owned.astype(f32).astype(bf16), before)
    rank_row = jnp.sum(jnp.where(owned, counted, 0.0), axis=0, keepdims=True)
    slot_row = owner_row.astype(f32) * SLOTS + rank_row
    slot_row_int = slot_row.astype(i32)
    wanted_row = (rowid_row + 1).astype(f32)
    step = min(slots, 256)

    def place_slots(at, carry):
        here = pl.ds(pl.multiple_of(at * step, step), step)
        placed = iota((step, tok), 0) + at * step == slot_row_int
        wanted = jnp.sum(jnp.where(placed, wanted_row, 0.0), axis=1, keepdims=True)
        high = jnp.floor(wanted * (1.0 / 64.0))
        low = wanted - 64.0 * high
        s.ask[here, :] = jnp.where(iota((step, 128), 1) < 64, high, low).astype(bf16)
        s.place[here, :] = placed.astype(f32).astype(bf16)
        return carry

    lax.fori_loop(0, slots // step, place_slots, 0)
    slot_col = column_of(slot_row).astype(i32)
    s.pick[...] = (iota((tok, slots), 1) == slot_col).astype(f32).astype(bf16)

    pl.semaphore_wait(barrier, devices - 1)

    def slot_rows(place):
        return pl.ds(pl.multiple_of(place * SLOTS, SLOTS), SLOTS)

    def swap_copy(src, dst, sems, to):
        send_sems, recv_sems = sems
        return pltpu.make_async_remote_copy(
            src_ref=src.at[slot_rows(to)],
            dst_ref=dst.at[slot_rows(me)],
            send_sem=send_sems.at[to],
            recv_sem=recv_sems.at[me],
            device_id=at_device(to),
            device_id_type=MESH,
        )

    def arrival(dst, sems, place):
        send_sems, recv_sems = sems
        return pltpu.make_async_remote_copy(
            src_ref=dst.at[slot_rows(place)],
            dst_ref=dst.at[slot_rows(place)],
            send_sem=send_sems.at[place],
            recv_sem=recv_sems.at[place],
            device_id=at_device(place),
            device_id_type=MESH,
        )

    def swap_start(src, dst, sems):
        def one(j, carry):
            swap_copy(src, dst, sems, other(j)).start()
            return carry

        lax.fori_loop(1, devices, one, 0)
        dst[slot_rows(me), :] = src[slot_rows(me), :]

    def swap_arrived(dst, sems):
        def one(j, carry):
            arrival(dst, sems, other(j)).wait_recv()
            return carry

        lax.fori_loop(1, devices, one, 0)

    def swap_sent(dst, sems):
        def one(j, carry):
            arrival(dst, sems, other(j)).wait_send()
            return carry

        lax.fori_loop(1, devices, one, 0)

    ask_sems = (s.ask_send, s.ask_recv)
    row_sems = (s.row_send, s.row_recv)
    out_sems = (s.out_send, s.out_recv)
    swap_start(s.ask, s.asked, ask_sems)
    for at in range(table_parts):
        table_copy(at).wait()
        s.table[pl.ds(at * stage_rows, stage_rows), :] = s.stage[at % 2].astype(bf16)
        if at + 2 < table_parts:
            table_copy(at + 2).start()
    swap_arrived(s.asked, ask_sems)

    per_block = BLOCK // SLOTS

    def look(at, carry):
        block = lax.rem(lax.div(me, per_block) + at, slots // BLOCK)
        rows = pl.ds(pl.multiple_of(block * BLOCK, BLOCK), BLOCK)
        asked = s.asked[rows, :].astype(f32)
        ident = asked[:, 0:1] * 64.0 + asked[:, 64:65] - 1.0
        eye = iota((BLOCK, BLOCK), 0) == iota((BLOCK, BLOCK), 1)
        ident_row = jnp.sum(jnp.where(eye, ident, 0.0), axis=0, keepdims=True)
        ids_out[:, rows] = jnp.broadcast_to(ident_row.astype(i32), (8, BLOCK))
        hot = (iota((BLOCK, table_rows), 1) == ident.astype(i32)).astype(f32).astype(bf16)
        s.found[rows, :] = nn(hot, s.table[...]).astype(bf16)

        def one(i, inner):
            to = block * per_block + lax.rem(lax.rem(me, per_block) + i, per_block)

            @pl.when(to != me)
            def _():
                swap_copy(s.found, s.returned, row_sems, to).start()

            return inner

        lax.fori_loop(0, per_block, one, 0)
        return carry

    lax.fori_loop(0, slots // BLOCK, look, 0)
    s.returned[slot_rows(me), :] = s.found[slot_rows(me), :]
    for copy in loads:
        copy.wait()
    swap_arrived(s.returned, row_sems)

    def rows_of(model, k):
        return pl.ds(pl.multiple_of(k * span + model * BLOCK, BLOCK), BLOCK)

    def own_rows(k):
        return pl.ds(k * BLOCK, BLOCK)

    class Gather:
        def __init__(self, buffer, k):
            self.buffer, self.k = buffer, k
            mine = buffer.at[rows_of(m, k)]
            self.far = net.send(mine, mine, by_side)
            self.near = net.send(mine, mine, by_core)

        def forward(self):
            self.far.wait_recv()
            there = self.buffer.at[rows_of(m2, self.k)]
            self.passed = net.send(there, there, by_core)

        def finish(self):
            self.near.wait_recv()
            self.passed.wait_recv()

    class Scatter:
        last = {}

        def __init__(self, k):
            self.k = k
            for copy in Scatter.last.get(k, []):
                net.sent(copy)
            part = s.partial.at[k]
            self.near = []
            for r, model in ((0, m3), (1, m1)):
                here = pl.ds(pl.multiple_of(model * BLOCK, BLOCK), BLOCK)
                s.near_send[k, r] = part[here, :].astype(bf16)
                self.near.append(
                    net.send(s.near_send.at[k, r], s.near_land.at[k, r], by_core)
                )

        def middle(self):
            k = self.k
            self.near[0].wait_recv()
            here = pl.ds(pl.multiple_of(m2 * BLOCK, BLOCK), BLOCK)
            total = s.partial[k, here, :] + s.near_land[k, 0].astype(f32)
            s.far_send[k] = total.astype(bf16)
            self.far = net.send(s.far_send.at[k], s.far_land.at[k], by_side)
            Scatter.last[k] = self.near + [self.far]

        def end(self):
            k = self.k
            self.near[1].wait_recv()
            here = pl.ds(pl.multiple_of(m * BLOCK, BLOCK), BLOCK)
            total = s.partial[k, here, :] + s.near_land[k, 1].astype(f32)
            self.far.wait_recv()
            return total + s.far_land[k].astype(f32)

    def tiles(total, step, fn):
        def one(at, carry):
            fn(pl.multiple_of(at * step, step))
            return carry

        lax.fori_loop(0, total // step, one, 0)

    x, proj, att, probs = s.x, s.proj, s.att, s.probs
    gathers = []
    for k in range(chunks):
        own = nn(s.pick[own_rows(k), :], s.returned[...])
        x[rows_of(m, k), :] = own.astype(bf16)
        gathers.append(Gather(x, k))

    lane = iota((BLOCK, BLOCK), 1)
    sub = iota((BLOCK, BLOCK), 0)
    first_half = lane < HEAD
    head_masks = [
        (lane < HEAD).astype(f32).astype(bf16),
        (lane >= HEAD).astype(f32).astype(bf16),
    ]
    heads = cols // HEAD
    long_blocks = n_model // 2
    per_long = tok // LONG_LEN
    per_short = tok // SHORT_LEN
    short_in_block = BLOCK // SHORT_LEN

    def key_mask(model, k, is_long):
        if is_long:
            return lane < long_ref[0, model * per_long + k]
        keep = None
        for j in range(short_in_block):
            size = short_ref[0, (model - long_blocks) * per_short + k * short_in_block + j]
            start = j * SHORT_LEN
            ok = (lane >= start) & (lane < start + size) & (sub >= start) & (sub < start + SHORT_LEN)
            keep = ok if keep is None else keep | ok
        return keep

    def head_parts(source, rows, h, part):
        g = h // 2
        return source[rows, pl.ds(part * pad + g * BLOCK, BLOCK)]

    def attend(k):
        def project(at):
            rows = pl.ds(pl.multiple_of(k * span + at, 256), 256)
            proj[rows, :] = nt(x[rows, :], wt[...]).astype(bf16)

        tiles(span, 256, project)

        def block(is_long, model):
            rows = rows_of(model, k)
            keep = key_mask(model, k, is_long)
            outs = []
            for h in range(heads):
                query = head_parts(proj, rows, h, 0) * head_masks[h % 2]
                scores = nt(query, head_parts(proj, rows, h, 1)) * 0.125
                scores = jnp.where(keep, scores, -1e30)
                weights = jnp.exp(scores - jnp.max(scores, axis=1, keepdims=True))
                weights = weights / jnp.sum(weights, axis=1, keepdims=True)
                probs[k, model, h] = weights
                outs.append(nn(weights.astype(bf16), head_parts(proj, rows, h, 2)))
            for g in range(pad // BLOCK):
                second = outs[2 * g + 1] if 2 * g + 1 < heads else jnp.zeros((BLOCK, BLOCK), f32)
                both = jnp.where(first_half, outs[2 * g], second)
                att[rows, pl.ds(g * BLOCK, BLOCK)] = both.astype(bf16)

        for is_long, low_model in ((True, 0), (False, long_blocks)):
            def one(at, carry, is_long=is_long, low_model=low_model):
                block(is_long, low_model + at)
                return carry

            lax.fori_loop(0, long_blocks, one, 0)

        def mix(at):
            rows = pl.ds(pl.multiple_of(k * span + at, 256), 256)
            s.partial[k, pl.ds(at, 256), :] = nn(att[rows, :], mixw[...])

        tiles(span, 256, mix)

    def pipeline(gathers, work, before=None, after=None, forwarded=None):
        scatters = []
        for k in range(chunks):
            if gathers:
                gathers[k].forward()
            if forwarded is not None:
                forwarded(k)
            if k:
                scatters[k - 1].middle()
            if gathers:
                gathers[k].finish()
            if before is not None:
                before(k)
            work(k)
            scatters.append(Scatter(k))
            if after is not None:
                after(k)
        scatters[-1].middle()
        return scatters

    scatters = pipeline(gathers, attend)

    gain_one, shift_one, gain_two, shift_two = [
        ref[...].reshape(1, width)
        for ref in (gain_one_ref, shift_one_ref, gain_two_ref, shift_two_ref)
    ]
    norm, act, slope = s.norm, s.act, s.slope
    gathers = []
    for k in range(chunks):
        hidden = x[rows_of(m, k), :].astype(f32) + scatters[k].end()
        normal, scale = norm_forward(hidden)
        s.normal_one[own_rows(k), :] = normal
        s.scale_one[own_rows(k), :] = jnp.broadcast_to(scale, (BLOCK, 128))
        normed = normal * gain_one + shift_one
        s.normed[own_rows(k), :] = normed
        norm[rows_of(m, k), :] = normed.astype(bf16)
        gathers.append(Gather(norm, k))

    def feed(k):
        def one(at):
            rows = pl.ds(pl.multiple_of(k * span + at, 128), 128)
            pre = nn(norm[rows, :], upw[...])
            cumulative = 0.5 * (1.0 + lax.erf(pre * 0.7071067811865476))
            act[rows, :] = (pre * cumulative).astype(bf16)
            slope[rows, :] = cumulative + pre * (0.3989422804014327 * jnp.exp(-0.5 * pre * pre))

        tiles(span, 128, one)

        def two(at):
            rows = pl.ds(pl.multiple_of(k * span + at, 256), 256)
            s.partial[k, pl.ds(at, 256), :] = nn(act[rows, :], downw[...])

        tiles(span, 256, two)

    scatters = pipeline(gathers, feed)

    for k in range(chunks):
        hidden = s.normed[own_rows(k), :] + scatters[k].end()
        normal, scale = norm_forward(hidden)
        s.normal_two[own_rows(k), :] = normal
        s.scale_two[own_rows(k), :] = jnp.broadcast_to(scale, (BLOCK, 128))
        rows_now = normal * gain_two + shift_two
        s.rows[own_rows(k), :] = rows_now
        block_out[own_rows(k), :] = rows_now.astype(bf16)

    gb, gp, gm, gproj = s.gb, s.gp, s.gm, s.gproj

    def second_back(k):
        rows = own_rows(k)
        return norm_back(
            s.grad_rows[rows, :], s.normal_two[rows, :], s.scale_two[rows, 0:1], gain_two
        )

    s.grad_rows[...] = s.upper[...].astype(f32)
    gathers = []
    for k in range(chunks):
        gb[rows_of(m, k), :] = second_back(k).astype(bf16)
        gathers.append(Gather(gb, k))

    pool = s.pool
    half = width // 2
    firsts = jnp.concatenate(
        [s.rows[pl.ds(i * SHORT_LEN, 1), :] for i in range(per_short)], axis=0
    )
    pool[d, m] = jnp.concatenate([firsts[:, :half], firsts[:, half:]], axis=0).astype(bf16)

    def pool_copy(j):
        return pltpu.make_async_remote_copy(
            src_ref=pool.at[d, m],
            dst_ref=pool.at[d, m],
            send_sem=s.pool_send.at[j],
            recv_sem=s.pool_recv.at[j],
            device_id=(lax.rem(d + j, n_data), m),
            device_id_type=MESH,
        )

    def pool_start(j, carry):
        pool_copy(j).start()
        return carry

    def pool_arrived(j, carry):
        pool_copy(j).wait_recv()
        return carry

    def pool_sent(j, carry):
        pool_copy(j).wait_send()
        return carry

    lax.fori_loop(1, n_data, pool_start, 0)
    lax.fori_loop(1, n_data, pool_arrived, 0)
    far = net.send(pool.at[:, m], pool.at[:, m], by_side)
    near = net.send(pool.at[:, m], pool.at[:, m], by_core)
    far.wait_recv()
    passed = net.send(pool.at[:, m2], pool.at[:, m2], by_core)
    near.wait_recv()
    passed.wait_recv()


    count = devices * per_short
    sentences = dims.longs + dims.shorts
    pairs2 = pairing_ref.shape[1]

    def sentence_of(index):
        place = lax.div(index, per_short)
        slot = lax.rem(index, per_short)
        model = lax.rem(place, n_model)
        data = lax.div(place, n_model)
        ratio = LONG_LEN // SHORT_LEN
        is_long = model < long_blocks
        valid = jnp.logical_or(jnp.logical_not(is_long), lax.rem(slot, ratio) == 0)
        number = jnp.where(
            is_long,
            model * per_long + lax.div(slot, ratio),
            dims.longs + (model - long_blocks) * per_short + slot,
        )
        return jnp.where(valid, data * sentences + number, -1)

    group_rows_first = n_model * per_short

    def unfold(at, carry):
        part = pool[at].astype(f32)
        here = pl.ds(pl.multiple_of(at * group_rows_first, 16), group_rows_first)
        s.left[here, :] = part[:, :per_short, :].reshape(group_rows_first, half).astype(bf16)
        s.right[here, :] = part[:, per_short:, :].reshape(group_rows_first, half).astype(bf16)
        return carry

    lax.fori_loop(0, n_data, unfold, 0)
    gram, known = s.gram, s.known
    pair_col = column_of(pairing_ref[...].astype(f32)).astype(i32)
    step = 256 if count <= 256 else 128

    def measure(number, carry):
        at = number * step
        block = pl.ds(pl.multiple_of(at, 128), step)
        gram[:, block] = nt(s.left[...], s.left[block, :]) + nt(
            s.right[...], s.right[block, :]
        )
        sent = sentence_of(iota((1, step), 1) + at)
        place = jnp.sum(
            jnp.where(pair_col == sent, iota((pairs2, step), 0), 0).astype(f32),
            axis=0,
            keepdims=True,
        )
        place = jnp.where(sent >= 0, place, -2.0)
        pair = jnp.floor(place * 0.5)
        eye = iota((step, step), 0) == iota((step, step), 1)
        square = jnp.sum(jnp.where(eye, gram[block, block], 0.0), axis=0, keepdims=True)
        known[0:1, block] = lax.rsqrt(square + 1e-06)
        known[1:2, block] = pair
        known[2:3, block] = jnp.where(sent >= 0, place - 2.0 * pair, 5.0)
        for i in range(3):
            s.known_col[block, i : i + 1] = column_of(known[i : i + 1, block])
        return carry

    lax.fori_loop(0, count // step, measure, 0)

    def logits_of(part, block, inv_col, pair_col, side_col):
        inv_row, pair_row, side_row = known[0:1, block], known[1:2, block], known[2:3, block]
        facing = side_col + side_row == 1.0
        same = (pair_col == pair_row) & facing
        cosine = part * inv_col * inv_row
        return 40.0 * (cosine - jnp.where(same, 0.3, 0.0)), facing, same

    def lose(number, loss):
        block = pl.ds(pl.multiple_of(number * step, 128), step)
        logits, facing, same = logits_of(
            gram[:, block],
            block,
            s.known_col[:, 0:1],
            s.known_col[:, 1:2],
            s.known_col[:, 2:3],
        )
        masked = jnp.where(facing, logits, -1e30)
        top = jnp.max(masked, axis=0, keepdims=True)
        total = jnp.sum(jnp.where(facing, jnp.exp(masked - top), 0.0), axis=0, keepdims=True)
        valid = known[1:2, block] >= 0.0
        log_total = jnp.where(valid, top + jnp.log(jnp.where(valid, total, 1.0)), 0.0)
        known[3:4, block] = log_total
        matched = jnp.sum(jnp.where(same, logits, 0.0), axis=0, keepdims=True)
        return loss + jnp.sum(log_total - matched, axis=1, keepdims=True)

    loss = lax.fori_loop(0, count // step, lose, jnp.zeros((1, 1), f32))
    loss_out[...] = jnp.broadcast_to(loss * (2.0 / pairs2), loss_out.shape)

    own_first = pl.ds(pl.multiple_of(me * per_short, 8), per_short)
    mine_mask = iota((per_short, count), 1) == iota((per_short, count), 0) + me * per_short

    def own_col(row):
        return jnp.sum(jnp.where(mine_mask, row, 0.0), axis=1, keepdims=True)

    inv_row, log_row = known[0:1, :], known[3:4, :]
    inv_own, log_own = own_col(inv_row), own_col(log_row)
    logits, facing, same = logits_of(
        gram[own_first, :],
        slice(None),
        inv_own,
        own_col(known[1:2, :]),
        own_col(known[2:3, :]),
    )
    pull = jnp.exp(jnp.where(facing, logits - log_own, -1e30)) + jnp.exp(
        jnp.where(facing, logits - log_row, -1e30)
    )
    pull = 40.0 * (pull - jnp.where(same, 2.0, 0.0)) * inv_row
    pull_high = pull.astype(bf16)
    pull_low = (pull - pull_high.astype(f32)).astype(bf16)
    grad_unit = jnp.concatenate(
        [nn(pull_high, n[...]) + nn(pull_low, n[...]) for n in (s.left, s.right)], axis=1
    )
    unit = firsts * inv_own
    grad_firsts = inv_own * (
        grad_unit - unit * jnp.sum(unit * grad_unit, axis=1, keepdims=True)
    )
    grad_rows = s.grad_rows
    for i in range(per_short):
        at = pl.ds(i * SHORT_LEN, 1)
        grad_rows[at, :] = grad_rows[at, :] + grad_firsts[i : i + 1, :]


    norm_sum = s.norm_sum
    norm_sum[0] = jnp.zeros((8, width), f32)
    for k in range(chunks):
        s.second[own_rows(k), :] = second_back(k)
    patch = s.patch
    firsts = jnp.concatenate(
        [s.second[pl.ds(i * SHORT_LEN, 1), :] for i in range(per_short)], axis=0
    )
    patch[m] = jnp.concatenate([firsts[:, :half], firsts[:, half:]], axis=0).astype(bf16)
    far = net.send(patch.at[m], patch.at[m], by_side)
    near = net.send(patch.at[m], patch.at[m], by_core)
    for k in range(chunks):
        grad = grad_rows[own_rows(k), :]
        normal = s.normal_two[own_rows(k), :]
        norm_sum[0, 2:3, :] = norm_sum[0, 2:3, :] + jnp.sum(grad * normal, axis=0, keepdims=True)
        norm_sum[0, 3:4, :] = norm_sum[0, 3:4, :] + jnp.sum(grad, axis=0, keepdims=True)
    for k in range(chunks):
        gathers[k].forward()
    far.wait_recv()
    passed = net.send(patch.at[m2], patch.at[m2], by_core)
    for k in range(chunks):
        gathers[k].finish()
        net.sent(gathers[k].far)
        net.sent(gathers[k].near)
        net.sent(gathers[k].passed)
    near.wait_recv()
    passed.wait_recv()
    top_row = iota((16, width), 0) == 0
    per_chunk = BLOCK // SHORT_LEN

    def mend(model, carry):
        fresh = patch[model].astype(f32)
        for i in range(per_short):
            at = (i // per_chunk) * span + model * BLOCK + (i % per_chunk) * SHORT_LEN
            rows = pl.ds(pl.multiple_of(at, 16), 16)
            new = jnp.concatenate(
                [fresh[i : i + 1], fresh[per_short + i : per_short + i + 1]], axis=1
            )
            gb[rows, :] = jnp.where(top_row, new, gb[rows, :].astype(f32)).astype(bf16)
        return carry

    lax.fori_loop(0, n_model, mend, 0)

    def feed_back(k):
        def one(at):
            rows = pl.ds(pl.multiple_of(k * span + at, 128), 128)
            gp[rows, :] = (nt(gb[rows, :], downw[...]) * slope[rows, :]).astype(bf16)

        tiles(span, 128, one)

        def two(at):
            rows = pl.ds(pl.multiple_of(k * span + at, 256), 256)
            s.partial[k, pl.ds(at, 256), :] = nt(gp[rows, :], upw[...])

        tiles(span, 256, two)

    def weight_grad(target, base, rows, left, right, left_at=0):
        step = 64

        def one(at):
            part = tn(left[:, pl.ds(pl.multiple_of(left_at + at, 64), step)], right[...])
            target[pl.ds(pl.multiple_of(base + at, 16), step), :] = part.astype(bf16)

        tiles(rows, step, one)

    def whole_grad(target, base, left, right, keep=None):
        total = left.shape[1]
        for at in range(0, total, 256):
            part = tn(left[:, at : at + 256], right[...]).astype(bf16)
            size = 256 if keep is None else keep
            target[pl.ds(base + (at // 256) * size, size), :] = part[:size]

    bits = tuple(range(n_data.bit_length() - 1))
    half_rows = width // 2
    reduces = [
        Reduce(
            net,
            s.grads.at[pl.ds(i * half_rows, half_rows)],
            s.sums.at[pl.ds(i * half_rows, half_rows)],
            s.sum_land.at[i],
            (d, m),
            bits,
        )
        for i in range(6)
    ]
    downs, ups, heads_sums = reduces[0:2], reduces[2:4], reduces[4:6]

    def steps(*order):
        for at in order:
            reduces[at].step()

    def begin(items, base, left, right):
        for i, item in enumerate(items):
            for at in range(i * half_rows, (i + 1) * half_rows, half_rows):
                part = tn(left[:, at : at + half_rows], right[...])
                s.grads[pl.ds(base + at, half_rows), :] = part.astype(bf16)
            item.start()

    begin(downs, 0, act, gb)
    scatters = pipeline([], feed_back)
    begin(ups, width, norm, gp)
    gathers = []
    for k in range(chunks):
        grad = s.second[own_rows(k), :] + scatters[k].end()
        normal = s.normal_one[own_rows(k), :]
        norm_sum[0, 0:1, :] = norm_sum[0, 0:1, :] + jnp.sum(grad * normal, axis=0, keepdims=True)
        norm_sum[0, 1:2, :] = norm_sum[0, 1:2, :] + jnp.sum(grad, axis=0, keepdims=True)
        back = norm_back(grad, normal, s.scale_one[own_rows(k), 0:1], gain_one)
        s.second[own_rows(k), :] = back
        gm[rows_of(m, k), :] = back.astype(bf16)
        gathers.append(Gather(gm, k))
        steps(0)

    def attend_back(k):
        def unmix(at):
            rows = pl.ds(pl.multiple_of(k * span + at, 256), 256)
            s.gatt[rows, :] = nt(gm[rows, :], mixw[...]).astype(bf16)

        tiles(span, 256, unmix)

        def block(model, carry):
            rows = rows_of(model, k)
            parts = ([], [], [])
            for h in range(heads):
                g = h // 2
                mask = head_masks[h % 2]
                grad_out = s.gatt[rows, pl.ds(g * BLOCK, BLOCK)] * mask
                weights = probs[k, model, h]
                grad_probs = nt(grad_out, head_parts(proj, rows, h, 2))
                inner = jnp.sum(weights * grad_probs, axis=1, keepdims=True)
                grad_scores = (weights * (grad_probs - inner)).astype(bf16)
                parts[0].append(nn(grad_scores, head_parts(proj, rows, h, 1)) * 0.125)
                parts[1].append(tn(grad_scores, head_parts(proj, rows, h, 0)) * 0.125)
                parts[2].append(tn(weights.astype(bf16), grad_out))
            for part in range(3):
                for g in range(pad // BLOCK):
                    outs = parts[part]
                    zero = jnp.zeros((BLOCK, BLOCK), f32)
                    second = outs[2 * g + 1] if 2 * g + 1 < heads else zero
                    both = jnp.where(first_half, outs[2 * g], second)
                    gproj[rows, pl.ds(part * pad + g * BLOCK, BLOCK)] = both.astype(bf16)
            return carry

        lax.fori_loop(0, n_model, block, 0)

        def one(at):
            rows = pl.ds(pl.multiple_of(k * span + at, 256), 256)
            s.partial[k, pl.ds(at, 256), :] = nn(gproj[rows, :], wt[...])

        tiles(span, 256, one)

    def forwarded(k):
        if k == 0:
            steps(1)

    def before_attend(k):
        if k == chunks - 1:
            steps(2)

    def after_attend(k):
        if k == 0:
            steps(0, 1)

    scatters = pipeline(gathers, attend_back, before_attend, after_attend, forwarded)
    steps(0, 1, 2)
    whole_grad(s.grads, 2 * width, att, gm, cols)
    whole_grad(s.grads, 2 * width + cols, gproj, x, cols)
    for item in heads_sums:
        item.start()
    steps(3, 0, 2, 1)
    swap_sent(s.returned, row_sems)
    for k in range(chunks):
        grad = s.second[own_rows(k), :] + scatters[k].end()
        s.grad_in[own_rows(k), :] = grad.astype(bf16)

    def pack(at):
        rows = pl.ds(at, 256)
        s.outgoing[rows, :] = nn(s.place[rows, :], s.grad_in[...]).astype(bf16)

    tiles(slots, 256, pack)
    swap_start(s.outgoing, s.incoming, out_sems)

    stages = [by_core, by_side]
    for bit in bits:
        stages.append(reduces[0].partner(bit)[1])

    def norm_step(at):
        copy = net.send(norm_sum.at[at], s.norm_land.at[at], stages[at])
        copy.wait_recv()
        norm_sum[at + 1] = norm_sum[at] + s.norm_land[at]

    order = [3, 1, 2, 3, 4, 2, 4, 5, 3, 4, 5, 3, 0, 1, 4, 5, 2, 4, 5, 3, 5, 4, 5]
    turn = 0
    while turn < len(stages) or any(item.todo for item in reduces):
        if turn < len(stages):
            norm_step(turn)
        if not order:
            order = [i for i, item in enumerate(reduces) if item.todo]
        for at in order[:4]:
            if reduces[at].todo:
                steps(at)
        order = order[4:]
        turn += 1
    norm_out[...] = norm_sum[len(stages)]
    swap_arrived(s.incoming, out_sems)
    outs = [
        pltpu.make_async_copy(s.sums, weight_out, s.load_sems.at[0]),
        pltpu.make_async_copy(s.incoming, incoming_out, s.load_sems.at[1]),
    ]
    for copy in outs:
        copy.start()
    for copy in outs:
        copy.wait()
    net.drain()
    lax.fori_loop(1, n_data, pool_sent, 0)
    swap_sent(s.asked, ask_sems)
    swap_sent(s.incoming, out_sems)


def table_kernel(
    cols,
    ids_ref,
    norm_ref,
    loss_ref,
    incoming_hbm,
    weights_hbm,
    table_hbm,
    first_hbm,
    second_hbm,
    step_hbm,
    first_out,
    second_out,
    down_out,
    up_out,
    mix_out,
    heads_out,
    loss_out,
    *rest,
):
    norm_outs = rest[:4]
    incoming, low, wide, state, in_sems, out_sems, low_sems, wide_sems = rest[4:]
    slots, width = incoming.shape
    parts = in_sems.shape[1]
    rows = state.shape[1] // parts

    def tile(at):
        return pl.ds(pl.multiple_of(at * rows, 8), rows)

    def load(i, at):
        src = (first_hbm, second_hbm, table_hbm)[i]
        return pltpu.make_async_copy(
            src.at[tile(at)], state.at[i, tile(at)], in_sems.at[i, at]
        )

    def store(i, at):
        dst = (first_out, second_out, step_hbm)[i]
        return pltpu.make_async_copy(
            state.at[i, tile(at)], dst.at[tile(at)], out_sems.at[i, at]
        )

    def each_part(step):
        def one(at, carry):
            for i in range(3):
                step(i, at)
            return carry

        lax.fori_loop(0, parts, one, 0)

    named = pltpu.make_async_copy(incoming_hbm, incoming, low_sems.at[0])
    named.start()
    lows = []
    for i in range(3):
        here = pl.ds(i * width, width)
        lows.append(
            pltpu.make_async_copy(weights_hbm.at[here], low.at[here], low_sems.at[1 + i])
        )
    for copy in lows[:1]:
        copy.start()
    each_part(lambda i, at: load(i, at).start())
    for copy in lows[1:]:
        copy.start()
    loss_out[...] = loss_ref[0:1, 0:1]
    for i, out in enumerate(norm_outs):
        out[...] = norm_ref[i, :]
    named.wait()

    wides = []
    starts = (0, width, 2 * width, 2 * width + cols, 3 * width)
    for i, out in enumerate((down_out, up_out, mix_out, heads_out)):
        here = pl.ds(starts[i], starts[i + 1] - starts[i])
        wides.append(pltpu.make_async_copy(wide.at[here], out, wide_sems.at[i]))

    def widen(i):
        lows[i].wait()
        step = 96

        def one(at, carry):
            here = pl.ds(pl.multiple_of(i * width + at * step, 16), step)
            wide[here, :] = low[here, :].astype(f32)
            return carry

        lax.fori_loop(0, width // step, one, 0)
        for copy in wides[i : i + 1] if i < 2 else wides[2:]:
            copy.start()

    widen(0)

    def update(at, carry):
        for i in range(3):
            load(i, at).wait()
        here = tile(at)
        hot = (iota((rows, slots), 0) + at * rows == ids_ref[0:1, :]).astype(f32)
        uses = jnp.sum(hot, axis=1, keepdims=True)
        row_grad = nn(hot.astype(bf16), incoming[...]) * (1.0 / jnp.maximum(uses, 1.0))
        first_new = 0.9 * state[0, here, :] + 0.1 * row_grad
        second_new = 0.95 * state[1, here, :] + 0.05 * row_grad * row_grad
        state[0, here, :] = first_new
        state[1, here, :] = second_new
        scale = jnp.sqrt(second_new * (1.0 / second_fix)) + 1e-08
        state[2, here, :] = first_new * (1.0 / first_fix) / scale + 0.01 * state[2, here, :]
        for i in range(3):
            store(i, at).start()
        return carry

    lax.fori_loop(0, parts, update, 0)
    widen(1)
    widen(2)
    each_part(lambda i, at: store(i, at).wait())
    for copy in wides:
        copy.wait()


def body(
    token_owner,
    token_row,
    long_len,
    short_len,
    pairing,
    embed_table,
    first_moment,
    second_moment,
    heads_weight,
    mix_weight,
    up_weight,
    down_weight,
    first_gain,
    first_shift,
    second_gain,
    second_shift,
    upper_grad,
):
    tok, width = upper_grad.shape
    n_model, n_data = lax.axis_size("mp"), lax.axis_size("dp")
    devices = n_model * n_data
    group = tok * n_model
    cols = heads_weight.shape[2]
    pad = -(-cols // BLOCK) * BLOCK
    ff = up_weight.shape[1]
    slots = devices * SLOTS
    chunks = tok // BLOCK
    span = BLOCK * n_model
    per_short = tok // SHORT_LEN
    firsts = devices * per_short
    table_rows = embed_table.shape[0]
    bits = n_data.bit_length() - 1
    n_sems = 96 + 16 * bits
    vmem = pltpu.VMEM
    dma = pltpu.SemaphoreType.DMA
    shapes = dict(
        stage=vmem((chunks, span, width), f32),
        table=vmem((table_rows, width), bf16),
        wt=vmem((3 * pad, width), bf16),
        mixw=vmem((pad, width), bf16),
        upw=vmem((width, ff), bf16),
        downw=vmem((ff, width), bf16),
        upper=vmem((tok, width), bf16),
        ask=vmem((slots, 128), bf16),
        asked=vmem((slots, 128), bf16),
        place=vmem((slots, tok), bf16),
        pick=vmem((tok, slots), bf16),
        found=vmem((slots, width), bf16),
        returned=vmem((slots, width), bf16),
        x=vmem((group, width), bf16),
        proj=vmem((group, 3 * pad), bf16),
        att=vmem((group, pad), bf16),
        gatt=vmem((group, pad), bf16),
        probs=vmem((chunks, n_model, cols // HEAD, BLOCK, BLOCK), f32),
        near_send=vmem((chunks, 2, BLOCK, width), bf16),
        near_land=vmem((chunks, 2, BLOCK, width), bf16),
        far_send=vmem((chunks, BLOCK, width), bf16),
        far_land=vmem((chunks, BLOCK, width), bf16),
        normal_one=vmem((tok, width), f32),
        scale_one=vmem((tok, 128), f32),
        normed=vmem((tok, width), f32),
        norm=vmem((group, width), bf16),
        act=vmem((group, ff), bf16),
        slope=vmem((group, ff), f32),
        normal_two=vmem((tok, width), f32),
        scale_two=vmem((tok, 128), f32),
        rows=vmem((tok, width), f32),
        grad_rows=vmem((tok, width), f32),
        patch=vmem((n_model, 2 * per_short, width // 2), bf16),
        pool=vmem((n_data, n_model, 2 * per_short, width // 2), bf16),
        left=vmem((firsts, width // 2), bf16),
        right=vmem((firsts, width // 2), bf16),
        gram=vmem((firsts, firsts), f32),
        known=vmem((8, firsts), f32),
        known_col=vmem((firsts, 128), f32),
        gb=vmem((group, width), bf16),
        gm=vmem((group, width), bf16),
        second=vmem((tok, width), f32),
        grad_in=vmem((tok, width), bf16),
        norm_sum=vmem((3 + bits, 8, width), f32),
        norm_land=vmem((2 + bits, 8, width), f32),
        grads=vmem((3 * width, width), bf16),
        sums=vmem((3 * width, width), bf16),
        sum_land=vmem((6, width, width // 2), bf16),
        send_sems=dma((n_sems,)),
        recv_sems=dma((n_sems,)),
        load_sems=dma((16,)),
        ask_send=dma((devices,)),
        ask_recv=dma((devices,)),
        row_send=dma((devices,)),
        row_recv=dma((devices,)),
        out_send=dma((devices,)),
        out_recv=dma((devices,)),
        pool_send=dma((n_data,)),
        pool_recv=dma((n_data,)),
    )
    dims = SimpleNamespace(
        n_data=n_data,
        n_model=n_model,
        names=tuple(shapes),
        tok=tok,
        width=width,
        cols=cols,
        pad=pad,
        ff=ff,
        longs=long_len.shape[1],
        shorts=short_len.shape[1],
    )
    in_vmem = pl.BlockSpec(memory_space=pltpu.VMEM)
    in_smem = pl.BlockSpec(memory_space=pltpu.SMEM)
    in_hbm = pl.BlockSpec(memory_space=pl.ANY)
    heads_rows = jnp.transpose(heads_weight, (1, 2, 0)).reshape(3 * cols, width)
    block_out, weights, norms, loss, incoming, ids = pl.pallas_call(
        functools.partial(layer_kernel, dims),
        out_shape=(
            jax.ShapeDtypeStruct((tok, width), bf16),
            jax.ShapeDtypeStruct((3 * width, width), bf16),
            jax.ShapeDtypeStruct((8, width), f32),
            jax.ShapeDtypeStruct((8, 128), f32),
            jax.ShapeDtypeStruct((slots, width), bf16),
            jax.ShapeDtypeStruct((8, slots), i32),
        ),
        in_specs=[in_vmem, in_vmem, in_smem, in_smem] + [in_vmem] * 5 + [in_hbm] * 6,
        out_specs=(in_vmem, in_hbm, in_vmem, in_vmem, in_hbm, in_vmem),
        scratch_shapes=list(shapes.values()),
        compiler_params=pltpu.CompilerParams(
            collective_id=0, has_side_effects=True, vmem_limit_bytes=63 * 2**20
        ),
    )(
        token_owner.reshape(1, group),
        token_row.reshape(1, group),
        long_len,
        short_len,
        pairing.reshape(1, -1),
        first_gain,
        first_shift,
        second_gain,
        second_shift,
        embed_table,
        heads_rows,
        mix_weight,
        up_weight,
        down_weight,
        upper_grad,
    )
    parts = 8
    whole = jax.ShapeDtypeStruct((table_rows, width), f32)
    table_step, first_new, second_new, down_grad, up_grad, mix_grad, heads_grad, loss, *norm_grads = (
        pl.pallas_call(
            functools.partial(table_kernel, cols),
            out_shape=(whole, whole, whole)
            + tuple(
                jax.ShapeDtypeStruct((rows, width), f32) for rows in (ff, width, cols, 3 * cols)
            )
            + (jax.ShapeDtypeStruct((1, 1), f32),)
            + (jax.ShapeDtypeStruct((width,), f32),) * 4,
            in_specs=[in_vmem] * 3 + [in_hbm] * 5,
            out_specs=(in_hbm,) * 7 + (in_vmem,) * 5,
            scratch_shapes=[
                vmem((slots, width), bf16),
                vmem((3 * width, width), bf16),
                vmem((3 * width, width), f32),
                vmem((3, table_rows, width), f32),
                dma((3, parts)),
                dma((3, parts)),
                dma((4,)),
                dma((4,)),
            ],
            compiler_params=pltpu.CompilerParams(vmem_limit_bytes=63 * 2**20),
        )(ids, norms, loss, incoming, weights, embed_table, first_moment, second_moment)
    )
    return (
        loss.reshape(()),
        block_out,
        jnp.transpose(heads_grad.reshape(3, cols, width), (2, 0, 1)),
        mix_grad,
        up_grad,
        down_grad,
        *norm_grads,
        table_step,
        first_new,
        second_new,
    )


def solution(mesh):
    rows = P(("dp", "mp"), None)
    in_specs = (
        P("dp", None),
        P("dp"),
        P("dp", None),
        P("dp", None),
        P(),
        rows,
        rows,
        rows,
        P(None, None, "mp"),
        P("mp", None),
        P(None, "mp"),
        P("mp", None),
        P(),
        P(),
        P(),
        P(),
        rows,
    )
    out_specs = (
        P(),
        rows,
        P(None, None, "mp"),
        P("mp", None),
        P(None, "mp"),
        P("mp", None),
        P(),
        P(),
        P(),
        P(),
        rows,
        rows,
        rows,
    )
    return jax.shard_map(body, mesh=mesh, in_specs=in_specs, out_specs=out_specs, check_vma=False)
```

```python
import functools
from types import SimpleNamespace

import jax
import jax.numpy as jnp
from jax import lax
from jax.experimental import pallas as pl
from jax.experimental.pallas import tpu as pltpu
from jax.sharding import PartitionSpec as P

HEAD = 64
LONG_LEN = 128
SHORT_LEN = 32
BLOCK = 128
SLOTS = 16
NORM = -1
MESH = pl.DeviceIdType.MESH
bf16 = jnp.bfloat16
f32 = jnp.float32
i32 = jnp.int32

first_fix = 1.0 - 0.9**10
second_fix = 1.0 - 0.95**10


def nn(left, right):
    return lax.dot_general(left, right, (((1,), (0,)), ((), ())), preferred_element_type=f32)


def nt(left, right):
    return lax.dot_general(left, right, (((1,), (1,)), ((), ())), preferred_element_type=f32)


def tn(left, right):
    return lax.dot_general(left, right, (((0,), (0,)), ((), ())), preferred_element_type=f32)


def iota(shape, axis):
    return lax.broadcasted_iota(i32, shape, axis)


def column_of(row):
    count = row.shape[1]
    eye = iota((count, count), 0) == iota((count, count), 1)
    return jnp.sum(jnp.where(eye, row, 0.0), axis=1, keepdims=True)


def mean_of(values):
    return jnp.mean(values, axis=-1, keepdims=True)


def norm_forward(hidden):
    centered = hidden - mean_of(hidden)
    scale = lax.rsqrt(mean_of(centered * centered) + 1e-12)
    return centered * scale, scale


def norm_back(grad, normal, scale, gain):
    scaled = grad * gain
    return scale * (scaled - mean_of(scaled) - normal * mean_of(scaled * normal))


class Net:
    def __init__(self, send_sems, recv_sems):
        self.send_sems, self.recv_sems = send_sems, recv_sems
        self.open = [None] * send_sems.shape[0]
        self.count = 0
        self.names = {}

    def send(self, src, dst, device, name=None):
        slot = self.count % len(self.open)
        if self.open[slot] is not None:
            self.open[slot].wait_send()
        at = self.names.setdefault(self.count if name is None else name, len(self.names))
        self.count += 1
        copy = pltpu.make_async_remote_copy(
            src_ref=src,
            dst_ref=dst,
            send_sem=self.send_sems.at[slot],
            recv_sem=self.recv_sems.at[at],
            device_id=device,
            device_id_type=MESH,
        )
        copy.start()
        self.open[slot] = copy
        return copy

    def sent(self, copy):
        for slot, item in enumerate(self.open):
            if item is copy:
                copy.wait_send()
                self.open[slot] = None

    def drain(self):
        for copy in self.open:
            if copy is not None:
                copy.wait_send()
        self.open = [None] * len(self.open)


class Reduce:
    def __init__(self, net, part, whole, land, place, bits):
        self.net, self.part, self.whole, self.land = net, part, whole, land
        self.data_pos, self.model_pos = place
        self.bits = bits
        rows, width = part.shape
        self.half = width // 2
        self.row, self.len = 0, rows
        self.offset = 0
        self.stage = 0
        self.halved = []
        grows = sum(1 for stage in range(len(bits)) if self.halves(stage))
        self.todo = [self.add] * len(bits) + [self.grow] * grows

    def step(self):
        if self.todo:
            self.todo.pop(0)()

    def halves(self, stage):
        return stage == 0 or (self.part.shape[0] >> (stage - 1)) % 32 == 0

    def partner(self, bit):
        mine = lax.rem(lax.div(self.data_pos, 1 << bit), 2)
        return mine, (self.data_pos + (1 - 2 * mine) * (1 << bit), self.model_pos)

    def start(self):
        mine, device = self.partner(self.bits[self.stage])
        halved = self.halves(self.stage)
        count = self.len
        if self.stage == 0:
            away = pl.multiple_of((1 - mine) * self.half, 128)
            self.col = pl.multiple_of(mine * self.half, 128)
            src = self.part.at[:, pl.ds(away, self.half)]
        else:
            away = self.row
            if halved:
                count = self.len // 2
                away = pl.multiple_of(self.row + (1 - mine) * count, 16)
                self.row = pl.multiple_of(self.row + mine * count, 16)
                self.len = count
            src = self.part.at[pl.ds(away, count), pl.ds(self.col, self.half)]
        self.halved.append(halved)
        self.now = self.land.at[pl.ds(self.offset, count)]
        self.offset += count
        self.copy = self.net.send(src, self.now, device)

    def add(self):
        self.copy.wait_recv()
        last = self.stage == len(self.bits) - 1
        if not self.halved[-1]:
            self.net.sent(self.copy)
        target = self.whole if last else self.part
        cols = pl.ds(self.col, self.half)
        step = 48 if self.len % 48 == 0 else min(self.len, 64)
        now, row, part = self.now, self.row, self.part

        def tile(at, carry):
            here = pl.multiple_of(at * step, 16)
            there = pl.ds(pl.multiple_of(row + here, 16), step)
            total = part[there, cols].astype(f32) + now[pl.ds(here, step), :].astype(f32)
            target[there, cols] = total.astype(bf16)
            return carry

        lax.fori_loop(0, self.len // step, tile, 0)
        if last:
            self.spread()
        else:
            self.stage += 1
            self.start()

    def spread(self):
        while self.stage and not self.halved[self.stage]:
            self.stage -= 1
        _, device = self.partner(self.bits[self.stage])
        rows = pl.ds(self.row, self.len) if self.stage else slice(None)
        here = self.whole.at[rows, pl.ds(self.col, self.half)]
        self.copy = self.net.send(here, here, device)

    def grow(self):
        self.copy.wait_recv()
        if self.stage == 0:
            return
        mine, _ = self.partner(self.bits[self.stage])
        self.row = pl.multiple_of(self.row - mine * self.len, 16)
        self.len *= 2
        self.stage -= 1
        self.spread()


def layer_kernel(
    dims,
    owner_hbm,
    rowid_hbm,
    long_hbm,
    short_hbm,
    pairing_hbm,
    gain_one_hbm,
    shift_one_hbm,
    gain_two_hbm,
    shift_two_hbm,
    table_hbm,
    heads_hbm,
    mix_hbm,
    up_hbm,
    down_hbm,
    upper_hbm,
    first_hbm,
    second_hbm,
    block_out,
    norm_out,
    loss_out,
    *rest,
):
    resident = dims.resident
    if resident:
        sums, step_out, first_out, second_out, *scratch = rest
    else:
        weight_out, incoming_out, ids_hbm, *scratch = rest
    n_data, n_model = dims.n_data, dims.n_model
    s = SimpleNamespace(**dict(zip(dims.names, scratch, strict=True)))
    tok, width, cols, pad, ff = dims.tok, dims.width, dims.cols, dims.pad, dims.ff
    devices = n_data * n_model
    group = tok * n_model
    chunks = tok // BLOCK
    span = BLOCK * n_model
    slots = devices * SLOTS
    table_rows = table_hbm.shape[0]

    if resident:
        wide_a, wide_b = first_out, second_out
    else:
        wide_a, wide_b, sums = s.wide_a, s.wide_b, s.sums
    slope = wide_a.at[pl.ds(0, group)]
    partial = [wide_a.at[pl.ds(group + k * span, span)] for k in range(chunks)]
    s.normal_one, s.normed, s.normal_two, s.rows, s.grad_rows, s.second = [
        wide_b.at[pl.ds(i * tok, tok)] for i in range(6)
    ]
    s.gproj = s.table.at[pl.ds(0, group)]
    s.gp = s.table.at[pl.ds(group, group)]
    s.outgoing = s.found
    s.incoming = s.returned
    d = lax.axis_index("dp")
    m = lax.axis_index("mp")
    me = d * n_model + m
    core = lax.rem(m, 2)
    side = lax.div(m, 2)
    m1 = m + 1 - 2 * core
    m2 = m + 2 - 4 * side
    m3 = m1 + m2 - m
    by_core = (d, m1)
    by_side = (d, m2)
    net = Net(s.send_sems, s.recv_sems)

    def at_device(place):
        return (lax.div(place, n_model), lax.rem(place, n_model))

    def other(j):
        return lax.rem(me + j, devices)

    owner_ref, rowid_ref, long_ref, short_ref = s.owner, s.rowid, s.long, s.short
    pairing_ref = s.pairing
    small = [
        pltpu.make_async_copy(src, dst, s.small_sems.at[i])
        for i, (src, dst) in enumerate(
            (
                (owner_hbm, s.owner),
                (rowid_hbm, s.rowid),
                (long_hbm, s.long),
                (short_hbm, s.short),
                (pairing_hbm, s.pairing),
                (gain_one_hbm, s.gain_one),
                (shift_one_hbm, s.shift_one),
                (gain_two_hbm, s.gain_two),
                (shift_two_hbm, s.shift_two),
            )
        )
    ]
    for copy in small:
        copy.start()

    barrier = pltpu.get_barrier_semaphore()

    def greet(j, carry):
        pl.semaphore_signal(barrier, inc=1, device_id=at_device(other(j)), device_id_type=MESH)
        return carry

    lax.fori_loop(1, devices, greet, 0)

    stage_rows = table_rows // 4 if resident else span
    table_parts = table_rows // stage_rows

    def table_part(at):
        if resident:
            return step_out.at[pl.ds(at * stage_rows, stage_rows)]
        return partial[at % 2]

    def table_copy(at):
        return pltpu.make_async_copy(
            table_hbm.at[pl.ds(at * stage_rows, stage_rows)],
            table_part(at),
            s.table_sems.at[at],
        )

    ahead = table_parts if resident else 2
    for at in range(ahead):
        table_copy(at).start()
    loads = []

    def load(src, dst):
        copy = pltpu.make_async_copy(src, dst, s.load_sems.at[len(loads)])
        copy.start()
        loads.append(copy)

    wt, mixw, upw, downw = s.wt, s.mixw, s.upw, s.downw
    for part in range(3):
        load(heads_hbm.at[pl.ds(part * cols, cols)], wt.at[pl.ds(part * pad, cols)])
        wt[pl.ds(part * pad + cols, pad - cols), :] = jnp.zeros((pad - cols, width), bf16)
    load(mix_hbm, mixw.at[pl.ds(0, cols)])
    mixw[pl.ds(cols, pad - cols), :] = jnp.zeros((pad - cols, width), bf16)
    load(up_hbm, upw)
    load(down_hbm, downw)
    load(upper_hbm, s.upper)

    for copy in small:
        copy.wait()
    own_at = pl.multiple_of(m * tok, 128)
    owner_row = owner_ref[:, pl.ds(own_at, tok)]
    rowid_row = rowid_ref[:, pl.ds(own_at, tok)]
    owned = iota((devices, tok), 0) == owner_row
    before = (iota((tok, tok), 0) < iota((tok, tok), 1)).astype(f32).astype(bf16)
    counted = nn(owned.astype(f32).astype(bf16), before)
    rank_row = jnp.sum(jnp.where(owned, counted, 0.0), axis=0, keepdims=True)
    slot_row = owner_row.astype(f32) * SLOTS + rank_row
    slot_row_int = slot_row.astype(i32)
    wanted_row = (rowid_row + 1).astype(f32)
    step = min(slots, 256)

    def place_slots(at, carry):
        here = pl.ds(pl.multiple_of(at * step, step), step)
        placed = iota((step, tok), 0) + at * step == slot_row_int
        wanted = jnp.sum(jnp.where(placed, wanted_row, 0.0), axis=1, keepdims=True)
        high = jnp.floor(wanted * (1.0 / 64.0))
        low = wanted - 64.0 * high
        s.ask[here, :] = jnp.where(iota((step, 128), 1) < 64, high, low).astype(bf16)
        s.place[here, :] = placed.astype(f32).astype(bf16)
        return carry

    lax.fori_loop(0, slots // step, place_slots, 0)
    slot_col = column_of(slot_row).astype(i32)
    s.pick[...] = (iota((tok, slots), 1) == slot_col).astype(f32).astype(bf16)

    pl.semaphore_wait(barrier, devices - 1)

    def slot_rows(place):
        return pl.ds(pl.multiple_of(place * SLOTS, SLOTS), SLOTS)

    def swap_copy(src, dst, sems, to):
        return pltpu.make_async_remote_copy(
            src_ref=src.at[slot_rows(to)],
            dst_ref=dst.at[slot_rows(me)],
            send_sem=sems.at[0],
            recv_sem=sems.at[1],
            device_id=at_device(to),
            device_id_type=MESH,
        )

    def swap_start(src, dst, sems):
        def one(j, carry):
            swap_copy(src, dst, sems, other(j)).start()
            return carry

        lax.fori_loop(1, devices, one, 0)
        dst[slot_rows(me), :] = src[slot_rows(me), :]

    def swap_wait(dst, sem):
        blocks = dst.at[pl.ds(0, slots - SLOTS)]
        pltpu.make_async_copy(blocks, blocks, sem).wait()

    def swap_arrived(dst, sems):
        swap_wait(dst, sems.at[1])

    def swap_sent(dst, sems):
        swap_wait(dst, sems.at[0])

    ask_sems, row_sems, out_sems = s.ask_sems, s.row_sems, s.out_sems
    swap_start(s.ask, s.asked, ask_sems)
    for at in range(table_parts):
        table_copy(at).wait()
        s.table[pl.ds(at * stage_rows, stage_rows), :] = table_part(at)[...].astype(bf16)
        if at + ahead < table_parts:
            table_copy(at + ahead).start()
    swap_arrived(s.asked, ask_sems)

    per_block = BLOCK // SLOTS

    def look(at, carry):
        block = lax.rem(lax.div(me, per_block) + at, slots // BLOCK)
        rows = pl.ds(pl.multiple_of(block * BLOCK, BLOCK), BLOCK)
        asked = s.asked[rows, :].astype(f32)
        ident = asked[:, 0:1] * 64.0 + asked[:, 64:65] - 1.0
        eye = iota((BLOCK, BLOCK), 0) == iota((BLOCK, BLOCK), 1)
        ident_row = jnp.sum(jnp.where(eye, ident, 0.0), axis=0, keepdims=True)
        s.ids[:, rows] = jnp.broadcast_to(ident_row.astype(i32), (8, BLOCK))
        hot = (iota((BLOCK, table_rows), 1) == ident.astype(i32)).astype(f32).astype(bf16)
        s.found[rows, :] = nn(hot, s.table[...]).astype(bf16)

        def one(i, inner):
            to = block * per_block + lax.rem(lax.rem(me, per_block) + i, per_block)

            @pl.when(to != me)
            def _():
                swap_copy(s.found, s.returned, row_sems, to).start()

            return inner

        lax.fori_loop(0, per_block, one, 0)
        return carry

    lax.fori_loop(0, slots // BLOCK, look, 0)
    s.returned[slot_rows(me), :] = s.found[slot_rows(me), :]
    for copy in loads:
        copy.wait()
    swap_arrived(s.returned, row_sems)

    def rows_of(model, k):
        return pl.ds(pl.multiple_of(k * span + model * BLOCK, BLOCK), BLOCK)

    def own_rows(k):
        return pl.ds(k * BLOCK, BLOCK)

    class Gather:
        def __init__(self, buffer, k):
            self.buffer, self.k = buffer, k
            mine = buffer.at[rows_of(m, k)]
            self.far = net.send(mine, mine, by_side, (k, 0))
            self.near = net.send(mine, mine, by_core, (k, 1))

        def forward(self):
            self.far.wait_recv()
            there = self.buffer.at[rows_of(m2, self.k)]
            self.passed = net.send(there, there, by_core, (self.k, 2))

        def finish(self):
            self.near.wait_recv()
            self.passed.wait_recv()

    class Scatter:
        last = {}

        def __init__(self, k):
            self.k = k
            for copy in Scatter.last.get(k, []):
                net.sent(copy)
            part = partial[k]
            self.near = []
            for r, model in ((0, m3), (1, m1)):
                here = pl.ds(pl.multiple_of(model * BLOCK, BLOCK), BLOCK)
                s.near_send[k, r] = part[here, :].astype(bf16)
                self.near.append(
                    net.send(s.near_send.at[k, r], s.near_land.at[k, r], by_core, (k, 3 + r))
                )

        def middle(self):
            k = self.k
            self.near[0].wait_recv()
            here = pl.ds(pl.multiple_of(m2 * BLOCK, BLOCK), BLOCK)
            total = partial[k][here, :] + s.near_land[k, 0].astype(f32)
            s.far_send[k] = total.astype(bf16)
            self.far = net.send(s.far_send.at[k], s.far_land.at[k], by_side, (k, 5))
            Scatter.last[k] = self.near + [self.far]

        def end(self):
            k = self.k
            self.near[1].wait_recv()
            here = pl.ds(pl.multiple_of(m * BLOCK, BLOCK), BLOCK)
            total = partial[k][here, :] + s.near_land[k, 1].astype(f32)
            self.far.wait_recv()
            return total + s.far_land[k].astype(f32)

    def tiles(total, step, fn):
        def one(at, carry):
            fn(pl.multiple_of(at * step, step))
            return carry

        lax.fori_loop(0, total // step, one, 0)

    x, proj, att, probs = s.x, s.proj, s.att, s.probs
    gathers = []
    for k in range(chunks):
        own = nn(s.pick[own_rows(k), :], s.returned[...])
        x[rows_of(m, k), :] = own.astype(bf16)
        gathers.append(Gather(x, k))

    lane = iota((BLOCK, BLOCK), 1)
    sub = iota((BLOCK, BLOCK), 0)
    first_half = lane < HEAD
    head_masks = [
        (lane < HEAD).astype(f32).astype(bf16),
        (lane >= HEAD).astype(f32).astype(bf16),
    ]
    heads = cols // HEAD
    long_blocks = n_model // 2
    per_long = tok // LONG_LEN
    per_short = tok // SHORT_LEN
    short_in_block = BLOCK // SHORT_LEN

    def key_mask(model, k, is_long):
        if is_long:
            return sub < long_ref[0, model * per_long + k]
        keep = None
        for j in range(short_in_block):
            size = short_ref[0, (model - long_blocks) * per_short + k * short_in_block + j]
            start = j * SHORT_LEN
            ok = (sub >= start) & (sub < start + size) & (lane >= start) & (lane < start + SHORT_LEN)
            keep = ok if keep is None else keep | ok
        return keep

    def head_parts(source, rows, h, part):
        g = h // 2
        return source[rows, pl.ds(part * pad + g * BLOCK, BLOCK)]

    def attend(k):
        def project(at):
            rows = pl.ds(pl.multiple_of(k * span + at, 256), 256)
            proj[rows, :] = nt(x[rows, :], wt[...]).astype(bf16)

        tiles(span, 256, project)

        def block(is_long, model):
            rows = rows_of(model, k)
            keep = key_mask(model, k, is_long)
            outs = []
            for h in range(heads):
                query = head_parts(proj, rows, h, 0) * head_masks[h % 2]
                scores = nt(head_parts(proj, rows, h, 1), query) * 0.125
                scores = jnp.where(keep, scores, -1e30)
                weights = jnp.exp(scores - jnp.max(scores, axis=0, keepdims=True))
                weights = weights * (1.0 / jnp.sum(weights, axis=0, keepdims=True))
                probs[k, model, h] = weights
                outs.append(tn(weights.astype(bf16), head_parts(proj, rows, h, 2)))
            for g in range(pad // BLOCK):
                second = outs[2 * g + 1] if 2 * g + 1 < heads else jnp.zeros((BLOCK, BLOCK), f32)
                both = jnp.where(first_half, outs[2 * g], second)
                att[rows, pl.ds(g * BLOCK, BLOCK)] = both.astype(bf16)

        for model in range(n_model):
            block(model < long_blocks, model)

        def mix(at):
            rows = pl.ds(pl.multiple_of(k * span + at, 256), 256)
            partial[k][pl.ds(at, 256), :] = nn(att[rows, :], mixw[...])

        tiles(span, 256, mix)

    nothing = ((),) * chunks

    def pipeline(gathers, work, forward=nothing, middle=nothing, finish=nothing, also=None):
        scatters = []
        for k in range(chunks):
            if gathers:
                steps(*forward[k])
                gathers[k].forward()
            if k:
                steps(*middle[k - 1])
                scatters[k - 1].middle()
            if gathers:
                steps(*finish[k])
                gathers[k].finish()
            if also is not None and k == chunks - 1:
                also()
            work(k)
            scatters.append(Scatter(k))
        steps(*middle[-1])
        scatters[-1].middle()
        return scatters

    bits = tuple(range(n_data.bit_length() - 1))
    part_rows = [width // 3] * 3 + [ff // 3] * 3 + [cols] * 4
    part_at = [sum(part_rows[:i]) for i in range(len(part_rows))]
    reduces = [
        Reduce(
            net,
            s.grads.at[pl.ds(at, rows)],
            sums.at[pl.ds(at, rows)],
            s.sum_land.at[i],
            (d, m),
            bits,
        )
        for i, (at, rows) in enumerate(zip(part_at, part_rows, strict=True))
    ]
    norm_sum = s.norm_sum
    norm_copies, norm_done = [], []
    stages = [by_core, by_side] + [reduces[0].partner(bit)[1] for bit in bits]

    def norm_send():
        at = len(norm_copies)
        if at < len(stages):
            norm_copies.append(net.send(norm_sum.at[at], s.norm_land.at[at], stages[at]))

    def norm_step():
        at = len(norm_copies) - 1
        norm_copies[at].wait_recv()
        norm_sum[at + 1] = norm_sum[at] + s.norm_land[at]
        norm_done.append(at)
        norm_send()

    def steps(*order):
        for at in order:
            if at == NORM:
                norm_step()
            else:
                reduces[at].step()

    scatters = pipeline(gathers, attend)

    gain_one, shift_one, gain_two, shift_two = [
        ref[...].reshape(1, width)
        for ref in (s.gain_one, s.shift_one, s.gain_two, s.shift_two)
    ]
    norm, act = s.norm, s.act
    gathers = []
    for k in range(chunks):
        hidden = x[rows_of(m, k), :].astype(f32) + scatters[k].end()
        normal, scale = norm_forward(hidden)
        s.normal_one[own_rows(k), :] = normal
        s.scale_one[own_rows(k), :] = jnp.broadcast_to(scale, (BLOCK, 128))
        normed = normal * gain_one + shift_one
        s.normed[own_rows(k), :] = normed
        norm[rows_of(m, k), :] = normed.astype(bf16)
        gathers.append(Gather(norm, k))

    def feed(k):
        def one(at):
            rows = pl.ds(pl.multiple_of(k * span + at, 128), 128)
            pre = nn(norm[rows, :], upw[...])
            cumulative = 0.5 * (1.0 + lax.erf(pre * 0.7071067811865476))
            act[rows, :] = (pre * cumulative).astype(bf16)
            slope[rows, :] = cumulative + pre * (0.3989422804014327 * jnp.exp(-0.5 * pre * pre))

        tiles(span, 128, one)

        def two(at):
            rows = pl.ds(pl.multiple_of(k * span + at, 256), 256)
            partial[k][pl.ds(at, 256), :] = nn(act[rows, :], downw[...])

        tiles(span, 256, two)

    scatters = pipeline(gathers, feed)

    for k in range(chunks):
        hidden = s.normed[own_rows(k), :] + scatters[k].end()
        normal, scale = norm_forward(hidden)
        s.normal_two[own_rows(k), :] = normal
        s.scale_two[own_rows(k), :] = jnp.broadcast_to(scale, (BLOCK, 128))
        rows_now = normal * gain_two + shift_two
        s.rows[own_rows(k), :] = rows_now
        block_out[own_rows(k), :] = rows_now.astype(bf16)

    gb, gp, gm, gproj = s.gb, s.gp, s.gm, s.gproj

    def second_back(k):
        rows = own_rows(k)
        return norm_back(
            s.grad_rows[rows, :], s.normal_two[rows, :], s.scale_two[rows, 0:1], gain_two
        )

    s.grad_rows[...] = s.upper[...].astype(f32)
    gathers = []
    for k in range(chunks):
        gb[rows_of(m, k), :] = second_back(k).astype(bf16)
        gathers.append(Gather(gb, k))

    pool = s.pool
    half = width // 2
    firsts = jnp.concatenate(
        [s.rows[pl.ds(i * SHORT_LEN, 1), :] for i in range(per_short)], axis=0
    )
    pool[d, m] = jnp.concatenate([firsts[:, :half], firsts[:, half:]], axis=0).astype(bf16)

    def pool_copy(j):
        return pltpu.make_async_remote_copy(
            src_ref=pool.at[d, m],
            dst_ref=pool.at[d, m],
            send_sem=s.pool_sems.at[0],
            recv_sem=s.pool_sems.at[1],
            device_id=(lax.rem(d + j, n_data), m),
            device_id_type=MESH,
        )

    def pool_start(j, carry):
        pool_copy(j).start()
        return carry

    def pool_wait(at):
        blocks = pool.at[pl.ds(0, n_data - 1), m]
        pltpu.make_async_copy(blocks, blocks, s.pool_sems.at[at]).wait()

    lax.fori_loop(1, n_data, pool_start, 0)
    pool_wait(1)
    far = net.send(pool.at[:, m], pool.at[:, m], by_side)
    near = net.send(pool.at[:, m], pool.at[:, m], by_core)
    far.wait_recv()
    passed = net.send(pool.at[:, m2], pool.at[:, m2], by_core)
    near.wait_recv()
    passed.wait_recv()


    count = devices * per_short
    sentences = dims.longs + dims.shorts
    pairs2 = pairing_ref.shape[1]

    def sentence_of(index):
        place = lax.div(index, per_short)
        slot = lax.rem(index, per_short)
        model = lax.rem(place, n_model)
        data = lax.div(place, n_model)
        ratio = LONG_LEN // SHORT_LEN
        is_long = model < long_blocks
        valid = jnp.logical_or(jnp.logical_not(is_long), lax.rem(slot, ratio) == 0)
        number = jnp.where(
            is_long,
            model * per_long + lax.div(slot, ratio),
            dims.longs + (model - long_blocks) * per_short + slot,
        )
        return jnp.where(valid, data * sentences + number, -1)

    group_rows_first = n_model * per_short

    def unfold(at, carry):
        part = pool[at].astype(f32)
        here = pl.ds(pl.multiple_of(at * group_rows_first, 16), group_rows_first)
        s.left[here, :] = part[:, :per_short, :].reshape(group_rows_first, half).astype(bf16)
        s.right[here, :] = part[:, per_short:, :].reshape(group_rows_first, half).astype(bf16)
        return carry

    lax.fori_loop(0, n_data, unfold, 0)
    gram, known = s.gram, s.known
    pair_col = column_of(pairing_ref[...].astype(f32)).astype(i32)
    step = 256 if count <= 256 else 128

    def measure(number, carry):
        at = number * step
        block = pl.ds(pl.multiple_of(at, 128), step)
        gram[:, block] = nt(s.left[...], s.left[block, :]) + nt(
            s.right[...], s.right[block, :]
        )
        sent = sentence_of(iota((1, step), 1) + at)
        place = jnp.sum(
            jnp.where(pair_col == sent, iota((pairs2, step), 0), 0).astype(f32),
            axis=0,
            keepdims=True,
        )
        place = jnp.where(sent >= 0, place, -2.0)
        pair = jnp.floor(place * 0.5)
        eye = iota((step, step), 0) == iota((step, step), 1)
        square = jnp.sum(jnp.where(eye, gram[block, block], 0.0), axis=0, keepdims=True)
        known[0:1, block] = lax.rsqrt(square + 1e-06)
        known[1:2, block] = pair
        known[2:3, block] = jnp.where(sent >= 0, place - 2.0 * pair, 5.0)
        for i in range(3):
            s.known_col[block, i : i + 1] = column_of(known[i : i + 1, block])
        return carry

    lax.fori_loop(0, count // step, measure, 0)

    def logits_of(part, block, inv_col, pair_col, side_col):
        inv_row, pair_row, side_row = known[0:1, block], known[1:2, block], known[2:3, block]
        facing = side_col + side_row == 1.0
        same = (pair_col == pair_row) & facing
        cosine = part * inv_col * inv_row
        return 40.0 * (cosine - jnp.where(same, 0.3, 0.0)), facing, same

    def lose(number, loss):
        block = pl.ds(pl.multiple_of(number * step, 128), step)
        logits, facing, same = logits_of(
            gram[:, block],
            block,
            s.known_col[:, 0:1],
            s.known_col[:, 1:2],
            s.known_col[:, 2:3],
        )
        masked = jnp.where(facing, logits, -1e30)
        top = jnp.max(masked, axis=0, keepdims=True)
        total = jnp.sum(jnp.where(facing, jnp.exp(masked - top), 0.0), axis=0, keepdims=True)
        valid = known[1:2, block] >= 0.0
        log_total = jnp.where(valid, top + jnp.log(jnp.where(valid, total, 1.0)), 0.0)
        known[3:4, block] = log_total
        matched = jnp.sum(jnp.where(same, logits, 0.0), axis=0, keepdims=True)
        return loss + jnp.sum(log_total - matched, axis=1, keepdims=True)

    loss = lax.fori_loop(0, count // step, lose, jnp.zeros((1, 1), f32))
    loss_out[...] = jnp.broadcast_to(loss * (2.0 / pairs2), loss_out.shape)

    own_first = pl.ds(pl.multiple_of(me * per_short, 8), per_short)
    mine_mask = iota((per_short, count), 1) == iota((per_short, count), 0) + me * per_short

    def own_col(row):
        return jnp.sum(jnp.where(mine_mask, row, 0.0), axis=1, keepdims=True)

    inv_row, log_row = known[0:1, :], known[3:4, :]
    inv_own, log_own = own_col(inv_row), own_col(log_row)
    logits, facing, same = logits_of(
        gram[own_first, :],
        slice(None),
        inv_own,
        own_col(known[1:2, :]),
        own_col(known[2:3, :]),
    )
    pull = jnp.exp(jnp.where(facing, logits - log_own, -1e30)) + jnp.exp(
        jnp.where(facing, logits - log_row, -1e30)
    )
    pull = 40.0 * (pull - jnp.where(same, 2.0, 0.0)) * inv_row
    pull_high = pull.astype(bf16)
    pull_low = (pull - pull_high.astype(f32)).astype(bf16)
    grad_unit = jnp.concatenate(
        [nn(pull_high, n[...]) + nn(pull_low, n[...]) for n in (s.left, s.right)], axis=1
    )
    unit = firsts * inv_own
    grad_firsts = inv_own * (
        grad_unit - unit * jnp.sum(unit * grad_unit, axis=1, keepdims=True)
    )
    grad_rows = s.grad_rows
    for i in range(per_short):
        at = pl.ds(i * SHORT_LEN, 1)
        grad_rows[at, :] = grad_rows[at, :] + grad_firsts[i : i + 1, :]


    norm_sum[0] = jnp.zeros((8, width), f32)
    for k in range(chunks):
        s.second[own_rows(k), :] = second_back(k)
    patch = s.patch
    firsts = jnp.concatenate(
        [s.second[pl.ds(i * SHORT_LEN, 1), :] for i in range(per_short)], axis=0
    )
    patch[m] = jnp.concatenate([firsts[:, :half], firsts[:, half:]], axis=0).astype(bf16)
    far = net.send(patch.at[m], patch.at[m], by_side)
    near = net.send(patch.at[m], patch.at[m], by_core)
    for k in range(chunks):
        grad = grad_rows[own_rows(k), :]
        normal = s.normal_two[own_rows(k), :]
        norm_sum[0, 2:3, :] = norm_sum[0, 2:3, :] + jnp.sum(grad * normal, axis=0, keepdims=True)
        norm_sum[0, 3:4, :] = norm_sum[0, 3:4, :] + jnp.sum(grad, axis=0, keepdims=True)
    for k in range(chunks):
        gathers[k].forward()
    far.wait_recv()
    passed = net.send(patch.at[m2], patch.at[m2], by_core)
    for k in range(chunks):
        gathers[k].finish()
        net.sent(gathers[k].far)
        net.sent(gathers[k].near)
        net.sent(gathers[k].passed)
    near.wait_recv()
    passed.wait_recv()
    top_row = iota((16, width), 0) == 0
    per_chunk = BLOCK // SHORT_LEN

    def mend(model, carry):
        fresh = patch[model].astype(f32)
        for i in range(per_short):
            at = (i // per_chunk) * span + model * BLOCK + (i % per_chunk) * SHORT_LEN
            rows = pl.ds(pl.multiple_of(at, 16), 16)
            new = jnp.concatenate(
                [fresh[i : i + 1], fresh[per_short + i : per_short + i + 1]], axis=1
            )
            gb[rows, :] = jnp.where(top_row, new, gb[rows, :].astype(f32)).astype(bf16)
        return carry

    lax.fori_loop(0, n_model, mend, 0)

    def feed_back(k):
        def one(at):
            rows = pl.ds(pl.multiple_of(k * span + at, 128), 128)
            gp[rows, :] = (nt(gb[rows, :], downw[...]) * slope[rows, :]).astype(bf16)

        tiles(span, 128, one)

        def two(at):
            rows = pl.ds(pl.multiple_of(k * span + at, 256), 256)
            partial[k][pl.ds(at, 256), :] = nt(gp[rows, :], upw[...])

        tiles(span, 256, two)

    def weight_grad(target, base, rows, left, right, left_at=0):
        step = 64

        def one(at):
            part = tn(left[:, pl.ds(pl.multiple_of(left_at + at, 64), step)], right[...])
            target[pl.ds(pl.multiple_of(base + at, 16), step), :] = part.astype(bf16)

        tiles(rows, step, one)

    def begin(first, left, right, step):
        for i, at in enumerate(range(0, left.shape[1], step)):
            item = reduces[first + i]
            part = tn(left[:, at : at + step], right[...]).astype(bf16)
            here = pl.ds(part_at[first + i], part_rows[first + i])
            s.grads[here, :] = part[: part_rows[first + i]]
            item.start()

    begin(0, act, gb, part_rows[0])
    scatters = pipeline([], feed_back, middle=((), (0,)))
    begin(3, norm, gp, part_rows[3])
    before_end = ((1,), (0, 2, 1))
    gathers = []
    for k in range(chunks):
        steps(*before_end[k])
        grad = s.second[own_rows(k), :] + scatters[k].end()
        normal = s.normal_one[own_rows(k), :]
        norm_sum[0, 0:1, :] = norm_sum[0, 0:1, :] + jnp.sum(grad * normal, axis=0, keepdims=True)
        norm_sum[0, 1:2, :] = norm_sum[0, 1:2, :] + jnp.sum(grad, axis=0, keepdims=True)
        back = norm_back(grad, normal, s.scale_one[own_rows(k), 0:1], gain_one)
        s.second[own_rows(k), :] = back
        gm[rows_of(m, k), :] = back.astype(bf16)
        gathers.append(Gather(gm, k))
    norm_send()

    def attend_back(k):
        def unmix(at):
            rows = pl.ds(pl.multiple_of(k * span + at, 256), 256)
            s.gatt[rows, :] = nt(gm[rows, :], mixw[...]).astype(bf16)

        tiles(span, 256, unmix)

        def block(model):
            rows = rows_of(model, k)
            parts = ([], [], [])
            for h in range(heads):
                g = h // 2
                mask = head_masks[h % 2]
                grad_out = s.gatt[rows, pl.ds(g * BLOCK, BLOCK)] * mask
                weights = probs[k, model, h]
                grad_probs = nt(head_parts(proj, rows, h, 2), grad_out)
                inner = jnp.sum(weights * grad_probs, axis=0, keepdims=True)
                grad_scores = (weights * (grad_probs - inner)).astype(bf16)
                parts[0].append(tn(grad_scores, head_parts(proj, rows, h, 1)) * 0.125)
                parts[1].append(nn(grad_scores, head_parts(proj, rows, h, 0)) * 0.125)
                parts[2].append(nn(weights.astype(bf16), grad_out))
            for part in range(3):
                for g in range(pad // BLOCK):
                    outs = parts[part]
                    zero = jnp.zeros((BLOCK, BLOCK), f32)
                    second = outs[2 * g + 1] if 2 * g + 1 < heads else zero
                    both = jnp.where(first_half, outs[2 * g], second)
                    gproj[rows, pl.ds(part * pad + g * BLOCK, BLOCK)] = both.astype(bf16)

        for model in range(n_model):
            block(model)

        def one(at):
            rows = pl.ds(pl.multiple_of(k * span + at, 256), 256)
            partial[k][pl.ds(at, 256), :] = nn(gproj[rows, :], wt[...])

        tiles(span, 256, one)

    scatters = pipeline(
        gathers,
        attend_back,
        forward=((0, 3, 2, NORM), (0, 4, 3, 2, NORM)),
        middle=((), (NORM, 0, 4)),
        finish=((1,), (1, 5)),
        also=lambda: begin(6, att, gm, pad),
    )
    begin(7, gproj, x, pad)
    steps(6, 3, 2)
    before_end = ((), (1, 0, 5, NORM))
    swap_sent(s.returned, row_sems)
    for k in range(chunks):
        steps(*before_end[k])
        grad = s.second[own_rows(k), :] + scatters[k].end()
        s.grad_in[own_rows(k), :] = grad.astype(bf16)

    def pack(at):
        rows = pl.ds(at, 256)
        s.outgoing[rows, :] = nn(s.place[rows, :], s.grad_in[...]).astype(bf16)

    tiles(slots, 256, pack)
    swap_start(s.outgoing, s.incoming, out_sems)

    tail = [4, 7, 6, 3, NORM, 8, 2, 5, 9, 1, 7, 4, 3, 2, 6, 8, 5, 9, 7, 3, 4]
    rest_of_tail = [6, 8, 5, 9, 7, 4, 6, 8, 9, 7, 5, 8, 9, 6, 7, 8, 9]
    if resident:
        moments = [
            pltpu.make_async_copy(first_hbm, first_out, s.load_sems.at[0]),
            pltpu.make_async_copy(second_hbm, second_out, s.load_sems.at[1]),
        ]
        for copy in moments:
            copy.start()
    steps(*tail)
    swap_arrived(s.incoming, out_sems)
    if resident:
        for copy in moments:
            copy.wait()
        rows = table_rows // 8
        for at in range(8):
            here = pl.ds(at * rows, rows)
            first_new, second_new, step = table_update(
                s.ids[0:1, :],
                s.incoming[...],
                first_out[here, :],
                second_out[here, :],
                step_out[here, :],
                at * rows,
            )
            first_out[here, :] = first_new
            second_out[here, :] = second_new
            step_out[here, :] = step
            steps(*rest_of_tail[2 * at : 2 * at + 2])
        rest_of_tail = rest_of_tail[16:]
    steps(*rest_of_tail)
    while any(item.todo for item in reduces):
        steps(*(i for i, item in enumerate(reduces) if item.todo))
    while len(norm_done) < len(stages):
        norm_step()
    norm_out[...] = norm_sum[len(stages)]
    if not resident:
        outs = [
            pltpu.make_async_copy(sums, weight_out, s.load_sems.at[0]),
            pltpu.make_async_copy(s.incoming, incoming_out, s.load_sems.at[1]),
            pltpu.make_async_copy(s.ids, ids_hbm, s.load_sems.at[2]),
        ]
        for copy in outs:
            copy.start()
        for copy in outs:
            copy.wait()
    net.drain()
    pool_wait(0)
    swap_sent(s.asked, ask_sems)
    swap_sent(s.incoming, out_sems)


def table_update(ids, incoming, first, second, table, base):
    rows, slots = first.shape[0], incoming.shape[0]
    hot = (iota((rows, slots), 0) + base == ids).astype(f32)
    uses = jnp.sum(hot, axis=1, keepdims=True)
    row_grad = nn(hot.astype(bf16), incoming) * (1.0 / jnp.maximum(uses, 1.0))
    first_new = 0.9 * first + 0.1 * row_grad
    second_new = 0.95 * second + 0.05 * row_grad * row_grad
    scale = jnp.sqrt(second_new * (1.0 / second_fix)) + 1e-08
    return first_new, second_new, first_new * (1.0 / first_fix) / scale + 0.01 * table


def finish_kernel(
    cols,
    norm_ref,
    loss_ref,
    low,
    step_ref,
    first_ref,
    second_ref,
    step_hbm,
    first_out,
    second_out,
    down_out,
    up_out,
    mix_out,
    heads_out,
    loss_out,
    *rest,
):
    norm_outs = rest[:4]
    wide, state_sems, wide_sems = rest[4:]
    width = low.shape[1]
    states = [
        pltpu.make_async_copy(src, dst, state_sems.at[i])
        for i, (src, dst) in enumerate(
            ((step_ref, step_hbm), (first_ref, first_out), (second_ref, second_out))
        )
    ]
    for copy in states:
        copy.start()
    loss_out[...] = loss_ref[0:1, 0:1]
    for i, out in enumerate(norm_outs):
        out[...] = norm_ref[i, :]
    starts = (0, width, 2 * width, 2 * width + cols, 3 * width)
    wides = []
    for i, out in enumerate((down_out, up_out, mix_out, heads_out)):
        count = starts[i + 1] - starts[i]
        here = pl.ds(starts[i], count)
        step = 96

        def one(at, carry, base=starts[i]):
            rows = pl.ds(pl.multiple_of(base + at * step, 16), step)
            wide[rows, :] = low[rows, :].astype(f32)
            return carry

        lax.fori_loop(0, count // step, one, 0)
        wides.append(pltpu.make_async_copy(wide.at[here], out, wide_sems.at[i]))
        wides[-1].start()
    for copy in states + wides:
        copy.wait()


def table_kernel(
    cols,
    ids_ref,
    norm_ref,
    loss_ref,
    incoming_hbm,
    weights_hbm,
    table_hbm,
    first_hbm,
    second_hbm,
    step_hbm,
    first_out,
    second_out,
    down_out,
    up_out,
    mix_out,
    heads_out,
    loss_out,
    *rest,
):
    norm_outs = rest[:4]
    incoming, low, wide, state, in_sems, out_sems, low_sems, wide_sems = rest[4:]
    slots, width = incoming.shape
    parts = in_sems.shape[1]
    rows = state.shape[1] // parts

    def tile(at):
        return pl.ds(pl.multiple_of(at * rows, 8), rows)

    def load(i, at):
        src = (first_hbm, second_hbm, table_hbm)[i]
        return pltpu.make_async_copy(
            src.at[tile(at)], state.at[i, tile(at)], in_sems.at[i, at]
        )

    def store(i, at):
        dst = (first_out, second_out, step_hbm)[i]
        return pltpu.make_async_copy(
            state.at[i, tile(at)], dst.at[tile(at)], out_sems.at[i, at]
        )

    def each_part(step):
        def one(at, carry):
            for i in range(3):
                step(i, at)
            return carry

        lax.fori_loop(0, parts, one, 0)

    named = pltpu.make_async_copy(incoming_hbm, incoming, low_sems.at[0])
    named.start()
    lows = []
    for i in range(3):
        here = pl.ds(i * width, width)
        lows.append(
            pltpu.make_async_copy(weights_hbm.at[here], low.at[here], low_sems.at[1 + i])
        )
    for copy in lows[:1]:
        copy.start()
    each_part(lambda i, at: load(i, at).start())
    for copy in lows[1:]:
        copy.start()
    loss_out[...] = loss_ref[0:1, 0:1]
    for i, out in enumerate(norm_outs):
        out[...] = norm_ref[i, :]
    named.wait()

    wides = []
    starts = (0, width, 2 * width, 2 * width + cols, 3 * width)
    for i, out in enumerate((down_out, up_out, mix_out, heads_out)):
        here = pl.ds(starts[i], starts[i + 1] - starts[i])
        wides.append(pltpu.make_async_copy(wide.at[here], out, wide_sems.at[i]))

    def widen(i):
        lows[i].wait()
        step = 96

        def one(at, carry):
            here = pl.ds(pl.multiple_of(i * width + at * step, 16), step)
            wide[here, :] = low[here, :].astype(f32)
            return carry

        lax.fori_loop(0, width // step, one, 0)
        for copy in wides[i : i + 1] if i < 2 else wides[2:]:
            copy.start()

    widen(0)

    def update(at, carry):
        for i in range(3):
            load(i, at).wait()
        here = tile(at)
        first_new, second_new, step = table_update(
            ids_ref[0:1, :],
            incoming[...],
            state[0, here, :],
            state[1, here, :],
            state[2, here, :],
            at * rows,
        )
        state[0, here, :] = first_new
        state[1, here, :] = second_new
        state[2, here, :] = step
        for i in range(3):
            store(i, at).start()
        return carry

    lax.fori_loop(0, parts, update, 0)
    widen(1)
    widen(2)
    each_part(lambda i, at: store(i, at).wait())
    for copy in wides:
        copy.wait()


def body(
    token_owner,
    token_row,
    long_len,
    short_len,
    pairing,
    embed_table,
    first_moment,
    second_moment,
    heads_weight,
    mix_weight,
    up_weight,
    down_weight,
    first_gain,
    first_shift,
    second_gain,
    second_shift,
    upper_grad,
):
    tok, width = upper_grad.shape
    n_model, n_data = lax.axis_size("mp"), lax.axis_size("dp")
    devices = n_model * n_data
    group = tok * n_model
    cols = heads_weight.shape[2]
    pad = -(-cols // BLOCK) * BLOCK
    ff = up_weight.shape[1]
    slots = devices * SLOTS
    chunks = tok // BLOCK
    span = BLOCK * n_model
    per_short = tok // SHORT_LEN
    firsts = devices * per_short
    table_rows = embed_table.shape[0]
    bits = n_data.bit_length() - 1
    vmem = pltpu.VMEM
    dma = pltpu.SemaphoreType.DMA
    shapes = dict(
        table=vmem((table_rows, width), bf16),
        wt=vmem((3 * pad, width), bf16),
        mixw=vmem((pad, width), bf16),
        upw=vmem((width, ff), bf16),
        downw=vmem((ff, width), bf16),
        upper=vmem((tok, width), bf16),
        ask=vmem((slots, 128), bf16),
        asked=vmem((slots, 128), bf16),
        place=vmem((slots, tok), bf16),
        pick=vmem((tok, slots), bf16),
        found=vmem((slots, width), bf16),
        returned=vmem((slots, width), bf16),
        x=vmem((group, width), bf16),
        proj=vmem((group, 3 * pad), bf16),
        att=vmem((group, pad), bf16),
        gatt=vmem((group, pad), bf16),
        probs=vmem((chunks, n_model, cols // HEAD, BLOCK, BLOCK), f32),
        near_send=vmem((chunks, 2, BLOCK, width), bf16),
        near_land=vmem((chunks, 2, BLOCK, width), bf16),
        far_send=vmem((chunks, BLOCK, width), bf16),
        far_land=vmem((chunks, BLOCK, width), bf16),
        scale_one=vmem((tok, 128), f32),
        norm=vmem((group, width), bf16),
        act=vmem((group, ff), bf16),
        scale_two=vmem((tok, 128), f32),
        patch=vmem((n_model, 2 * per_short, width // 2), bf16),
        pool=vmem((n_data, n_model, 2 * per_short, width // 2), bf16),
        left=vmem((firsts, width // 2), bf16),
        right=vmem((firsts, width // 2), bf16),
        gram=vmem((firsts, firsts), f32),
        known=vmem((8, firsts), f32),
        known_col=vmem((firsts, 128), f32),
        gb=vmem((group, width), bf16),
        gm=vmem((group, width), bf16),
        grad_in=vmem((tok, width), bf16),
        norm_sum=vmem((3 + bits, 8, width), f32),
        norm_land=vmem((2 + bits, 8, width), f32),
        grads=vmem((3 * width, width), bf16),
        sum_land=vmem((10, 3 * width // 4, width // 2), bf16),
        send_sems=dma((32,)),
        recv_sems=dma((20 + 21 * bits,)),
        owner=vmem((1, group), i32),
        rowid=vmem((1, group), i32),
        long=pltpu.SMEM(long_len.shape, i32),
        short=pltpu.SMEM(short_len.shape, i32),
        pairing=vmem((1, pairing.shape[0]), i32),
        gain_one=vmem((width,), f32),
        shift_one=vmem((width,), f32),
        gain_two=vmem((width,), f32),
        shift_two=vmem((width,), f32),
        small_sems=dma((9,)),
        load_sems=dma((8,)),
        table_sems=dma((max(4, table_rows // span),)),
        ids=vmem((8, slots), i32),
        ask_sems=dma((2,)),
        row_sems=dma((2,)),
        out_sems=dma((2,)),
        pool_sems=dma((2,)),
    )
    resident = devices <= 32
    if not resident:
        shapes.update(
            wide_a=vmem((2 * group, width), f32),
            wide_b=vmem((6 * tok, width), f32),
            sums=vmem((3 * width, width), bf16),
        )
    dims = SimpleNamespace(
        resident=resident,
        n_data=n_data,
        n_model=n_model,
        names=tuple(shapes),
        tok=tok,
        width=width,
        cols=cols,
        pad=pad,
        ff=ff,
        longs=long_len.shape[1],
        shorts=short_len.shape[1],
    )
    in_vmem = pl.BlockSpec(memory_space=pltpu.VMEM)
    in_hbm = pl.BlockSpec(memory_space=pl.ANY)
    heads_rows = jnp.transpose(heads_weight, (1, 2, 0)).reshape(3 * cols, width)
    whole = jax.ShapeDtypeStruct((table_rows, width), f32)
    out_shape = (
        jax.ShapeDtypeStruct((tok, width), bf16),
        jax.ShapeDtypeStruct((8, width), f32),
        jax.ShapeDtypeStruct((8, 128), f32),
    )
    if resident:
        out_shape = out_shape[:1] + (vmem((8, width), f32), vmem((8, 128), f32))
        out_shape += (vmem((3 * width, width), bf16),) + (vmem((table_rows, width), f32),) * 3
        out_specs = (in_vmem,) * 7
    else:
        out_shape += (
            jax.ShapeDtypeStruct((3 * width, width), bf16),
            jax.ShapeDtypeStruct((slots, width), bf16),
            jax.ShapeDtypeStruct((8, slots), i32),
        )
        out_specs = (in_vmem,) * 3 + (in_hbm,) * 3
    block_out, norms, loss, *more = pl.pallas_call(
        functools.partial(layer_kernel, dims),
        out_shape=out_shape,
        in_specs=[in_hbm] * 17,
        out_specs=out_specs,
        scratch_shapes=list(shapes.values()),
        compiler_params=pltpu.CompilerParams(
            collective_id=0,
            has_side_effects=True,
            vmem_limit_bytes=(40 if resident else 63) * 2**20,
        ),
    )(
        token_owner.reshape(1, group),
        token_row.reshape(1, group),
        long_len,
        short_len,
        pairing.reshape(1, -1),
        first_gain,
        first_shift,
        second_gain,
        second_shift,
        embed_table,
        heads_rows,
        mix_weight,
        up_weight,
        down_weight,
        upper_grad,
        first_moment,
        second_moment,
    )
    out_shape = (
        (whole, whole, whole)
        + tuple(jax.ShapeDtypeStruct((rows, width), f32) for rows in (ff, width, cols, 3 * cols))
        + (jax.ShapeDtypeStruct((1, 1), f32),)
        + (jax.ShapeDtypeStruct((width,), f32),) * 4
    )
    out_specs = (in_hbm,) * 7 + (in_vmem,) * 5
    if resident:
        finished = pl.pallas_call(
            functools.partial(finish_kernel, cols),
            out_shape=out_shape,
            in_specs=[in_vmem] * 6,
            out_specs=out_specs,
            scratch_shapes=[vmem((3 * width, width), f32), dma((3,)), dma((4,))],
            compiler_params=pltpu.CompilerParams(vmem_limit_bytes=20 * 2**20),
        )(norms, loss, *more)
    else:
        weights, incoming, ids = more
        parts = 8
        finished = pl.pallas_call(
            functools.partial(table_kernel, cols),
            out_shape=out_shape,
            in_specs=[in_vmem] * 3 + [in_hbm] * 5,
            out_specs=out_specs,
            scratch_shapes=[
                vmem((slots, width), bf16),
                vmem((3 * width, width), bf16),
                vmem((3 * width, width), f32),
                vmem((3, table_rows, width), f32),
                dma((3, parts)),
                dma((3, parts)),
                dma((4,)),
                dma((4,)),
            ],
            compiler_params=pltpu.CompilerParams(vmem_limit_bytes=63 * 2**20),
        )(ids, norms, loss, incoming, weights, embed_table, first_moment, second_moment)
    table_step, first_new, second_new, down_grad, up_grad, mix_grad, heads_grad, loss = finished[:8]
    norm_grads = finished[8:]
    return (
        loss.reshape(()),
        block_out,
        jnp.transpose(heads_grad.reshape(3, cols, width), (2, 0, 1)),
        mix_grad,
        up_grad,
        down_grad,
        *norm_grads,
        table_step,
        first_new,
        second_new,
    )


def solution(mesh):
    rows = P(("dp", "mp"), None)
    in_specs = (
        P("dp", None),
        P("dp"),
        P("dp", None),
        P("dp", None),
        P(),
        rows,
        rows,
        rows,
        P(None, None, "mp"),
        P("mp", None),
        P(None, "mp"),
        P("mp", None),
        P(),
        P(),
        P(),
        P(),
        rows,
    )
    out_specs = (
        P(),
        rows,
        P(None, None, "mp"),
        P("mp", None),
        P(None, "mp"),
        P("mp", None),
        P(),
        P(),
        P(),
        P(),
        rows,
        rows,
        rows,
    )
    return jax.shard_map(body, mesh=mesh, in_specs=in_specs, out_specs=out_specs, check_vma=False)
```

```python
import functools
from types import SimpleNamespace

import jax
import jax.numpy as jnp
from jax import lax
from jax.experimental import pallas as pl
from jax.experimental.pallas import tpu as pltpu
from jax.sharding import PartitionSpec as P

HEAD = 64
LONG_LEN = 128
SHORT_LEN = 32
BLOCK = 128
SLOTS = 16
NORM = -1
MESH = pl.DeviceIdType.MESH
bf16 = jnp.bfloat16
f32 = jnp.float32
i32 = jnp.int32

first_fix = 1.0 - 0.9**10
second_fix = 1.0 - 0.95**10


def nn(left, right):
    return lax.dot_general(left, right, (((1,), (0,)), ((), ())), preferred_element_type=f32)


def nt(left, right):
    return lax.dot_general(left, right, (((1,), (1,)), ((), ())), preferred_element_type=f32)


def tn(left, right):
    return lax.dot_general(left, right, (((0,), (0,)), ((), ())), preferred_element_type=f32)


def iota(shape, axis):
    return lax.broadcasted_iota(i32, shape, axis)


def column_of(row):
    count = row.shape[1]
    eye = iota((count, count), 0) == iota((count, count), 1)
    return jnp.sum(jnp.where(eye, row, 0.0), axis=1, keepdims=True)


def mean_of(values):
    return jnp.mean(values, axis=-1, keepdims=True)


def norm_forward(hidden):
    centered = hidden - mean_of(hidden)
    scale = lax.rsqrt(mean_of(centered * centered) + 1e-12)
    return centered * scale, scale


def norm_back(grad, normal, scale, gain):
    scaled = grad * gain
    return scale * (scaled - mean_of(scaled) - normal * mean_of(scaled * normal))


class Net:
    def __init__(self, send_sems, recv_sems):
        self.send_sems, self.recv_sems = send_sems, recv_sems
        self.open = [None] * send_sems.shape[0]
        self.count = 0
        self.names = {}

    def send(self, src, dst, device, name=None):
        slot = self.count % len(self.open)
        if self.open[slot] is not None:
            self.open[slot].wait_send()
        at = self.names.setdefault(self.count if name is None else name, len(self.names))
        self.count += 1
        copy = pltpu.make_async_remote_copy(
            src_ref=src,
            dst_ref=dst,
            send_sem=self.send_sems.at[slot],
            recv_sem=self.recv_sems.at[at],
            device_id=device,
            device_id_type=MESH,
        )
        copy.start()
        self.open[slot] = copy
        return copy

    def sent(self, copy):
        for slot, item in enumerate(self.open):
            if item is copy:
                copy.wait_send()
                self.open[slot] = None

    def drain(self):
        for copy in self.open:
            if copy is not None:
                copy.wait_send()
        self.open = [None] * len(self.open)


class Reduce:
    def __init__(self, net, part, whole, land, place, bits):
        self.net, self.part, self.whole, self.land = net, part, whole, land
        self.data_pos, self.model_pos = place
        self.bits = bits
        rows, width = part.shape
        self.half = width // 2
        self.row, self.len = 0, rows
        self.offset = 0
        self.stage = 0
        self.halved = []
        grows = sum(1 for stage in range(len(bits)) if self.halves(stage))
        self.todo = [self.add] * len(bits) + [self.grow] * grows

    def step(self):
        if self.todo:
            self.todo.pop(0)()

    def halves(self, stage):
        return stage == 0 or (self.part.shape[0] >> (stage - 1)) % 32 == 0

    def partner(self, bit):
        mine = lax.rem(lax.div(self.data_pos, 1 << bit), 2)
        return mine, (self.data_pos + (1 - 2 * mine) * (1 << bit), self.model_pos)

    def start(self):
        mine, device = self.partner(self.bits[self.stage])
        halved = self.halves(self.stage)
        count = self.len
        if self.stage == 0:
            away = pl.multiple_of((1 - mine) * self.half, 128)
            self.col = pl.multiple_of(mine * self.half, 128)
            src = self.part.at[:, pl.ds(away, self.half)]
        else:
            away = self.row
            if halved:
                count = self.len // 2
                away = pl.multiple_of(self.row + (1 - mine) * count, 16)
                self.row = pl.multiple_of(self.row + mine * count, 16)
                self.len = count
            src = self.part.at[pl.ds(away, count), pl.ds(self.col, self.half)]
        self.halved.append(halved)
        self.now = self.land.at[pl.ds(self.offset, count)]
        self.offset += count
        self.copy = self.net.send(src, self.now, device)

    def add(self):
        self.copy.wait_recv()
        last = self.stage == len(self.bits) - 1
        if not self.halved[-1]:
            self.net.sent(self.copy)
        target = self.whole if last else self.part
        cols = pl.ds(self.col, self.half)
        step = 48 if self.len % 48 == 0 else min(self.len, 64)
        now, row, part = self.now, self.row, self.part

        def tile(at, carry):
            here = pl.multiple_of(at * step, 16)
            there = pl.ds(pl.multiple_of(row + here, 16), step)
            total = part[there, cols].astype(f32) + now[pl.ds(here, step), :].astype(f32)
            target[there, cols] = total.astype(bf16)
            return carry

        lax.fori_loop(0, self.len // step, tile, 0)
        if last:
            self.spread()
        else:
            self.stage += 1
            self.start()

    def spread(self):
        while self.stage and not self.halved[self.stage]:
            self.stage -= 1
        _, device = self.partner(self.bits[self.stage])
        rows = pl.ds(self.row, self.len) if self.stage else slice(None)
        here = self.whole.at[rows, pl.ds(self.col, self.half)]
        self.copy = self.net.send(here, here, device)

    def grow(self):
        self.copy.wait_recv()
        if self.stage == 0:
            return
        mine, _ = self.partner(self.bits[self.stage])
        self.row = pl.multiple_of(self.row - mine * self.len, 16)
        self.len *= 2
        self.stage -= 1
        self.spread()


def layer_kernel(
    dims,
    owner_hbm,
    rowid_hbm,
    long_hbm,
    short_hbm,
    pairing_hbm,
    gain_one_hbm,
    shift_one_hbm,
    gain_two_hbm,
    shift_two_hbm,
    table_hbm,
    heads_hbm,
    mix_hbm,
    up_hbm,
    down_hbm,
    upper_hbm,
    first_hbm,
    second_hbm,
    block_out,
    norm_out,
    loss_out,
    *rest,
):
    resident = dims.resident
    if resident:
        sums, step_out, first_out, second_out, *scratch = rest
    else:
        weight_out, incoming_out, ids_hbm, *scratch = rest
    n_data, n_model = dims.n_data, dims.n_model
    s = SimpleNamespace(**dict(zip(dims.names, scratch, strict=True)))
    tok, width, cols, pad, ff = dims.tok, dims.width, dims.cols, dims.pad, dims.ff
    devices = n_data * n_model
    group = tok * n_model
    chunks = tok // BLOCK
    span = BLOCK * n_model
    slots = devices * SLOTS
    table_rows = table_hbm.shape[0]

    if resident:
        wide_a, wide_b = first_out, second_out
    else:
        wide_a, wide_b, sums = s.wide_a, s.wide_b, s.sums
    slope = wide_a.at[pl.ds(0, group)]
    partial = [wide_a.at[pl.ds(group + k * span, span)] for k in range(chunks)]
    s.normal_one, s.normed, s.normal_two, s.rows, s.grad_rows, s.second = [
        wide_b.at[pl.ds(i * tok, tok)] for i in range(6)
    ]
    s.gproj = s.table.at[pl.ds(0, group)]
    s.gp = s.table.at[pl.ds(group, group)]
    s.outgoing = s.found
    s.incoming = s.returned
    d = lax.axis_index("dp")
    m = lax.axis_index("mp")
    me = d * n_model + m
    core = lax.rem(m, 2)
    side = lax.div(m, 2)
    m1 = m + 1 - 2 * core
    m2 = m + 2 - 4 * side
    m3 = m1 + m2 - m
    by_core = (d, m1)
    by_side = (d, m2)
    net = Net(s.send_sems, s.recv_sems)

    def at_device(place):
        return (lax.div(place, n_model), lax.rem(place, n_model))

    def other(j):
        return lax.rem(me + j, devices)

    owner_ref, rowid_ref, long_ref, short_ref = s.owner, s.rowid, s.long, s.short
    pairing_ref = s.pairing
    small = [
        pltpu.make_async_copy(src, dst, s.small_sems.at[i])
        for i, (src, dst) in enumerate(
            (
                (owner_hbm, s.owner),
                (rowid_hbm, s.rowid),
                (long_hbm, s.long),
                (short_hbm, s.short),
                (pairing_hbm, s.pairing),
                (gain_one_hbm, s.gain_one),
                (shift_one_hbm, s.shift_one),
                (gain_two_hbm, s.gain_two),
                (shift_two_hbm, s.shift_two),
            )
        )
    ]
    for copy in small:
        copy.start()

    barrier = pltpu.get_barrier_semaphore()

    def greet(j, carry):
        pl.semaphore_signal(barrier, inc=1, device_id=at_device(other(j)), device_id_type=MESH)
        return carry

    lax.fori_loop(1, devices, greet, 0)

    stage_rows = table_rows // 4 if resident else span
    table_parts = table_rows // stage_rows

    def table_part(at):
        if resident:
            return step_out.at[pl.ds(at * stage_rows, stage_rows)]
        return partial[at % 2]

    def table_copy(at):
        return pltpu.make_async_copy(
            table_hbm.at[pl.ds(at * stage_rows, stage_rows)],
            table_part(at),
            s.table_sems.at[at],
        )

    ahead = table_parts if resident else 2
    for at in range(ahead):
        table_copy(at).start()
    loads = []

    def load(src, dst):
        copy = pltpu.make_async_copy(src, dst, s.load_sems.at[len(loads)])
        copy.start()
        loads.append(copy)

    wt, mixw, upw, downw = s.wt, s.mixw, s.upw, s.downw
    for part in range(3):
        load(heads_hbm.at[pl.ds(part * cols, cols)], wt.at[pl.ds(part * pad, cols)])
        wt[pl.ds(part * pad + cols, pad - cols), :] = jnp.zeros((pad - cols, width), bf16)
    load(mix_hbm, mixw.at[pl.ds(0, cols)])
    mixw[pl.ds(cols, pad - cols), :] = jnp.zeros((pad - cols, width), bf16)
    load(up_hbm, upw)
    load(down_hbm, downw)
    load(upper_hbm, s.upper)

    for copy in small:
        copy.wait()
    own_at = pl.multiple_of(m * tok, 128)
    owner_row = owner_ref[:, pl.ds(own_at, tok)]
    rowid_row = rowid_ref[:, pl.ds(own_at, tok)]
    owned = iota((devices, tok), 0) == owner_row
    before = (iota((tok, tok), 0) < iota((tok, tok), 1)).astype(f32).astype(bf16)
    counted = nn(owned.astype(f32).astype(bf16), before)
    rank_row = jnp.sum(jnp.where(owned, counted, 0.0), axis=0, keepdims=True)
    slot_row = owner_row.astype(f32) * SLOTS + rank_row
    slot_row_int = slot_row.astype(i32)
    wanted_row = (rowid_row + 1).astype(f32)
    step = min(slots, 256)

    def place_slots(at, carry):
        here = pl.ds(pl.multiple_of(at * step, step), step)
        placed = iota((step, tok), 0) + at * step == slot_row_int
        wanted = jnp.sum(jnp.where(placed, wanted_row, 0.0), axis=1, keepdims=True)
        high = jnp.floor(wanted * (1.0 / 64.0))
        low = wanted - 64.0 * high
        s.ask[here, :] = jnp.where(iota((step, 128), 1) < 64, high, low).astype(bf16)
        s.place[here, :] = placed.astype(f32).astype(bf16)
        return carry

    lax.fori_loop(0, slots // step, place_slots, 0)
    slot_col = column_of(slot_row).astype(i32)
    s.pick[...] = (iota((tok, slots), 1) == slot_col).astype(f32).astype(bf16)

    pl.semaphore_wait(barrier, devices - 1)

    def slot_rows(place):
        return pl.ds(pl.multiple_of(place * SLOTS, SLOTS), SLOTS)

    def swap_copy(src, dst, sems, to):
        return pltpu.make_async_remote_copy(
            src_ref=src.at[slot_rows(to)],
            dst_ref=dst.at[slot_rows(me)],
            send_sem=sems.at[0],
            recv_sem=sems.at[1],
            device_id=at_device(to),
            device_id_type=MESH,
        )

    def swap_start(src, dst, sems):
        def one(j, carry):
            swap_copy(src, dst, sems, other(j)).start()
            return carry

        lax.fori_loop(1, devices, one, 0)
        dst[slot_rows(me), :] = src[slot_rows(me), :]

    def swap_wait(dst, sem):
        blocks = dst.at[pl.ds(0, slots - SLOTS)]
        pltpu.make_async_copy(blocks, blocks, sem).wait()

    def swap_arrived(dst, sems):
        swap_wait(dst, sems.at[1])

    def swap_sent(dst, sems):
        swap_wait(dst, sems.at[0])

    ask_sems, row_sems, out_sems = s.ask_sems, s.row_sems, s.out_sems
    swap_start(s.ask, s.asked, ask_sems)
    for at in range(table_parts):
        table_copy(at).wait()
        s.table[pl.ds(at * stage_rows, stage_rows), :] = table_part(at)[...].astype(bf16)
        if at + ahead < table_parts:
            table_copy(at + ahead).start()
    swap_arrived(s.asked, ask_sems)

    per_block = BLOCK // SLOTS

    def look(at, carry):
        block = lax.rem(lax.div(me, per_block) + at, slots // BLOCK)
        rows = pl.ds(pl.multiple_of(block * BLOCK, BLOCK), BLOCK)
        asked = s.asked[rows, :].astype(f32)
        ident = asked[:, 0:1] * 64.0 + asked[:, 64:65] - 1.0
        eye = iota((BLOCK, BLOCK), 0) == iota((BLOCK, BLOCK), 1)
        ident_row = jnp.sum(jnp.where(eye, ident, 0.0), axis=0, keepdims=True)
        s.ids[:, rows] = jnp.broadcast_to(ident_row.astype(i32), (8, BLOCK))
        hot = (iota((BLOCK, table_rows), 1) == ident.astype(i32)).astype(f32).astype(bf16)
        s.found[rows, :] = nn(hot, s.table[...]).astype(bf16)

        def one(i, inner):
            to = block * per_block + lax.rem(lax.rem(me, per_block) + i, per_block)

            @pl.when(to != me)
            def _():
                swap_copy(s.found, s.returned, row_sems, to).start()

            return inner

        lax.fori_loop(0, per_block, one, 0)
        return carry

    lax.fori_loop(0, slots // BLOCK, look, 0)
    s.returned[slot_rows(me), :] = s.found[slot_rows(me), :]
    for copy in loads:
        copy.wait()
    swap_arrived(s.returned, row_sems)

    def rows_of(model, k):
        return pl.ds(pl.multiple_of(k * span + model * BLOCK, BLOCK), BLOCK)

    def own_rows(k):
        return pl.ds(k * BLOCK, BLOCK)

    class Gather:
        def __init__(self, buffer, k):
            self.buffer, self.k = buffer, k
            mine = buffer.at[rows_of(m, k)]
            self.far = net.send(mine, mine, by_side, (k, 0))
            self.near = net.send(mine, mine, by_core, (k, 1))

        def forward(self):
            self.far.wait_recv()
            there = self.buffer.at[rows_of(m2, self.k)]
            self.passed = net.send(there, there, by_core, (self.k, 2))

        def finish(self):
            self.near.wait_recv()
            self.passed.wait_recv()

    class Scatter:
        last = {}

        def __init__(self, k):
            self.k = k
            for copy in Scatter.last.get(k, []):
                net.sent(copy)
            part = partial[k]
            self.near = []
            for r, model in ((0, m3), (1, m1)):
                here = pl.ds(pl.multiple_of(model * BLOCK, BLOCK), BLOCK)
                s.near_send[k, r] = part[here, :].astype(bf16)
                self.near.append(
                    net.send(s.near_send.at[k, r], s.near_land.at[k, r], by_core, (k, 3 + r))
                )

        def middle(self):
            k = self.k
            self.near[0].wait_recv()
            here = pl.ds(pl.multiple_of(m2 * BLOCK, BLOCK), BLOCK)
            total = partial[k][here, :] + s.near_land[k, 0].astype(f32)
            s.far_send[k] = total.astype(bf16)
            self.far = net.send(s.far_send.at[k], s.far_land.at[k], by_side, (k, 5))
            Scatter.last[k] = self.near + [self.far]

        def end(self):
            k = self.k
            self.near[1].wait_recv()
            here = pl.ds(pl.multiple_of(m * BLOCK, BLOCK), BLOCK)
            total = partial[k][here, :] + s.near_land[k, 1].astype(f32)
            self.far.wait_recv()
            return total + s.far_land[k].astype(f32)

    def tiles(total, step, fn):
        def one(at, carry):
            fn(pl.multiple_of(at * step, step))
            return carry

        lax.fori_loop(0, total // step, one, 0)

    x, proj, att, probs = s.x, s.proj, s.att, s.probs
    gathers = []
    for k in range(chunks):
        own = nn(s.pick[own_rows(k), :], s.returned[...])
        x[rows_of(m, k), :] = own.astype(bf16)
        gathers.append(Gather(x, k))

    lane = iota((BLOCK, BLOCK), 1)
    sub = iota((BLOCK, BLOCK), 0)
    first_half = lane < HEAD
    head_masks = [
        (lane < HEAD).astype(f32).astype(bf16),
        (lane >= HEAD).astype(f32).astype(bf16),
    ]
    heads = cols // HEAD
    long_blocks = n_model // 2
    per_long = tok // LONG_LEN
    per_short = tok // SHORT_LEN
    short_in_block = BLOCK // SHORT_LEN

    def key_mask(model, k, is_long):
        if is_long:
            return sub < long_ref[0, model * per_long + k]
        keep = None
        for j in range(short_in_block):
            size = short_ref[0, (model - long_blocks) * per_short + k * short_in_block + j]
            start = j * SHORT_LEN
            ok = (sub >= start) & (sub < start + size) & (lane >= start) & (lane < start + SHORT_LEN)
            keep = ok if keep is None else keep | ok
        return keep

    def head_parts(source, rows, h, part):
        g = h // 2
        return source[rows, pl.ds(part * pad + g * BLOCK, BLOCK)]

    def attend(k):
        def project(at):
            rows = pl.ds(pl.multiple_of(k * span + at, 512), 512)
            proj[rows, :] = nt(x[rows, :], wt[...]).astype(bf16)

        tiles(span, 512, project)

        units = [(model, h) for model in range(n_model) for h in range(heads)]
        keeps = [key_mask(model, k, model < long_blocks) for model in range(n_model)]
        scores = []
        for model, h in units:
            rows = rows_of(model, k)
            query = head_parts(proj, rows, h, 0) * head_masks[h % 2]
            scores.append(nt(head_parts(proj, rows, h, 1), query))
        weights = []
        for (model, h), score in zip(units, scores, strict=True):
            score = jnp.where(keeps[model], score * 0.125, -1e30)
            part = jnp.exp(score - jnp.max(score, axis=0, keepdims=True))
            weights.append(part * (1.0 / jnp.sum(part, axis=0, keepdims=True)))
        outs = {}
        for unit, weight in zip(units, weights, strict=True):
            value = head_parts(proj, rows_of(unit[0], k), unit[1], 2)
            outs[unit] = tn(weight.astype(bf16), value)
        for unit, weight in zip(units, weights, strict=True):
            probs[(k, *unit)] = weight
        for model in range(n_model):
            for g in range(pad // BLOCK):
                second = outs.get((model, 2 * g + 1))
                if second is None:
                    second = jnp.zeros((BLOCK, BLOCK), f32)
                both = jnp.where(first_half, outs[model, 2 * g], second)
                att[rows_of(model, k), pl.ds(g * BLOCK, BLOCK)] = both.astype(bf16)

        def mix(at):
            rows = pl.ds(pl.multiple_of(k * span + at, 512), 512)
            partial[k][pl.ds(at, 512), :] = nn(att[rows, :], mixw[...])

        tiles(span, 512, mix)

    nothing = ((),) * chunks

    def pipeline(gathers, work, forward=nothing, middle=nothing, finish=nothing, also=None):
        scatters = []
        for k in range(chunks):
            if gathers:
                steps(*forward[k])
                gathers[k].forward()
            if k:
                steps(*middle[k - 1])
                scatters[k - 1].middle()
            if gathers:
                steps(*finish[k])
                gathers[k].finish()
            if also is not None and k == chunks - 1:
                also()
            work(k)
            scatters.append(Scatter(k))
        steps(*middle[-1])
        scatters[-1].middle()
        return scatters

    bits = tuple(range(n_data.bit_length() - 1))
    part_rows = [ff // 4] * 4 + [width // 4] * 4 + [cols] * 4
    part_at = [sum(part_rows[:i]) for i in range(len(part_rows))]
    reduces = [
        Reduce(
            net,
            s.grads.at[pl.ds(at, rows)],
            sums.at[pl.ds(at, rows)],
            s.sum_land.at[i],
            (d, m),
            bits,
        )
        for i, (at, rows) in enumerate(zip(part_at, part_rows, strict=True))
    ]
    norm_sum = s.norm_sum
    norm_copies, norm_done = [], []
    stages = [by_core, by_side] + [reduces[0].partner(bit)[1] for bit in bits]

    def norm_send():
        at = len(norm_copies)
        if at < len(stages):
            norm_copies.append(net.send(norm_sum.at[at], s.norm_land.at[at], stages[at]))

    def norm_step():
        at = len(norm_copies) - 1
        norm_copies[at].wait_recv()
        norm_sum[at + 1] = norm_sum[at] + s.norm_land[at]
        norm_done.append(at)
        norm_send()

    def steps(*order):
        for at in order:
            if at == NORM:
                norm_step()
            else:
                reduces[at].step()

    scatters = pipeline(gathers, attend)

    gain_one, shift_one, gain_two, shift_two = [
        ref[...].reshape(1, width)
        for ref in (s.gain_one, s.shift_one, s.gain_two, s.shift_two)
    ]
    norm, act = s.norm, s.act
    gathers = []
    for k in range(chunks):
        hidden = x[rows_of(m, k), :].astype(f32) + scatters[k].end()
        normal, scale = norm_forward(hidden)
        s.normal_one[own_rows(k), :] = normal
        s.scale_one[own_rows(k), :] = jnp.broadcast_to(scale, (BLOCK, 128))
        normed = normal * gain_one + shift_one
        s.normed[own_rows(k), :] = normed
        norm[rows_of(m, k), :] = normed.astype(bf16)
        gathers.append(Gather(norm, k))

    def feed(k):
        def one(at):
            rows = pl.ds(pl.multiple_of(k * span + at, 512), 512)
            pre = nn(norm[rows, :], upw[...])
            cumulative = 0.5 * (1.0 + lax.erf(pre * 0.7071067811865476))
            act[rows, :] = (pre * cumulative).astype(bf16)
            slope[rows, :] = cumulative + pre * (0.3989422804014327 * jnp.exp(-0.5 * pre * pre))

        tiles(span, 512, one)

        def two(at):
            rows = pl.ds(pl.multiple_of(k * span + at, 512), 512)
            partial[k][pl.ds(at, 512), :] = nn(act[rows, :], downw[...])

        tiles(span, 512, two)

    scatters = pipeline(gathers, feed)

    for k in range(chunks):
        hidden = s.normed[own_rows(k), :] + scatters[k].end()
        normal, scale = norm_forward(hidden)
        s.normal_two[own_rows(k), :] = normal
        s.scale_two[own_rows(k), :] = jnp.broadcast_to(scale, (BLOCK, 128))
        rows_now = normal * gain_two + shift_two
        s.rows[own_rows(k), :] = rows_now
        block_out[own_rows(k), :] = rows_now.astype(bf16)

    gb, gp, gm, gproj = s.gb, s.gp, s.gm, s.gproj

    def second_back(k):
        rows = own_rows(k)
        return norm_back(
            s.grad_rows[rows, :], s.normal_two[rows, :], s.scale_two[rows, 0:1], gain_two
        )

    s.grad_rows[...] = s.upper[...].astype(f32)
    gathers = []
    for k in range(chunks):
        gb[rows_of(m, k), :] = second_back(k).astype(bf16)
        gathers.append(Gather(gb, k))

    pool = s.pool
    half = width // 2
    firsts = jnp.concatenate(
        [s.rows[pl.ds(i * SHORT_LEN, 1), :] for i in range(per_short)], axis=0
    )
    pool[d, m] = jnp.concatenate([firsts[:, :half], firsts[:, half:]], axis=0).astype(bf16)

    def pool_copy(j):
        return pltpu.make_async_remote_copy(
            src_ref=pool.at[d, m],
            dst_ref=pool.at[d, m],
            send_sem=s.pool_sems.at[0],
            recv_sem=s.pool_sems.at[1],
            device_id=(lax.rem(d + j, n_data), m),
            device_id_type=MESH,
        )

    def pool_start(j, carry):
        pool_copy(j).start()
        return carry

    def pool_wait(at):
        blocks = pool.at[pl.ds(0, n_data - 1), m]
        pltpu.make_async_copy(blocks, blocks, s.pool_sems.at[at]).wait()

    lax.fori_loop(1, n_data, pool_start, 0)
    pool_wait(1)
    far = net.send(pool.at[:, m], pool.at[:, m], by_side)
    near = net.send(pool.at[:, m], pool.at[:, m], by_core)
    far.wait_recv()
    passed = net.send(pool.at[:, m2], pool.at[:, m2], by_core)
    near.wait_recv()
    passed.wait_recv()


    count = devices * per_short
    sentences = dims.longs + dims.shorts
    pairs2 = pairing_ref.shape[1]

    def sentence_of(index):
        place = lax.div(index, per_short)
        slot = lax.rem(index, per_short)
        model = lax.rem(place, n_model)
        data = lax.div(place, n_model)
        ratio = LONG_LEN // SHORT_LEN
        is_long = model < long_blocks
        valid = jnp.logical_or(jnp.logical_not(is_long), lax.rem(slot, ratio) == 0)
        number = jnp.where(
            is_long,
            model * per_long + lax.div(slot, ratio),
            dims.longs + (model - long_blocks) * per_short + slot,
        )
        return jnp.where(valid, data * sentences + number, -1)

    group_rows_first = n_model * per_short

    def unfold(at, carry):
        part = pool[at].astype(f32)
        here = pl.ds(pl.multiple_of(at * group_rows_first, 16), group_rows_first)
        s.left[here, :] = part[:, :per_short, :].reshape(group_rows_first, half).astype(bf16)
        s.right[here, :] = part[:, per_short:, :].reshape(group_rows_first, half).astype(bf16)
        return carry

    lax.fori_loop(0, n_data, unfold, 0)
    gram, known = s.gram, s.known
    pair_col = column_of(pairing_ref[...].astype(f32)).astype(i32)
    step = 256 if count <= 256 else 128

    def measure(number, carry):
        at = number * step
        block = pl.ds(pl.multiple_of(at, 128), step)
        gram[:, block] = nt(s.left[...], s.left[block, :]) + nt(
            s.right[...], s.right[block, :]
        )
        sent = sentence_of(iota((1, step), 1) + at)
        place = jnp.sum(
            jnp.where(pair_col == sent, iota((pairs2, step), 0), 0).astype(f32),
            axis=0,
            keepdims=True,
        )
        place = jnp.where(sent >= 0, place, -2.0)
        pair = jnp.floor(place * 0.5)
        eye = iota((step, step), 0) == iota((step, step), 1)
        square = jnp.sum(jnp.where(eye, gram[block, block], 0.0), axis=0, keepdims=True)
        known[0:1, block] = lax.rsqrt(square + 1e-06)
        known[1:2, block] = pair
        known[2:3, block] = jnp.where(sent >= 0, place - 2.0 * pair, 5.0)
        for i in range(3):
            s.known_col[block, i : i + 1] = column_of(known[i : i + 1, block])
        return carry

    lax.fori_loop(0, count // step, measure, 0)

    def logits_of(part, block, inv_col, pair_col, side_col):
        inv_row, pair_row, side_row = known[0:1, block], known[1:2, block], known[2:3, block]
        facing = side_col + side_row == 1.0
        same = (pair_col == pair_row) & facing
        cosine = part * inv_col * inv_row
        return 40.0 * (cosine - jnp.where(same, 0.3, 0.0)), facing, same

    def lose(number, loss):
        block = pl.ds(pl.multiple_of(number * step, 128), step)
        logits, facing, same = logits_of(
            gram[:, block],
            block,
            s.known_col[:, 0:1],
            s.known_col[:, 1:2],
            s.known_col[:, 2:3],
        )
        masked = jnp.where(facing, logits, -1e30)
        top = jnp.max(masked, axis=0, keepdims=True)
        total = jnp.sum(jnp.where(facing, jnp.exp(masked - top), 0.0), axis=0, keepdims=True)
        valid = known[1:2, block] >= 0.0
        log_total = jnp.where(valid, top + jnp.log(jnp.where(valid, total, 1.0)), 0.0)
        known[3:4, block] = log_total
        matched = jnp.sum(jnp.where(same, logits, 0.0), axis=0, keepdims=True)
        return loss + jnp.sum(log_total - matched, axis=1, keepdims=True)

    loss = lax.fori_loop(0, count // step, lose, jnp.zeros((1, 1), f32))
    loss_out[...] = jnp.broadcast_to(loss * (2.0 / pairs2), loss_out.shape)

    own_first = pl.ds(pl.multiple_of(me * per_short, 8), per_short)
    mine_mask = iota((per_short, count), 1) == iota((per_short, count), 0) + me * per_short

    def own_col(row):
        return jnp.sum(jnp.where(mine_mask, row, 0.0), axis=1, keepdims=True)

    inv_row, log_row = known[0:1, :], known[3:4, :]
    inv_own, log_own = own_col(inv_row), own_col(log_row)
    logits, facing, same = logits_of(
        gram[own_first, :],
        slice(None),
        inv_own,
        own_col(known[1:2, :]),
        own_col(known[2:3, :]),
    )
    pull = jnp.exp(jnp.where(facing, logits - log_own, -1e30)) + jnp.exp(
        jnp.where(facing, logits - log_row, -1e30)
    )
    pull = 40.0 * (pull - jnp.where(same, 2.0, 0.0)) * inv_row
    pull_high = pull.astype(bf16)
    pull_low = (pull - pull_high.astype(f32)).astype(bf16)
    grad_unit = jnp.concatenate(
        [nn(pull_high, n[...]) + nn(pull_low, n[...]) for n in (s.left, s.right)], axis=1
    )
    unit = firsts * inv_own
    grad_firsts = inv_own * (
        grad_unit - unit * jnp.sum(unit * grad_unit, axis=1, keepdims=True)
    )
    grad_rows = s.grad_rows
    for i in range(per_short):
        at = pl.ds(i * SHORT_LEN, 1)
        grad_rows[at, :] = grad_rows[at, :] + grad_firsts[i : i + 1, :]


    norm_sum[0] = jnp.zeros((8, width), f32)
    for k in range(chunks):
        s.second[own_rows(k), :] = second_back(k)
    patch = s.patch
    firsts = jnp.concatenate(
        [s.second[pl.ds(i * SHORT_LEN, 1), :] for i in range(per_short)], axis=0
    )
    patch[m] = jnp.concatenate([firsts[:, :half], firsts[:, half:]], axis=0).astype(bf16)
    far = net.send(patch.at[m], patch.at[m], by_side)
    near = net.send(patch.at[m], patch.at[m], by_core)
    for k in range(chunks):
        grad = grad_rows[own_rows(k), :]
        normal = s.normal_two[own_rows(k), :]
        norm_sum[0, 2:3, :] = norm_sum[0, 2:3, :] + jnp.sum(grad * normal, axis=0, keepdims=True)
        norm_sum[0, 3:4, :] = norm_sum[0, 3:4, :] + jnp.sum(grad, axis=0, keepdims=True)
    for k in range(chunks):
        gathers[k].forward()
    far.wait_recv()
    passed = net.send(patch.at[m2], patch.at[m2], by_core)
    for k in range(chunks):
        gathers[k].finish()
        net.sent(gathers[k].far)
        net.sent(gathers[k].near)
        net.sent(gathers[k].passed)
    near.wait_recv()
    passed.wait_recv()
    top_row = iota((16, width), 0) == 0
    per_chunk = BLOCK // SHORT_LEN

    def mend(model, carry):
        fresh = patch[model].astype(f32)
        for i in range(per_short):
            at = (i // per_chunk) * span + model * BLOCK + (i % per_chunk) * SHORT_LEN
            rows = pl.ds(pl.multiple_of(at, 16), 16)
            new = jnp.concatenate(
                [fresh[i : i + 1], fresh[per_short + i : per_short + i + 1]], axis=1
            )
            gb[rows, :] = jnp.where(top_row, new, gb[rows, :].astype(f32)).astype(bf16)
        return carry

    lax.fori_loop(0, n_model, mend, 0)

    def feed_back(k):
        def one(at):
            rows = pl.ds(pl.multiple_of(k * span + at, 512), 512)
            gp[rows, :] = (nt(gb[rows, :], downw[...]) * slope[rows, :]).astype(bf16)

        tiles(span, 512, one)

        def two(at):
            rows = pl.ds(pl.multiple_of(k * span + at, 512), 512)
            partial[k][pl.ds(at, 512), :] = nt(gp[rows, :], upw[...])

        tiles(span, 512, two)

    def weight_grad(target, base, rows, left, right, left_at=0):
        step = 64

        def one(at):
            part = tn(left[:, pl.ds(pl.multiple_of(left_at + at, 64), step)], right[...])
            target[pl.ds(pl.multiple_of(base + at, 16), step), :] = part.astype(bf16)

        tiles(rows, step, one)

    def begin(first, last, left, right, keep=None):
        base = made = part_at[first]
        for at in range(0, left.shape[1], 256):
            part = tn(left[:, at : at + 256], right[...]).astype(bf16)
            count = 256 if keep is None else keep
            s.grads[pl.ds(made, count), :] = part[:count]
            made += count
            while first < last and part_at[first] + part_rows[first] <= made:
                reduces[first].start()
                first += 1

    begin(0, 4, act, gb)
    scatters = pipeline([], feed_back, middle=((), (0,)))
    begin(4, 8, norm, gp)
    before_end = ((1, 0), (2, 1, 0))
    gathers = []
    for k in range(chunks):
        steps(*before_end[k])
        grad = s.second[own_rows(k), :] + scatters[k].end()
        normal = s.normal_one[own_rows(k), :]
        norm_sum[0, 0:1, :] = norm_sum[0, 0:1, :] + jnp.sum(grad * normal, axis=0, keepdims=True)
        norm_sum[0, 1:2, :] = norm_sum[0, 1:2, :] + jnp.sum(grad, axis=0, keepdims=True)
        back = norm_back(grad, normal, s.scale_one[own_rows(k), 0:1], gain_one)
        s.second[own_rows(k), :] = back
        gm[rows_of(m, k), :] = back.astype(bf16)
        gathers.append(Gather(gm, k))
    norm_send()
    steps(3, 2)

    def attend_back(k):
        def unmix(at):
            rows = pl.ds(pl.multiple_of(k * span + at, 512), 512)
            s.gatt[rows, :] = nt(gm[rows, :], mixw[...]).astype(bf16)

        tiles(span, 512, unmix)

        units = [(model, h) for model in range(n_model) for h in range(heads)]
        grads_out, grads_probs = [], []
        for model, h in units:
            rows = rows_of(model, k)
            grad_out = s.gatt[rows, pl.ds((h // 2) * BLOCK, BLOCK)] * head_masks[h % 2]
            grads_out.append(grad_out)
            grads_probs.append(nt(head_parts(proj, rows, h, 2), grad_out))
        lows, grads_scores = [], []
        for unit, grad_probs in zip(units, grads_probs, strict=True):
            weight = probs[(k, *unit)]
            inner = jnp.sum(weight * grad_probs, axis=0, keepdims=True)
            lows.append(weight.astype(bf16))
            grads_scores.append((weight * (grad_probs - inner)).astype(bf16))
        outs = {}
        for i, (model, h) in enumerate(units):
            rows = rows_of(model, k)
            outs[0, model, h] = tn(grads_scores[i], head_parts(proj, rows, h, 1)) * 0.125
            outs[1, model, h] = nn(grads_scores[i], head_parts(proj, rows, h, 0)) * 0.125
            outs[2, model, h] = nn(lows[i], grads_out[i])
        for model in range(n_model):
            for part in range(3):
                for g in range(pad // BLOCK):
                    second = outs.get((part, model, 2 * g + 1))
                    if second is None:
                        second = jnp.zeros((BLOCK, BLOCK), f32)
                    both = jnp.where(first_half, outs[part, model, 2 * g], second)
                    gproj[rows_of(model, k), pl.ds(part * pad + g * BLOCK, BLOCK)] = both.astype(
                        bf16
                    )

        def one(at):
            rows = pl.ds(pl.multiple_of(k * span + at, 512), 512)
            partial[k][pl.ds(at, 512), :] = nn(gproj[rows, :], wt[...])

        tiles(span, 512, one)

    scatters = pipeline(
        gathers,
        attend_back,
        forward=((1, NORM, 4, 0), (2, 5, 1, 4)),
        middle=((NORM, 0, 6), (3, 2, 5, 7, NORM)),
        finish=((3,), ()),
        also=lambda: begin(8, 9, att, gm, cols),
    )
    begin(9, 12, gproj, x, cols)
    steps(1, 4, 6, 0)
    before_end = ((), (3, 2, 8, 5))
    swap_sent(s.returned, row_sems)
    for k in range(chunks):
        steps(*before_end[k])
        grad = s.second[own_rows(k), :] + scatters[k].end()
        s.grad_in[own_rows(k), :] = grad.astype(bf16)

    def pack(at):
        rows = pl.ds(at, 256)
        s.outgoing[rows, :] = nn(s.place[rows, :], s.grad_in[...]).astype(bf16)

    tiles(slots, 256, pack)
    swap_start(s.outgoing, s.incoming, out_sems)

    tail = [7, NORM, 9, 4, 6, 3, 10, 8, 5, 11, 1, 2, 9, 7, NORM, 4, 6, 10, 3]
    rest_of_tail = [8, 5, 11, 4, 9, 7, 6, 5, 10, 8, 11, 9, 7, 6, 10, 8]
    rest_of_tail += [11, 9, 7, 10, 11, 8, 9, 10, 11]
    if resident:
        moments = [
            pltpu.make_async_copy(first_hbm, first_out, s.load_sems.at[0]),
            pltpu.make_async_copy(second_hbm, second_out, s.load_sems.at[1]),
        ]
        for copy in moments:
            copy.start()
    steps(*tail)
    swap_arrived(s.incoming, out_sems)
    if resident:
        for copy in moments:
            copy.wait()
        rows = table_rows // 8
        for at in range(8):
            here = pl.ds(at * rows, rows)
            first_new, second_new, step = table_update(
                s.ids[0:1, :],
                s.incoming[...],
                first_out[here, :],
                second_out[here, :],
                step_out[here, :],
                at * rows,
            )
            first_out[here, :] = first_new
            second_out[here, :] = second_new
            step_out[here, :] = step
            steps(*rest_of_tail[2 * at : 2 * at + 2])
        rest_of_tail = rest_of_tail[16:]
    steps(*rest_of_tail)
    while any(item.todo for item in reduces):
        steps(*(i for i, item in enumerate(reduces) if item.todo))
    while len(norm_done) < len(stages):
        norm_step()
    norm_out[...] = norm_sum[len(stages)]
    if not resident:
        outs = [
            pltpu.make_async_copy(sums, weight_out, s.load_sems.at[0]),
            pltpu.make_async_copy(s.incoming, incoming_out, s.load_sems.at[1]),
            pltpu.make_async_copy(s.ids, ids_hbm, s.load_sems.at[2]),
        ]
        for copy in outs:
            copy.start()
        for copy in outs:
            copy.wait()
    net.drain()
    pool_wait(0)
    swap_sent(s.asked, ask_sems)
    swap_sent(s.incoming, out_sems)


def table_update(ids, incoming, first, second, table, base):
    rows, slots = first.shape[0], incoming.shape[0]
    hot = (iota((rows, slots), 0) + base == ids).astype(f32)
    uses = jnp.sum(hot, axis=1, keepdims=True)
    row_grad = nn(hot.astype(bf16), incoming) * (1.0 / jnp.maximum(uses, 1.0))
    first_new = 0.9 * first + 0.1 * row_grad
    second_new = 0.95 * second + 0.05 * row_grad * row_grad
    scale = jnp.sqrt(second_new * (1.0 / second_fix)) + 1e-08
    return first_new, second_new, first_new * (1.0 / first_fix) / scale + 0.01 * table


def finish_kernel(
    cols,
    block_ref,
    norm_ref,
    loss_ref,
    low,
    step_ref,
    first_ref,
    second_ref,
    step_hbm,
    first_out,
    second_out,
    down_out,
    up_out,
    mix_out,
    heads_out,
    loss_out,
    *rest,
):
    norm_outs, block_out = rest[:4], rest[4]
    wide, state_sems, wide_sems = rest[5:]
    width = low.shape[1]
    states = [
        pltpu.make_async_copy(src, dst, state_sems.at[i])
        for i, (src, dst) in enumerate(
            (
                (step_ref, step_hbm),
                (first_ref, first_out),
                (second_ref, second_out),
                (block_ref, block_out),
            )
        )
    ]
    for copy in states:
        copy.start()
    loss_out[...] = loss_ref[0:1, 0:1]
    for i, out in enumerate(norm_outs):
        out[...] = norm_ref[i, :]
    starts = (0, width, 2 * width, 2 * width + cols, 3 * width)
    wides = []
    for i, out in enumerate((down_out, up_out, mix_out, heads_out)):
        count = starts[i + 1] - starts[i]
        here = pl.ds(starts[i], count)
        step = 96

        def one(at, carry, base=starts[i]):
            rows = pl.ds(pl.multiple_of(base + at * step, 16), step)
            wide[rows, :] = low[rows, :].astype(f32)
            return carry

        lax.fori_loop(0, count // step, one, 0)
        wides.append(pltpu.make_async_copy(wide.at[here], out, wide_sems.at[i]))
        wides[-1].start()
    for copy in states + wides:
        copy.wait()


def table_kernel(
    cols,
    ids_ref,
    norm_ref,
    loss_ref,
    incoming_hbm,
    weights_hbm,
    table_hbm,
    first_hbm,
    second_hbm,
    step_hbm,
    first_out,
    second_out,
    down_out,
    up_out,
    mix_out,
    heads_out,
    loss_out,
    *rest,
):
    norm_outs = rest[:4]
    incoming, low, wide, state, in_sems, out_sems, low_sems, wide_sems = rest[4:]
    slots, width = incoming.shape
    parts = in_sems.shape[1]
    rows = state.shape[1] // parts

    def tile(at):
        return pl.ds(pl.multiple_of(at * rows, 8), rows)

    def load(i, at):
        src = (first_hbm, second_hbm, table_hbm)[i]
        return pltpu.make_async_copy(
            src.at[tile(at)], state.at[i, tile(at)], in_sems.at[i, at]
        )

    def store(i, at):
        dst = (first_out, second_out, step_hbm)[i]
        return pltpu.make_async_copy(
            state.at[i, tile(at)], dst.at[tile(at)], out_sems.at[i, at]
        )

    def each_part(step):
        def one(at, carry):
            for i in range(3):
                step(i, at)
            return carry

        lax.fori_loop(0, parts, one, 0)

    named = pltpu.make_async_copy(incoming_hbm, incoming, low_sems.at[0])
    named.start()
    lows = []
    for i in range(3):
        here = pl.ds(i * width, width)
        lows.append(
            pltpu.make_async_copy(weights_hbm.at[here], low.at[here], low_sems.at[1 + i])
        )
    for copy in lows[:1]:
        copy.start()
    each_part(lambda i, at: load(i, at).start())
    for copy in lows[1:]:
        copy.start()
    loss_out[...] = loss_ref[0:1, 0:1]
    for i, out in enumerate(norm_outs):
        out[...] = norm_ref[i, :]
    named.wait()

    wides = []
    starts = (0, width, 2 * width, 2 * width + cols, 3 * width)
    for i, out in enumerate((down_out, up_out, mix_out, heads_out)):
        here = pl.ds(starts[i], starts[i + 1] - starts[i])
        wides.append(pltpu.make_async_copy(wide.at[here], out, wide_sems.at[i]))

    def widen(i):
        lows[i].wait()
        step = 96

        def one(at, carry):
            here = pl.ds(pl.multiple_of(i * width + at * step, 16), step)
            wide[here, :] = low[here, :].astype(f32)
            return carry

        lax.fori_loop(0, width // step, one, 0)
        for copy in wides[i : i + 1] if i < 2 else wides[2:]:
            copy.start()

    widen(0)

    def update(at, carry):
        for i in range(3):
            load(i, at).wait()
        here = tile(at)
        first_new, second_new, step = table_update(
            ids_ref[0:1, :],
            incoming[...],
            state[0, here, :],
            state[1, here, :],
            state[2, here, :],
            at * rows,
        )
        state[0, here, :] = first_new
        state[1, here, :] = second_new
        state[2, here, :] = step
        for i in range(3):
            store(i, at).start()
        return carry

    lax.fori_loop(0, parts, update, 0)
    widen(1)
    widen(2)
    each_part(lambda i, at: store(i, at).wait())
    for copy in wides:
        copy.wait()


def body(
    token_owner,
    token_row,
    long_len,
    short_len,
    pairing,
    embed_table,
    first_moment,
    second_moment,
    heads_weight,
    mix_weight,
    up_weight,
    down_weight,
    first_gain,
    first_shift,
    second_gain,
    second_shift,
    upper_grad,
):
    tok, width = upper_grad.shape
    n_model, n_data = lax.axis_size("mp"), lax.axis_size("dp")
    devices = n_model * n_data
    group = tok * n_model
    cols = heads_weight.shape[2]
    pad = -(-cols // BLOCK) * BLOCK
    ff = up_weight.shape[1]
    slots = devices * SLOTS
    chunks = tok // BLOCK
    span = BLOCK * n_model
    per_short = tok // SHORT_LEN
    firsts = devices * per_short
    table_rows = embed_table.shape[0]
    bits = n_data.bit_length() - 1
    vmem = pltpu.VMEM
    dma = pltpu.SemaphoreType.DMA
    shapes = dict(
        table=vmem((table_rows, width), bf16),
        wt=vmem((3 * pad, width), bf16),
        mixw=vmem((pad, width), bf16),
        upw=vmem((width, ff), bf16),
        downw=vmem((ff, width), bf16),
        upper=vmem((tok, width), bf16),
        ask=vmem((slots, 128), bf16),
        asked=vmem((slots, 128), bf16),
        place=vmem((slots, tok), bf16),
        pick=vmem((tok, slots), bf16),
        found=vmem((slots, width), bf16),
        returned=vmem((slots, width), bf16),
        x=vmem((group, width), bf16),
        proj=vmem((group, 3 * pad), bf16),
        att=vmem((group, pad), bf16),
        gatt=vmem((group, pad), bf16),
        probs=vmem((chunks, n_model, cols // HEAD, BLOCK, BLOCK), f32),
        near_send=vmem((chunks, 2, BLOCK, width), bf16),
        near_land=vmem((chunks, 2, BLOCK, width), bf16),
        far_send=vmem((chunks, BLOCK, width), bf16),
        far_land=vmem((chunks, BLOCK, width), bf16),
        scale_one=vmem((tok, 128), f32),
        norm=vmem((group, width), bf16),
        act=vmem((group, ff), bf16),
        scale_two=vmem((tok, 128), f32),
        patch=vmem((n_model, 2 * per_short, width // 2), bf16),
        pool=vmem((n_data, n_model, 2 * per_short, width // 2), bf16),
        left=vmem((firsts, width // 2), bf16),
        right=vmem((firsts, width // 2), bf16),
        gram=vmem((firsts, firsts), f32),
        known=vmem((8, firsts), f32),
        known_col=vmem((firsts, 128), f32),
        gb=vmem((group, width), bf16),
        gm=vmem((group, width), bf16),
        grad_in=vmem((tok, width), bf16),
        norm_sum=vmem((3 + bits, 8, width), f32),
        norm_land=vmem((2 + bits, 8, width), f32),
        grads=vmem((3 * width, width), bf16),
        sum_land=vmem((12, 2 * cols + 64, width // 2), bf16),
        send_sems=dma((32,)),
        recv_sems=dma((20 + 25 * bits,)),
        owner=vmem((1, group), i32),
        rowid=vmem((1, group), i32),
        long=pltpu.SMEM(long_len.shape, i32),
        short=pltpu.SMEM(short_len.shape, i32),
        pairing=vmem((1, pairing.shape[0]), i32),
        gain_one=vmem((width,), f32),
        shift_one=vmem((width,), f32),
        gain_two=vmem((width,), f32),
        shift_two=vmem((width,), f32),
        small_sems=dma((9,)),
        load_sems=dma((8,)),
        table_sems=dma((max(4, table_rows // span),)),
        ids=vmem((8, slots), i32),
        ask_sems=dma((2,)),
        row_sems=dma((2,)),
        out_sems=dma((2,)),
        pool_sems=dma((2,)),
    )
    resident = devices <= 32
    if not resident:
        shapes.update(
            wide_a=vmem((2 * group, width), f32),
            wide_b=vmem((6 * tok, width), f32),
            sums=vmem((3 * width, width), bf16),
        )
    dims = SimpleNamespace(
        resident=resident,
        n_data=n_data,
        n_model=n_model,
        names=tuple(shapes),
        tok=tok,
        width=width,
        cols=cols,
        pad=pad,
        ff=ff,
        longs=long_len.shape[1],
        shorts=short_len.shape[1],
    )
    in_vmem = pl.BlockSpec(memory_space=pltpu.VMEM)
    in_hbm = pl.BlockSpec(memory_space=pl.ANY)
    heads_rows = jnp.transpose(heads_weight, (1, 2, 0)).reshape(3 * cols, width)
    whole = jax.ShapeDtypeStruct((table_rows, width), f32)
    out_shape = (
        jax.ShapeDtypeStruct((tok, width), bf16),
        jax.ShapeDtypeStruct((8, width), f32),
        jax.ShapeDtypeStruct((8, 128), f32),
    )
    if resident:
        out_shape = (vmem((tok, width), bf16), vmem((8, width), f32), vmem((8, 128), f32))
        out_shape += (vmem((3 * width, width), bf16),) + (vmem((table_rows, width), f32),) * 3
        out_specs = (in_vmem,) * 7
    else:
        out_shape += (
            jax.ShapeDtypeStruct((3 * width, width), bf16),
            jax.ShapeDtypeStruct((slots, width), bf16),
            jax.ShapeDtypeStruct((8, slots), i32),
        )
        out_specs = (in_vmem,) * 3 + (in_hbm,) * 3
    block_out, norms, loss, *more = pl.pallas_call(
        functools.partial(layer_kernel, dims),
        out_shape=out_shape,
        in_specs=[in_hbm] * 17,
        out_specs=out_specs,
        scratch_shapes=list(shapes.values()),
        compiler_params=pltpu.CompilerParams(
            collective_id=0,
            has_side_effects=True,
            vmem_limit_bytes=(40 if resident else 63) * 2**20,
        ),
    )(
        token_owner.reshape(1, group),
        token_row.reshape(1, group),
        long_len,
        short_len,
        pairing.reshape(1, -1),
        first_gain,
        first_shift,
        second_gain,
        second_shift,
        embed_table,
        heads_rows,
        mix_weight,
        up_weight,
        down_weight,
        upper_grad,
        first_moment,
        second_moment,
    )
    out_shape = (
        (whole, whole, whole)
        + tuple(jax.ShapeDtypeStruct((rows, width), f32) for rows in (ff, width, cols, 3 * cols))
        + (jax.ShapeDtypeStruct((1, 1), f32),)
        + (jax.ShapeDtypeStruct((width,), f32),) * 4
    )
    out_specs = (in_hbm,) * 7 + (in_vmem,) * 5
    if resident:
        finished = pl.pallas_call(
            functools.partial(finish_kernel, cols),
            out_shape=out_shape + (jax.ShapeDtypeStruct((tok, width), bf16),),
            in_specs=[in_vmem] * 7,
            out_specs=out_specs + (in_hbm,),
            scratch_shapes=[vmem((3 * width, width), f32), dma((4,)), dma((4,))],
            compiler_params=pltpu.CompilerParams(vmem_limit_bytes=20 * 2**20),
        )(block_out, norms, loss, *more)
        *finished, block_out = finished
    else:
        weights, incoming, ids = more
        parts = 8
        finished = pl.pallas_call(
            functools.partial(table_kernel, cols),
            out_shape=out_shape,
            in_specs=[in_vmem] * 3 + [in_hbm] * 5,
            out_specs=out_specs,
            scratch_shapes=[
                vmem((slots, width), bf16),
                vmem((3 * width, width), bf16),
                vmem((3 * width, width), f32),
                vmem((3, table_rows, width), f32),
                dma((3, parts)),
                dma((3, parts)),
                dma((4,)),
                dma((4,)),
            ],
            compiler_params=pltpu.CompilerParams(vmem_limit_bytes=63 * 2**20),
        )(ids, norms, loss, incoming, weights, embed_table, first_moment, second_moment)
    table_step, first_new, second_new, down_grad, up_grad, mix_grad, heads_grad, loss = finished[:8]
    norm_grads = finished[8:]
    return (
        loss.reshape(()),
        block_out,
        jnp.transpose(heads_grad.reshape(3, cols, width), (2, 0, 1)),
        mix_grad,
        up_grad,
        down_grad,
        *norm_grads,
        table_step,
        first_new,
        second_new,
    )


def solution(mesh):
    rows = P(("dp", "mp"), None)
    in_specs = (
        P("dp", None),
        P("dp"),
        P("dp", None),
        P("dp", None),
        P(),
        rows,
        rows,
        rows,
        P(None, None, "mp"),
        P("mp", None),
        P(None, "mp"),
        P("mp", None),
        P(),
        P(),
        P(),
        P(),
        rows,
    )
    out_specs = (
        P(),
        rows,
        P(None, None, "mp"),
        P("mp", None),
        P(None, "mp"),
        P("mp", None),
        P(),
        P(),
        P(),
        P(),
        rows,
        rows,
        rows,
    )
    return jax.shard_map(body, mesh=mesh, in_specs=in_specs, out_specs=out_specs, check_vma=False)
```

```python
import functools
from types import SimpleNamespace

import jax
import jax.numpy as jnp
from jax import lax
from jax.experimental import pallas as pl
from jax.experimental.pallas import tpu as pltpu
from jax.sharding import PartitionSpec as P

HEAD = 64
LONG_LEN = 128
SHORT_LEN = 32
BLOCK = 128
SLOTS = 16
NORM = -1
MESH = pl.DeviceIdType.MESH
bf16 = jnp.bfloat16
f32 = jnp.float32
i32 = jnp.int32

first_fix = 1.0 - 0.9**10
second_fix = 1.0 - 0.95**10


def nn(left, right):
    return lax.dot_general(left, right, (((1,), (0,)), ((), ())), preferred_element_type=f32)


def nt(left, right):
    return lax.dot_general(left, right, (((1,), (1,)), ((), ())), preferred_element_type=f32)


def tn(left, right):
    return lax.dot_general(left, right, (((0,), (0,)), ((), ())), preferred_element_type=f32)


def iota(shape, axis):
    return lax.broadcasted_iota(i32, shape, axis)


def column_of(row):
    count = row.shape[1]
    eye = iota((count, count), 0) == iota((count, count), 1)
    return jnp.sum(jnp.where(eye, row, 0.0), axis=1, keepdims=True)


def mean_of(values):
    return jnp.mean(values, axis=-1, keepdims=True)


def norm_forward(hidden):
    centered = hidden - mean_of(hidden)
    scale = lax.rsqrt(mean_of(centered * centered) + 1e-12)
    return centered * scale, scale


def norm_back(grad, normal, scale, gain):
    scaled = grad * gain
    return scale * (scaled - mean_of(scaled) - normal * mean_of(scaled * normal))


class Net:
    def __init__(self, send_sems, recv_sems):
        self.send_sems, self.recv_sems = send_sems, recv_sems
        self.open = [None] * send_sems.shape[0]
        self.count = 0
        self.names = {}

    def send(self, src, dst, device, name=None):
        slot = self.count % len(self.open)
        if self.open[slot] is not None:
            self.open[slot].wait_send()
        at = self.names.setdefault(self.count if name is None else name, len(self.names))
        self.count += 1
        copy = pltpu.make_async_remote_copy(
            src_ref=src,
            dst_ref=dst,
            send_sem=self.send_sems.at[slot],
            recv_sem=self.recv_sems.at[at],
            device_id=device,
            device_id_type=MESH,
        )
        copy.start()
        self.open[slot] = copy
        return copy

    def sent(self, copy):
        for slot, item in enumerate(self.open):
            if item is copy:
                copy.wait_send()
                self.open[slot] = None

    def drain(self):
        for copy in self.open:
            if copy is not None:
                copy.wait_send()
        self.open = [None] * len(self.open)


class Reduce:
    def __init__(self, net, part, whole, land, place, bits):
        self.net, self.part, self.whole, self.land = net, part, whole, land
        self.data_pos, self.model_pos = place
        self.bits = bits
        rows, width = part.shape
        self.half = width // 2
        self.row, self.len = 0, rows
        self.offset = 0
        self.stage = 0
        self.halved = []
        grows = sum(1 for stage in range(len(bits)) if self.halves(stage))
        self.todo = [self.add] * len(bits) + [self.grow] * grows

    def step(self):
        if self.todo:
            self.todo.pop(0)()

    def halves(self, stage):
        return stage == 0 or (self.part.shape[0] >> (stage - 1)) % 32 == 0

    def partner(self, bit):
        mine = lax.rem(lax.div(self.data_pos, 1 << bit), 2)
        return mine, (self.data_pos + (1 - 2 * mine) * (1 << bit), self.model_pos)

    def start(self):
        mine, device = self.partner(self.bits[self.stage])
        halved = self.halves(self.stage)
        count = self.len
        if self.stage == 0:
            away = pl.multiple_of((1 - mine) * self.half, 128)
            self.col = pl.multiple_of(mine * self.half, 128)
            src = self.part.at[:, pl.ds(away, self.half)]
        else:
            away = self.row
            if halved:
                count = self.len // 2
                away = pl.multiple_of(self.row + (1 - mine) * count, 16)
                self.row = pl.multiple_of(self.row + mine * count, 16)
                self.len = count
            src = self.part.at[pl.ds(away, count), pl.ds(self.col, self.half)]
        self.halved.append(halved)
        self.now = self.land.at[pl.ds(self.offset, count)]
        self.offset += count
        self.copy = self.net.send(src, self.now, device)

    def add(self):
        self.copy.wait_recv()
        last = self.stage == len(self.bits) - 1
        if not self.halved[-1]:
            self.net.sent(self.copy)
        target = self.whole if last else self.part
        cols = pl.ds(self.col, self.half)
        step = 48 if self.len % 48 == 0 else min(self.len, 64)
        now, row, part = self.now, self.row, self.part

        def tile(at, carry):
            here = pl.multiple_of(at * step, 16)
            there = pl.ds(pl.multiple_of(row + here, 16), step)
            total = part[there, cols].astype(f32) + now[pl.ds(here, step), :].astype(f32)
            target[there, cols] = total.astype(bf16)
            return carry

        lax.fori_loop(0, self.len // step, tile, 0)
        if last:
            self.spread()
        else:
            self.stage += 1
            self.start()

    def spread(self):
        while self.stage and not self.halved[self.stage]:
            self.stage -= 1
        _, device = self.partner(self.bits[self.stage])
        rows = pl.ds(self.row, self.len) if self.stage else slice(None)
        here = self.whole.at[rows, pl.ds(self.col, self.half)]
        self.copy = self.net.send(here, here, device)

    def grow(self):
        self.copy.wait_recv()
        if self.stage == 0:
            return
        mine, _ = self.partner(self.bits[self.stage])
        self.row = pl.multiple_of(self.row - mine * self.len, 16)
        self.len *= 2
        self.stage -= 1
        self.spread()


def layer_kernel(
    dims,
    owner_hbm,
    rowid_hbm,
    long_hbm,
    short_hbm,
    pairing_hbm,
    gain_one_hbm,
    shift_one_hbm,
    gain_two_hbm,
    shift_two_hbm,
    table_hbm,
    heads_hbm,
    mix_hbm,
    up_hbm,
    down_hbm,
    upper_hbm,
    first_hbm,
    second_hbm,
    block_out,
    norm_out,
    loss_out,
    *rest,
):
    resident = dims.resident
    if resident:
        sums, step_out, first_out, second_out, *scratch = rest
    else:
        weight_out, incoming_out, ids_hbm, *scratch = rest
    n_data, n_model = dims.n_data, dims.n_model
    s = SimpleNamespace(**dict(zip(dims.names, scratch, strict=True)))
    tok, width, cols, pad, ff = dims.tok, dims.width, dims.cols, dims.pad, dims.ff
    devices = n_data * n_model
    group = tok * n_model
    chunks = tok // BLOCK
    span = BLOCK * n_model
    slots = devices * SLOTS
    table_rows = table_hbm.shape[0]

    if resident:
        wide_a, wide_b = first_out, second_out
    else:
        wide_a, wide_b, sums = s.wide_a, s.wide_b, s.sums
    slope = wide_a.at[pl.ds(0, group)]
    partial = [wide_a.at[pl.ds(group + k * span, span)] for k in range(chunks)]
    s.normal_one, s.normed, s.normal_two, s.rows, s.grad_rows, s.second = [
        wide_b.at[pl.ds(i * tok, tok)] for i in range(6)
    ]
    s.gproj = s.table.at[pl.ds(0, group)]
    s.gp = s.table.at[pl.ds(group, group)]
    s.outgoing = s.found
    s.incoming = s.returned
    d = lax.axis_index("dp")
    m = lax.axis_index("mp")
    me = d * n_model + m
    core = lax.rem(m, 2)
    side = lax.div(m, 2)
    m1 = m + 1 - 2 * core
    m2 = m + 2 - 4 * side
    m3 = m1 + m2 - m
    by_core = (d, m1)
    by_side = (d, m2)
    net = Net(s.send_sems, s.recv_sems)

    def at_device(place):
        return (lax.div(place, n_model), lax.rem(place, n_model))

    def other(j):
        return lax.rem(me + j, devices)

    owner_ref, rowid_ref, long_ref, short_ref = s.owner, s.rowid, s.long, s.short
    pairing_ref = s.pairing
    small = [
        pltpu.make_async_copy(src, dst, s.small_sems.at[i])
        for i, (src, dst) in enumerate(
            (
                (owner_hbm, s.owner),
                (rowid_hbm, s.rowid),
                (long_hbm, s.long),
                (short_hbm, s.short),
                (pairing_hbm, s.pairing),
                (gain_one_hbm, s.gain_one),
                (shift_one_hbm, s.shift_one),
                (gain_two_hbm, s.gain_two),
                (shift_two_hbm, s.shift_two),
            )
        )
    ]
    for copy in small:
        copy.start()

    barrier = pltpu.get_barrier_semaphore()

    def greet(j, carry):
        pl.semaphore_signal(barrier, inc=1, device_id=at_device(other(j)), device_id_type=MESH)
        return carry

    lax.fori_loop(1, devices, greet, 0)

    stage_rows = table_rows // 4 if resident else span
    table_parts = table_rows // stage_rows

    def table_part(at):
        if resident:
            return step_out.at[pl.ds(at * stage_rows, stage_rows)]
        return partial[at % 2]

    def table_copy(at):
        return pltpu.make_async_copy(
            table_hbm.at[pl.ds(at * stage_rows, stage_rows)],
            table_part(at),
            s.table_sems.at[at],
        )

    ahead = table_parts if resident else 2
    for at in range(ahead):
        table_copy(at).start()
    loads = []

    def load(src, dst):
        copy = pltpu.make_async_copy(src, dst, s.load_sems.at[len(loads)])
        copy.start()
        loads.append(copy)

    wt, mixw, upw, downw = s.wt, s.mixw, s.upw, s.downw
    for part in range(3):
        load(heads_hbm.at[pl.ds(part * cols, cols)], wt.at[pl.ds(part * pad, cols)])
        wt[pl.ds(part * pad + cols, pad - cols), :] = jnp.zeros((pad - cols, width), bf16)
    load(mix_hbm, mixw.at[pl.ds(0, cols)])
    mixw[pl.ds(cols, pad - cols), :] = jnp.zeros((pad - cols, width), bf16)
    load(up_hbm, upw)
    load(down_hbm, downw)
    load(upper_hbm, s.upper)

    for copy in small:
        copy.wait()
    own_at = pl.multiple_of(m * tok, 128)
    owner_row = owner_ref[:, pl.ds(own_at, tok)]
    rowid_row = rowid_ref[:, pl.ds(own_at, tok)]
    owned = iota((devices, tok), 0) == owner_row
    before = (iota((tok, tok), 0) < iota((tok, tok), 1)).astype(f32).astype(bf16)
    counted = nn(owned.astype(f32).astype(bf16), before)
    rank_row = jnp.sum(jnp.where(owned, counted, 0.0), axis=0, keepdims=True)
    slot_row = owner_row.astype(f32) * SLOTS + rank_row
    slot_row_int = slot_row.astype(i32)
    wanted_row = (rowid_row + 1).astype(f32)
    step = min(slots, 256)

    def place_slots(at, carry):
        here = pl.ds(pl.multiple_of(at * step, step), step)
        placed = iota((step, tok), 0) + at * step == slot_row_int
        wanted = jnp.sum(jnp.where(placed, wanted_row, 0.0), axis=1, keepdims=True)
        high = jnp.floor(wanted * (1.0 / 64.0))
        low = wanted - 64.0 * high
        s.ask[here, :] = jnp.where(iota((step, 128), 1) < 64, high, low).astype(bf16)
        s.place[here, :] = placed.astype(f32).astype(bf16)
        return carry

    lax.fori_loop(0, slots // step, place_slots, 0)
    slot_col = column_of(slot_row).astype(i32)
    s.pick[...] = (iota((tok, slots), 1) == slot_col).astype(f32).astype(bf16)

    pl.semaphore_wait(barrier, devices - 1)

    def slot_rows(place):
        return pl.ds(pl.multiple_of(place * SLOTS, SLOTS), SLOTS)

    def swap_copy(src, dst, sems, to):
        return pltpu.make_async_remote_copy(
            src_ref=src.at[slot_rows(to)],
            dst_ref=dst.at[slot_rows(me)],
            send_sem=sems.at[0],
            recv_sem=sems.at[1],
            device_id=at_device(to),
            device_id_type=MESH,
        )

    def swap_start(src, dst, sems):
        def one(j, carry):
            swap_copy(src, dst, sems, other(j)).start()
            return carry

        lax.fori_loop(1, devices, one, 0)
        dst[slot_rows(me), :] = src[slot_rows(me), :]

    def swap_wait(dst, sem):
        blocks = dst.at[pl.ds(0, slots - SLOTS)]
        pltpu.make_async_copy(blocks, blocks, sem).wait()

    def swap_arrived(dst, sems):
        swap_wait(dst, sems.at[1])

    def swap_sent(dst, sems):
        swap_wait(dst, sems.at[0])

    ask_sems, row_sems, out_sems = s.ask_sems, s.row_sems, s.out_sems
    swap_start(s.ask, s.asked, ask_sems)
    for at in range(table_parts):
        table_copy(at).wait()
        s.table[pl.ds(at * stage_rows, stage_rows), :] = table_part(at)[...].astype(bf16)
        if at + ahead < table_parts:
            table_copy(at + ahead).start()
    swap_arrived(s.asked, ask_sems)

    per_block = BLOCK // SLOTS

    def look(at, carry):
        block = lax.rem(lax.div(me, per_block) + at, slots // BLOCK)
        rows = pl.ds(pl.multiple_of(block * BLOCK, BLOCK), BLOCK)
        asked = s.asked[rows, :].astype(f32)
        ident = asked[:, 0:1] * 64.0 + asked[:, 64:65] - 1.0
        eye = iota((BLOCK, BLOCK), 0) == iota((BLOCK, BLOCK), 1)
        ident_row = jnp.sum(jnp.where(eye, ident, 0.0), axis=0, keepdims=True)
        s.ids[:, rows] = jnp.broadcast_to(ident_row.astype(i32), (8, BLOCK))
        hot = (iota((BLOCK, table_rows), 1) == ident.astype(i32)).astype(f32).astype(bf16)
        s.found[rows, :] = nn(hot, s.table[...]).astype(bf16)

        def one(i, inner):
            to = block * per_block + lax.rem(lax.rem(me, per_block) + i, per_block)

            @pl.when(to != me)
            def _():
                swap_copy(s.found, s.returned, row_sems, to).start()

            return inner

        lax.fori_loop(0, per_block, one, 0)
        return carry

    lax.fori_loop(0, slots // BLOCK, look, 0)
    s.returned[slot_rows(me), :] = s.found[slot_rows(me), :]
    for copy in loads:
        copy.wait()
    swap_arrived(s.returned, row_sems)

    def rows_of(model, k):
        return pl.ds(pl.multiple_of(k * span + model * BLOCK, BLOCK), BLOCK)

    def own_rows(k):
        return pl.ds(k * BLOCK, BLOCK)

    class Gather:
        def __init__(self, buffer, k):
            self.buffer, self.k = buffer, k
            mine = buffer.at[rows_of(m, k)]
            self.far = net.send(mine, mine, by_side, (k, 0))
            self.near = net.send(mine, mine, by_core, (k, 1))

        def forward(self):
            self.far.wait_recv()
            there = self.buffer.at[rows_of(m2, self.k)]
            self.passed = net.send(there, there, by_core, (self.k, 2))

        def finish(self):
            self.near.wait_recv()
            self.passed.wait_recv()

    class Scatter:
        last = {}

        def __init__(self, k):
            self.k = k
            for copy in Scatter.last.get(k, []):
                net.sent(copy)
            part = partial[k]
            self.near = []
            for r, model in ((0, m3), (1, m1)):
                here = pl.ds(pl.multiple_of(model * BLOCK, BLOCK), BLOCK)
                s.near_send[k, r] = part[here, :].astype(bf16)
                self.near.append(
                    net.send(s.near_send.at[k, r], s.near_land.at[k, r], by_core, (k, 3 + r))
                )

        def middle(self):
            k = self.k
            self.near[0].wait_recv()
            here = pl.ds(pl.multiple_of(m2 * BLOCK, BLOCK), BLOCK)
            total = partial[k][here, :] + s.near_land[k, 0].astype(f32)
            s.far_send[k] = total.astype(bf16)
            self.far = net.send(s.far_send.at[k], s.far_land.at[k], by_side, (k, 5))
            Scatter.last[k] = self.near + [self.far]

        def end(self):
            k = self.k
            self.near[1].wait_recv()
            here = pl.ds(pl.multiple_of(m * BLOCK, BLOCK), BLOCK)
            total = partial[k][here, :] + s.near_land[k, 1].astype(f32)
            self.far.wait_recv()
            return total + s.far_land[k].astype(f32)

    def tiles(total, step, fn):
        def one(at, carry):
            fn(pl.multiple_of(at * step, step))
            return carry

        lax.fori_loop(0, total // step, one, 0)

    x, proj, att, probs = s.x, s.proj, s.att, s.probs
    gathers = []
    for k in range(chunks):
        own = nn(s.pick[own_rows(k), :], s.returned[...])
        x[rows_of(m, k), :] = own.astype(bf16)
        gathers.append(Gather(x, k))

    lane = iota((BLOCK, BLOCK), 1)
    sub = iota((BLOCK, BLOCK), 0)
    first_half = lane < HEAD
    head_masks = [
        (lane < HEAD).astype(f32).astype(bf16),
        (lane >= HEAD).astype(f32).astype(bf16),
    ]
    heads = cols // HEAD
    long_blocks = n_model // 2
    per_long = tok // LONG_LEN
    per_short = tok // SHORT_LEN
    short_in_block = BLOCK // SHORT_LEN

    def key_mask(model, k, is_long):
        if is_long:
            return sub < long_ref[0, model * per_long + k]
        keep = None
        for j in range(short_in_block):
            size = short_ref[0, (model - long_blocks) * per_short + k * short_in_block + j]
            start = j * SHORT_LEN
            ok = (sub >= start) & (sub < start + size) & (lane >= start) & (lane < start + SHORT_LEN)
            keep = ok if keep is None else keep | ok
        return keep

    def head_parts(source, rows, h, part):
        g = h // 2
        return source[rows, pl.ds(part * pad + g * BLOCK, BLOCK)]

    def attend(k):
        def project(at):
            rows = pl.ds(pl.multiple_of(k * span + at, 512), 512)
            proj[rows, :] = nt(x[rows, :], wt[...]).astype(bf16)

        tiles(span, 512, project)

        units = [(model, h) for model in range(n_model) for h in range(heads)]
        keeps = [key_mask(model, k, model < long_blocks) for model in range(n_model)]
        scores = []
        for model, h in units:
            rows = rows_of(model, k)
            query = head_parts(proj, rows, h, 0) * head_masks[h % 2]
            scores.append(nt(head_parts(proj, rows, h, 1), query))
        weights = []
        for (model, h), score in zip(units, scores, strict=True):
            score = jnp.where(keeps[model], score * 0.125, -1e30)
            part = jnp.exp(score - jnp.max(score, axis=0, keepdims=True))
            weights.append(part * (1.0 / jnp.sum(part, axis=0, keepdims=True)))
        outs = {}
        for unit, weight in zip(units, weights, strict=True):
            value = head_parts(proj, rows_of(unit[0], k), unit[1], 2)
            outs[unit] = tn(weight.astype(bf16), value)
        for unit, weight in zip(units, weights, strict=True):
            probs[(k, *unit)] = weight
        for model in range(n_model):
            for g in range(pad // BLOCK):
                second = outs.get((model, 2 * g + 1))
                if second is None:
                    second = jnp.zeros((BLOCK, BLOCK), f32)
                both = jnp.where(first_half, outs[model, 2 * g], second)
                att[rows_of(model, k), pl.ds(g * BLOCK, BLOCK)] = both.astype(bf16)

        def mix(at):
            rows = pl.ds(pl.multiple_of(k * span + at, 512), 512)
            partial[k][pl.ds(at, 512), :] = nn(att[rows, :], mixw[...])

        tiles(span, 512, mix)

    nothing = ((),) * chunks

    def pipeline(gathers, work, forward=nothing, middle=nothing, finish=nothing, also=None):
        scatters = []
        for k in range(chunks):
            if gathers:
                steps(*forward[k])
                gathers[k].forward()
            if k:
                steps(*middle[k - 1])
                scatters[k - 1].middle()
            if gathers:
                steps(*finish[k])
                gathers[k].finish()
            if also is not None and k == chunks - 1:
                also()
            work(k)
            scatters.append(Scatter(k))
        steps(*middle[-1])
        scatters[-1].middle()
        return scatters

    bits = tuple(range(n_data.bit_length() - 1))
    part_rows = [ff // 4] * 4 + [width // 4] * 4 + [cols] * 4
    part_at = [sum(part_rows[:i]) for i in range(len(part_rows))]
    reduces = [
        Reduce(
            net,
            s.grads.at[pl.ds(at, rows)],
            sums.at[pl.ds(at, rows)],
            s.sum_land.at[i],
            (d, m),
            bits if i else bits[1::-1] + bits[2:],
        )
        for i, (at, rows) in enumerate(zip(part_at, part_rows, strict=True))
    ]
    norm_sum = s.norm_sum
    norm_copies, norm_done = [], []
    stages = [by_core, by_side] + [reduces[0].partner(bit)[1] for bit in bits]

    def norm_send():
        at = len(norm_copies)
        if at < len(stages):
            norm_copies.append(net.send(norm_sum.at[at], s.norm_land.at[at], stages[at]))

    def norm_step():
        at = len(norm_copies) - 1
        norm_copies[at].wait_recv()
        norm_sum[at + 1] = norm_sum[at] + s.norm_land[at]
        norm_done.append(at)
        norm_send()

    def steps(*order):
        for at in order:
            if at == NORM:
                norm_step()
            else:
                reduces[at].step()

    scatters = pipeline(gathers, attend)

    gain_one, shift_one, gain_two, shift_two = [
        ref[...].reshape(1, width)
        for ref in (s.gain_one, s.shift_one, s.gain_two, s.shift_two)
    ]
    norm, act = s.norm, s.act
    gathers = []
    for k in range(chunks):
        hidden = x[rows_of(m, k), :].astype(f32) + scatters[k].end()
        normal, scale = norm_forward(hidden)
        s.normal_one[own_rows(k), :] = normal
        s.scale_one[own_rows(k), :] = jnp.broadcast_to(scale, (BLOCK, 128))
        normed = normal * gain_one + shift_one
        s.normed[own_rows(k), :] = normed
        norm[rows_of(m, k), :] = normed.astype(bf16)
        gathers.append(Gather(norm, k))

    def feed(k):
        def one(at):
            rows = pl.ds(pl.multiple_of(k * span + at, 512), 512)
            pre = nn(norm[rows, :], upw[...])
            cumulative = 0.5 * (1.0 + lax.erf(pre * 0.7071067811865476))
            act[rows, :] = (pre * cumulative).astype(bf16)
            slope[rows, :] = cumulative + pre * (0.3989422804014327 * jnp.exp(-0.5 * pre * pre))

        tiles(span, 512, one)

        def two(at):
            rows = pl.ds(pl.multiple_of(k * span + at, 512), 512)
            partial[k][pl.ds(at, 512), :] = nn(act[rows, :], downw[...])

        tiles(span, 512, two)

    scatters = pipeline(gathers, feed)

    gb, gp, gm, gproj = s.gb, s.gp, s.gm, s.gproj

    def second_back(k):
        rows = own_rows(k)
        return norm_back(
            s.grad_rows[rows, :], s.normal_two[rows, :], s.scale_two[rows, 0:1], gain_two
        )

    def early_gather(k):
        gb[rows_of(m, k), :] = second_back(k).astype(bf16)
        gathers.append(Gather(gb, k))

    s.grad_rows[...] = s.upper[...].astype(f32)
    gathers = []
    for k in range(chunks):
        hidden = s.normed[own_rows(k), :] + scatters[k].end()
        normal, scale = norm_forward(hidden)
        s.normal_two[own_rows(k), :] = normal
        s.scale_two[own_rows(k), :] = jnp.broadcast_to(scale, (BLOCK, 128))
        rows_now = normal * gain_two + shift_two
        s.rows[own_rows(k), :] = rows_now
        block_out[own_rows(k), :] = rows_now.astype(bf16)
        if k < chunks - 1:
            early_gather(k)

    pool = s.pool
    half = width // 2
    firsts = jnp.concatenate(
        [s.rows[pl.ds(i * SHORT_LEN, 1), :] for i in range(per_short)], axis=0
    )
    pool[d, m] = jnp.concatenate([firsts[:, :half], firsts[:, half:]], axis=0).astype(bf16)

    def pool_copy(j, model):
        return pltpu.make_async_remote_copy(
            src_ref=pool.at[d, m],
            dst_ref=pool.at[d, m],
            send_sem=s.pool_sems.at[0],
            recv_sem=s.pool_sems.at[1],
            device_id=(lax.rem(d + j, n_data), model),
            device_id_type=MESH,
        )

    def pool_start(j, carry):
        pool_copy(j, m).start()
        pool_copy(j, m2).start()
        return carry

    def pool_wait(at):
        blocks = pool.at[pl.ds(0, (2 * n_data - 1) // 3), pl.ds(0, 3)]
        pltpu.make_async_copy(blocks, blocks, s.pool_sems.at[at]).wait()

    lax.fori_loop(1, n_data, pool_start, 0)
    pool_copy(0, m2).start()
    early_gather(chunks - 1)
    pool_wait(1)
    near = net.send(pool.at[:, m], pool.at[:, m], by_core)
    passed = net.send(pool.at[:, m2], pool.at[:, m2], by_core)
    near.wait_recv()
    passed.wait_recv()

    count = devices * per_short
    sentences = dims.longs + dims.shorts
    pairs2 = pairing_ref.shape[1]

    def sentence_of(index):
        place = lax.div(index, per_short)
        slot = lax.rem(index, per_short)
        model = lax.rem(place, n_model)
        data = lax.div(place, n_model)
        ratio = LONG_LEN // SHORT_LEN
        is_long = model < long_blocks
        valid = jnp.logical_or(jnp.logical_not(is_long), lax.rem(slot, ratio) == 0)
        number = jnp.where(
            is_long,
            model * per_long + lax.div(slot, ratio),
            dims.longs + (model - long_blocks) * per_short + slot,
        )
        return jnp.where(valid, data * sentences + number, -1)

    group_rows_first = n_model * per_short

    def unfold(at, carry):
        part = pool[at].astype(f32)
        here = pl.ds(pl.multiple_of(at * group_rows_first, 16), group_rows_first)
        s.left[here, :] = part[:, :per_short, :].reshape(group_rows_first, half).astype(bf16)
        s.right[here, :] = part[:, per_short:, :].reshape(group_rows_first, half).astype(bf16)
        return carry

    lax.fori_loop(0, n_data, unfold, 0)
    gram, known = s.gram, s.known
    pair_col = column_of(pairing_ref[...].astype(f32)).astype(i32)
    step = 256 if count <= 256 else 128

    def measure(number, carry):
        at = number * step
        block = pl.ds(pl.multiple_of(at, 128), step)
        gram[:, block] = nt(s.left[...], s.left[block, :]) + nt(
            s.right[...], s.right[block, :]
        )
        sent = sentence_of(iota((1, step), 1) + at)
        place = jnp.sum(
            jnp.where(pair_col == sent, iota((pairs2, step), 0), 0).astype(f32),
            axis=0,
            keepdims=True,
        )
        place = jnp.where(sent >= 0, place, -2.0)
        pair = jnp.floor(place * 0.5)
        eye = iota((step, step), 0) == iota((step, step), 1)
        square = jnp.sum(jnp.where(eye, gram[block, block], 0.0), axis=0, keepdims=True)
        known[0:1, block] = lax.rsqrt(square + 1e-06)
        known[1:2, block] = pair
        known[2:3, block] = jnp.where(sent >= 0, place - 2.0 * pair, 5.0)
        for i in range(3):
            s.known_col[block, i : i + 1] = column_of(known[i : i + 1, block])
        return carry

    lax.fori_loop(0, count // step, measure, 0)

    def logits_of(part, block, inv_col, pair_col, side_col):
        inv_row, pair_row, side_row = known[0:1, block], known[1:2, block], known[2:3, block]
        facing = side_col + side_row == 1.0
        same = (pair_col == pair_row) & facing
        cosine = part * inv_col * inv_row
        return 40.0 * (cosine - jnp.where(same, 0.3, 0.0)), facing, same

    def lose(number, loss):
        block = pl.ds(pl.multiple_of(number * step, 128), step)
        logits, facing, same = logits_of(
            gram[:, block],
            block,
            s.known_col[:, 0:1],
            s.known_col[:, 1:2],
            s.known_col[:, 2:3],
        )
        masked = jnp.where(facing, logits, -1e30)
        top = jnp.max(masked, axis=0, keepdims=True)
        total = jnp.sum(jnp.where(facing, jnp.exp(masked - top), 0.0), axis=0, keepdims=True)
        valid = known[1:2, block] >= 0.0
        log_total = jnp.where(valid, top + jnp.log(jnp.where(valid, total, 1.0)), 0.0)
        known[3:4, block] = log_total
        matched = jnp.sum(jnp.where(same, logits, 0.0), axis=0, keepdims=True)
        return loss + jnp.sum(log_total - matched, axis=1, keepdims=True)

    loss = lax.fori_loop(0, count // step, lose, jnp.zeros((1, 1), f32))
    loss_out[...] = jnp.broadcast_to(loss * (2.0 / pairs2), loss_out.shape)

    own_first = pl.ds(pl.multiple_of(me * per_short, 8), per_short)
    mine_mask = iota((per_short, count), 1) == iota((per_short, count), 0) + me * per_short

    def own_col(row):
        return jnp.sum(jnp.where(mine_mask, row, 0.0), axis=1, keepdims=True)

    inv_row, log_row = known[0:1, :], known[3:4, :]
    inv_own, log_own = own_col(inv_row), own_col(log_row)
    logits, facing, same = logits_of(
        gram[own_first, :],
        slice(None),
        inv_own,
        own_col(known[1:2, :]),
        own_col(known[2:3, :]),
    )
    pull = jnp.exp(jnp.where(facing, logits - log_own, -1e30)) + jnp.exp(
        jnp.where(facing, logits - log_row, -1e30)
    )
    pull = 40.0 * (pull - jnp.where(same, 2.0, 0.0)) * inv_row
    pull_high = pull.astype(bf16)
    pull_low = (pull - pull_high.astype(f32)).astype(bf16)
    grad_unit = jnp.concatenate(
        [nn(pull_high, n[...]) + nn(pull_low, n[...]) for n in (s.left, s.right)], axis=1
    )
    unit = firsts * inv_own
    grad_firsts = inv_own * (
        grad_unit - unit * jnp.sum(unit * grad_unit, axis=1, keepdims=True)
    )
    grad_rows = s.grad_rows
    for i in range(per_short):
        at = pl.ds(i * SHORT_LEN, 1)
        grad_rows[at, :] = grad_rows[at, :] + grad_firsts[i : i + 1, :]


    norm_sum[0] = jnp.zeros((8, width), f32)
    for k in range(chunks):
        s.second[own_rows(k), :] = second_back(k)
    patch = s.patch
    firsts = jnp.concatenate(
        [s.second[pl.ds(i * SHORT_LEN, 1), :] for i in range(per_short)], axis=0
    )
    patch[m] = jnp.concatenate([firsts[:, :half], firsts[:, half:]], axis=0).astype(bf16)
    far = net.send(patch.at[m], patch.at[m], by_side)
    near = net.send(patch.at[m], patch.at[m], by_core)
    for k in range(chunks):
        grad = grad_rows[own_rows(k), :]
        normal = s.normal_two[own_rows(k), :]
        norm_sum[0, 2:3, :] = norm_sum[0, 2:3, :] + jnp.sum(grad * normal, axis=0, keepdims=True)
        norm_sum[0, 3:4, :] = norm_sum[0, 3:4, :] + jnp.sum(grad, axis=0, keepdims=True)
    for k in range(chunks):
        gathers[k].forward()
    far.wait_recv()
    passed = net.send(patch.at[m2], patch.at[m2], by_core)
    for k in range(chunks):
        gathers[k].finish()
        net.sent(gathers[k].far)
        net.sent(gathers[k].near)
        net.sent(gathers[k].passed)
    near.wait_recv()
    passed.wait_recv()
    top_row = iota((16, width), 0) == 0
    per_chunk = BLOCK // SHORT_LEN

    def mend(model, carry):
        fresh = patch[model].astype(f32)
        for i in range(per_short):
            at = (i // per_chunk) * span + model * BLOCK + (i % per_chunk) * SHORT_LEN
            rows = pl.ds(pl.multiple_of(at, 16), 16)
            new = jnp.concatenate(
                [fresh[i : i + 1], fresh[per_short + i : per_short + i + 1]], axis=1
            )
            gb[rows, :] = jnp.where(top_row, new, gb[rows, :].astype(f32)).astype(bf16)
        return carry

    lax.fori_loop(0, n_model, mend, 0)

    def feed_back(k):
        def one(at):
            rows = pl.ds(pl.multiple_of(k * span + at, 512), 512)
            gp[rows, :] = (nt(gb[rows, :], downw[...]) * slope[rows, :]).astype(bf16)

        tiles(span, 512, one)

        def two(at):
            rows = pl.ds(pl.multiple_of(k * span + at, 512), 512)
            partial[k][pl.ds(at, 512), :] = nt(gp[rows, :], upw[...])

        tiles(span, 512, two)

    def weight_grad(target, base, rows, left, right, left_at=0):
        step = 64

        def one(at):
            part = tn(left[:, pl.ds(pl.multiple_of(left_at + at, 64), step)], right[...])
            target[pl.ds(pl.multiple_of(base + at, 16), step), :] = part.astype(bf16)

        tiles(rows, step, one)

    def begin(first, last, left, right, keep=None):
        base = made = part_at[first]
        for at in range(0, left.shape[1], 256):
            part = tn(left[:, at : at + 256], right[...]).astype(bf16)
            count = 256 if keep is None else keep
            s.grads[pl.ds(made, count), :] = part[:count]
            made += count
            while first < last and part_at[first] + part_rows[first] <= made:
                reduces[first].start()
                first += 1

    begin(0, 4, act, gb)
    scatters = pipeline([], feed_back, middle=((), (0, 1)))
    begin(4, 8, norm, gp)
    before_end = ((2, 1), (3, 2, 0, 1))
    gathers = []
    for k in range(chunks):
        steps(*before_end[k])
        grad = s.second[own_rows(k), :] + scatters[k].end()
        normal = s.normal_one[own_rows(k), :]
        norm_sum[0, 0:1, :] = norm_sum[0, 0:1, :] + jnp.sum(grad * normal, axis=0, keepdims=True)
        norm_sum[0, 1:2, :] = norm_sum[0, 1:2, :] + jnp.sum(grad, axis=0, keepdims=True)
        back = norm_back(grad, normal, s.scale_one[own_rows(k), 0:1], gain_one)
        s.second[own_rows(k), :] = back
        gm[rows_of(m, k), :] = back.astype(bf16)
        gathers.append(Gather(gm, k))
    norm_send()
    steps(3, 4, 2, NORM, 0)

    def attend_back(k):
        def unmix(at):
            rows = pl.ds(pl.multiple_of(k * span + at, 512), 512)
            s.gatt[rows, :] = nt(gm[rows, :], mixw[...]).astype(bf16)

        tiles(span, 512, unmix)

        units = [(model, h) for model in range(n_model) for h in range(heads)]
        grads_out, grads_probs = [], []
        for model, h in units:
            rows = rows_of(model, k)
            grad_out = s.gatt[rows, pl.ds((h // 2) * BLOCK, BLOCK)] * head_masks[h % 2]
            grads_out.append(grad_out)
            grads_probs.append(nt(head_parts(proj, rows, h, 2), grad_out))
        lows, grads_scores = [], []
        for unit, grad_probs in zip(units, grads_probs, strict=True):
            weight = probs[(k, *unit)]
            inner = jnp.sum(weight * grad_probs, axis=0, keepdims=True)
            lows.append(weight.astype(bf16))
            grads_scores.append((weight * (grad_probs - inner)).astype(bf16))
        outs = {}
        for i, (model, h) in enumerate(units):
            rows = rows_of(model, k)
            outs[0, model, h] = tn(grads_scores[i], head_parts(proj, rows, h, 1)) * 0.125
            outs[1, model, h] = nn(grads_scores[i], head_parts(proj, rows, h, 0)) * 0.125
            outs[2, model, h] = nn(lows[i], grads_out[i])
        for model in range(n_model):
            for part in range(3):
                for g in range(pad // BLOCK):
                    second = outs.get((part, model, 2 * g + 1))
                    if second is None:
                        second = jnp.zeros((BLOCK, BLOCK), f32)
                    both = jnp.where(first_half, outs[part, model, 2 * g], second)
                    gproj[rows_of(model, k), pl.ds(part * pad + g * BLOCK, BLOCK)] = both.astype(
                        bf16
                    )

        def one(at):
            rows = pl.ds(pl.multiple_of(k * span + at, 512), 512)
            partial[k][pl.ds(at, 512), :] = nn(gproj[rows, :], wt[...])

        tiles(span, 512, one)

    scatters = pipeline(
        gathers,
        attend_back,
        forward=((), (3, 6, 2, 5, NORM, 0, 1, 7, 4, NORM)),
        middle=((), (2, 5, 1, 7)),
        finish=((5, 1, 4), (3, 6, 0)),
        also=lambda: begin(8, 9, att, gm, cols),
    )
    begin(9, 12, gproj, x, cols)
    steps(4, NORM, 8, 3)
    before_end = ((), (6, NORM, 2))
    swap_sent(s.returned, row_sems)
    for k in range(chunks):
        steps(*before_end[k])
        grad = s.second[own_rows(k), :] + scatters[k].end()
        s.grad_in[own_rows(k), :] = grad.astype(bf16)

    def pack(at):
        rows = pl.ds(at, 256)
        s.outgoing[rows, :] = nn(s.place[rows, :], s.grad_in[...]).astype(bf16)

    tiles(slots, 256, pack)
    swap_start(s.outgoing, s.incoming, out_sems)

    tail = [0, 5, 9, 7, 4, 8, 10, 6, 11, 3, 5, 9, 7]
    rest_of_tail = [4, 8, 10, 6, 5, 11, 9, 7, 6, 8, 10, 11]
    rest_of_tail += [9, 8, 7, 10, 11, 9, 10, 8, 11, 9, 10, 11]
    if resident:
        moments = [
            pltpu.make_async_copy(first_hbm, first_out, s.load_sems.at[0]),
            pltpu.make_async_copy(second_hbm, second_out, s.load_sems.at[1]),
        ]
        for copy in moments:
            copy.start()
    steps(*tail)
    swap_arrived(s.incoming, out_sems)
    if resident:
        for copy in moments:
            copy.wait()
        rows = table_rows // 8
        for at in range(8):
            here = pl.ds(at * rows, rows)
            first_new, second_new, step = table_update(
                s.ids[0:1, :],
                s.incoming[...],
                first_out[here, :],
                second_out[here, :],
                step_out[here, :],
                at * rows,
            )
            first_out[here, :] = first_new
            second_out[here, :] = second_new
            step_out[here, :] = step
            steps(*rest_of_tail[2 * at : 2 * at + 2])
        rest_of_tail = rest_of_tail[16:]
    steps(*rest_of_tail)
    while any(item.todo for item in reduces):
        steps(*(i for i, item in enumerate(reduces) if item.todo))
    while len(norm_done) < len(stages):
        norm_step()
    norm_out[...] = norm_sum[len(stages)]
    if not resident:
        outs = [
            pltpu.make_async_copy(sums, weight_out, s.load_sems.at[0]),
            pltpu.make_async_copy(s.incoming, incoming_out, s.load_sems.at[1]),
            pltpu.make_async_copy(s.ids, ids_hbm, s.load_sems.at[2]),
        ]
        for copy in outs:
            copy.start()
        for copy in outs:
            copy.wait()
    net.drain()
    pool_wait(0)
    swap_sent(s.asked, ask_sems)
    swap_sent(s.incoming, out_sems)


def table_update(ids, incoming, first, second, table, base):
    rows, slots = first.shape[0], incoming.shape[0]
    hot = (iota((rows, slots), 0) + base == ids).astype(f32)
    uses = jnp.sum(hot, axis=1, keepdims=True)
    row_grad = nn(hot.astype(bf16), incoming) * (1.0 / jnp.maximum(uses, 1.0))
    first_new = 0.9 * first + 0.1 * row_grad
    second_new = 0.95 * second + 0.05 * row_grad * row_grad
    scale = jnp.sqrt(second_new * (1.0 / second_fix)) + 1e-08
    return first_new, second_new, first_new * (1.0 / first_fix) / scale + 0.01 * table


def finish_kernel(
    cols,
    block_ref,
    norm_ref,
    loss_ref,
    low,
    step_ref,
    first_ref,
    second_ref,
    step_hbm,
    first_out,
    second_out,
    down_out,
    up_out,
    mix_out,
    heads_out,
    loss_out,
    *rest,
):
    norm_outs, block_out = rest[:4], rest[4]
    wide, state_sems, wide_sems = rest[5:]
    width = low.shape[1]
    states = [
        pltpu.make_async_copy(src, dst, state_sems.at[i])
        for i, (src, dst) in enumerate(
            (
                (step_ref, step_hbm),
                (first_ref, first_out),
                (second_ref, second_out),
                (block_ref, block_out),
            )
        )
    ]
    for copy in states:
        copy.start()
    loss_out[...] = loss_ref[0:1, 0:1]
    for i, out in enumerate(norm_outs):
        out[...] = norm_ref[i, :]
    starts = (0, width, 2 * width, 2 * width + cols, 3 * width)
    wides = []
    for i, out in enumerate((down_out, up_out, mix_out, heads_out)):
        count = starts[i + 1] - starts[i]
        here = pl.ds(starts[i], count)
        step = 96

        def one(at, carry, base=starts[i]):
            rows = pl.ds(pl.multiple_of(base + at * step, 16), step)
            wide[rows, :] = low[rows, :].astype(f32)
            return carry

        lax.fori_loop(0, count // step, one, 0)
        wides.append(pltpu.make_async_copy(wide.at[here], out, wide_sems.at[i]))
        wides[-1].start()
    for copy in states + wides:
        copy.wait()


def table_kernel(
    cols,
    ids_ref,
    norm_ref,
    loss_ref,
    incoming_hbm,
    weights_hbm,
    table_hbm,
    first_hbm,
    second_hbm,
    step_hbm,
    first_out,
    second_out,
    down_out,
    up_out,
    mix_out,
    heads_out,
    loss_out,
    *rest,
):
    norm_outs = rest[:4]
    incoming, low, wide, state, in_sems, out_sems, low_sems, wide_sems = rest[4:]
    slots, width = incoming.shape
    parts = in_sems.shape[1]
    rows = state.shape[1] // parts

    def tile(at):
        return pl.ds(pl.multiple_of(at * rows, 8), rows)

    def load(i, at):
        src = (first_hbm, second_hbm, table_hbm)[i]
        return pltpu.make_async_copy(
            src.at[tile(at)], state.at[i, tile(at)], in_sems.at[i, at]
        )

    def store(i, at):
        dst = (first_out, second_out, step_hbm)[i]
        return pltpu.make_async_copy(
            state.at[i, tile(at)], dst.at[tile(at)], out_sems.at[i, at]
        )

    def each_part(step):
        def one(at, carry):
            for i in range(3):
                step(i, at)
            return carry

        lax.fori_loop(0, parts, one, 0)

    named = pltpu.make_async_copy(incoming_hbm, incoming, low_sems.at[0])
    named.start()
    lows = []
    for i in range(3):
        here = pl.ds(i * width, width)
        lows.append(
            pltpu.make_async_copy(weights_hbm.at[here], low.at[here], low_sems.at[1 + i])
        )
    for copy in lows[:1]:
        copy.start()
    each_part(lambda i, at: load(i, at).start())
    for copy in lows[1:]:
        copy.start()
    loss_out[...] = loss_ref[0:1, 0:1]
    for i, out in enumerate(norm_outs):
        out[...] = norm_ref[i, :]
    named.wait()

    wides = []
    starts = (0, width, 2 * width, 2 * width + cols, 3 * width)
    for i, out in enumerate((down_out, up_out, mix_out, heads_out)):
        here = pl.ds(starts[i], starts[i + 1] - starts[i])
        wides.append(pltpu.make_async_copy(wide.at[here], out, wide_sems.at[i]))

    def widen(i):
        lows[i].wait()
        step = 96

        def one(at, carry):
            here = pl.ds(pl.multiple_of(i * width + at * step, 16), step)
            wide[here, :] = low[here, :].astype(f32)
            return carry

        lax.fori_loop(0, width // step, one, 0)
        for copy in wides[i : i + 1] if i < 2 else wides[2:]:
            copy.start()

    widen(0)

    def update(at, carry):
        for i in range(3):
            load(i, at).wait()
        here = tile(at)
        first_new, second_new, step = table_update(
            ids_ref[0:1, :],
            incoming[...],
            state[0, here, :],
            state[1, here, :],
            state[2, here, :],
            at * rows,
        )
        state[0, here, :] = first_new
        state[1, here, :] = second_new
        state[2, here, :] = step
        for i in range(3):
            store(i, at).start()
        return carry

    lax.fori_loop(0, parts, update, 0)
    widen(1)
    widen(2)
    each_part(lambda i, at: store(i, at).wait())
    for copy in wides:
        copy.wait()


def body(
    token_owner,
    token_row,
    long_len,
    short_len,
    pairing,
    embed_table,
    first_moment,
    second_moment,
    heads_weight,
    mix_weight,
    up_weight,
    down_weight,
    first_gain,
    first_shift,
    second_gain,
    second_shift,
    upper_grad,
):
    tok, width = upper_grad.shape
    n_model, n_data = lax.axis_size("mp"), lax.axis_size("dp")
    devices = n_model * n_data
    group = tok * n_model
    cols = heads_weight.shape[2]
    pad = -(-cols // BLOCK) * BLOCK
    ff = up_weight.shape[1]
    slots = devices * SLOTS
    chunks = tok // BLOCK
    span = BLOCK * n_model
    per_short = tok // SHORT_LEN
    firsts = devices * per_short
    table_rows = embed_table.shape[0]
    bits = n_data.bit_length() - 1
    vmem = pltpu.VMEM
    dma = pltpu.SemaphoreType.DMA
    shapes = dict(
        table=vmem((table_rows, width), bf16),
        wt=vmem((3 * pad, width), bf16),
        mixw=vmem((pad, width), bf16),
        upw=vmem((width, ff), bf16),
        downw=vmem((ff, width), bf16),
        upper=vmem((tok, width), bf16),
        ask=vmem((slots, 128), bf16),
        asked=vmem((slots, 128), bf16),
        place=vmem((slots, tok), bf16),
        pick=vmem((tok, slots), bf16),
        found=vmem((slots, width), bf16),
        returned=vmem((slots, width), bf16),
        x=vmem((group, width), bf16),
        proj=vmem((group, 3 * pad), bf16),
        att=vmem((group, pad), bf16),
        gatt=vmem((group, pad), bf16),
        probs=vmem((chunks, n_model, cols // HEAD, BLOCK, BLOCK), f32),
        near_send=vmem((chunks, 2, BLOCK, width), bf16),
        near_land=vmem((chunks, 2, BLOCK, width), bf16),
        far_send=vmem((chunks, BLOCK, width), bf16),
        far_land=vmem((chunks, BLOCK, width), bf16),
        scale_one=vmem((tok, 128), f32),
        norm=vmem((group, width), bf16),
        act=vmem((group, ff), bf16),
        scale_two=vmem((tok, 128), f32),
        patch=vmem((n_model, 2 * per_short, width // 2), bf16),
        pool=vmem((n_data, n_model, 2 * per_short, width // 2), bf16),
        left=vmem((firsts, width // 2), bf16),
        right=vmem((firsts, width // 2), bf16),
        gram=vmem((firsts, firsts), f32),
        known=vmem((8, firsts), f32),
        known_col=vmem((firsts, 128), f32),
        gb=vmem((group, width), bf16),
        gm=vmem((group, width), bf16),
        grad_in=vmem((tok, width), bf16),
        norm_sum=vmem((3 + bits, 8, width), f32),
        norm_land=vmem((2 + bits, 8, width), f32),
        grads=vmem((3 * width, width), bf16),
        sum_land=vmem((12, 2 * cols + 64, width // 2), bf16),
        send_sems=dma((32,)),
        recv_sems=dma((20 + 25 * bits,)),
        owner=vmem((1, group), i32),
        rowid=vmem((1, group), i32),
        long=pltpu.SMEM(long_len.shape, i32),
        short=pltpu.SMEM(short_len.shape, i32),
        pairing=vmem((1, pairing.shape[0]), i32),
        gain_one=vmem((width,), f32),
        shift_one=vmem((width,), f32),
        gain_two=vmem((width,), f32),
        shift_two=vmem((width,), f32),
        small_sems=dma((9,)),
        load_sems=dma((8,)),
        table_sems=dma((max(4, table_rows // span),)),
        ids=vmem((8, slots), i32),
        ask_sems=dma((2,)),
        row_sems=dma((2,)),
        out_sems=dma((2,)),
        pool_sems=dma((2,)),
    )
    resident = devices <= 32
    if not resident:
        shapes.update(
            wide_a=vmem((2 * group, width), f32),
            wide_b=vmem((6 * tok, width), f32),
            sums=vmem((3 * width, width), bf16),
        )
    dims = SimpleNamespace(
        resident=resident,
        n_data=n_data,
        n_model=n_model,
        names=tuple(shapes),
        tok=tok,
        width=width,
        cols=cols,
        pad=pad,
        ff=ff,
        longs=long_len.shape[1],
        shorts=short_len.shape[1],
    )
    in_vmem = pl.BlockSpec(memory_space=pltpu.VMEM)
    in_hbm = pl.BlockSpec(memory_space=pl.ANY)
    heads_rows = jnp.transpose(heads_weight, (1, 2, 0)).reshape(3 * cols, width)
    whole = jax.ShapeDtypeStruct((table_rows, width), f32)
    out_shape = (
        jax.ShapeDtypeStruct((tok, width), bf16),
        jax.ShapeDtypeStruct((8, width), f32),
        jax.ShapeDtypeStruct((8, 128), f32),
    )
    if resident:
        out_shape = (vmem((tok, width), bf16), vmem((8, width), f32), vmem((8, 128), f32))
        out_shape += (vmem((3 * width, width), bf16),) + (vmem((table_rows, width), f32),) * 3
        out_specs = (in_vmem,) * 7
    else:
        out_shape += (
            jax.ShapeDtypeStruct((3 * width, width), bf16),
            jax.ShapeDtypeStruct((slots, width), bf16),
            jax.ShapeDtypeStruct((8, slots), i32),
        )
        out_specs = (in_vmem,) * 3 + (in_hbm,) * 3
    block_out, norms, loss, *more = pl.pallas_call(
        functools.partial(layer_kernel, dims),
        out_shape=out_shape,
        in_specs=[in_hbm] * 17,
        out_specs=out_specs,
        scratch_shapes=list(shapes.values()),
        compiler_params=pltpu.CompilerParams(
            collective_id=0,
            has_side_effects=True,
            vmem_limit_bytes=(40 if resident else 63) * 2**20,
        ),
    )(
        token_owner.reshape(1, group),
        token_row.reshape(1, group),
        long_len,
        short_len,
        pairing.reshape(1, -1),
        first_gain,
        first_shift,
        second_gain,
        second_shift,
        embed_table,
        heads_rows,
        mix_weight,
        up_weight,
        down_weight,
        upper_grad,
        first_moment,
        second_moment,
    )
    out_shape = (
        (whole, whole, whole)
        + tuple(jax.ShapeDtypeStruct((rows, width), f32) for rows in (ff, width, cols, 3 * cols))
        + (jax.ShapeDtypeStruct((1, 1), f32),)
        + (jax.ShapeDtypeStruct((width,), f32),) * 4
    )
    out_specs = (in_hbm,) * 7 + (in_vmem,) * 5
    if resident:
        finished = pl.pallas_call(
            functools.partial(finish_kernel, cols),
            out_shape=out_shape + (jax.ShapeDtypeStruct((tok, width), bf16),),
            in_specs=[in_vmem] * 7,
            out_specs=out_specs + (in_hbm,),
            scratch_shapes=[vmem((3 * width, width), f32), dma((4,)), dma((4,))],
            compiler_params=pltpu.CompilerParams(vmem_limit_bytes=20 * 2**20),
        )(block_out, norms, loss, *more)
        *finished, block_out = finished
    else:
        weights, incoming, ids = more
        parts = 8
        finished = pl.pallas_call(
            functools.partial(table_kernel, cols),
            out_shape=out_shape,
            in_specs=[in_vmem] * 3 + [in_hbm] * 5,
            out_specs=out_specs,
            scratch_shapes=[
                vmem((slots, width), bf16),
                vmem((3 * width, width), bf16),
                vmem((3 * width, width), f32),
                vmem((3, table_rows, width), f32),
                dma((3, parts)),
                dma((3, parts)),
                dma((4,)),
                dma((4,)),
            ],
            compiler_params=pltpu.CompilerParams(vmem_limit_bytes=63 * 2**20),
        )(ids, norms, loss, incoming, weights, embed_table, first_moment, second_moment)
    table_step, first_new, second_new, down_grad, up_grad, mix_grad, heads_grad, loss = finished[:8]
    norm_grads = finished[8:]
    return (
        loss.reshape(()),
        block_out,
        jnp.transpose(heads_grad.reshape(3, cols, width), (2, 0, 1)),
        mix_grad,
        up_grad,
        down_grad,
        *norm_grads,
        table_step,
        first_new,
        second_new,
    )


def solution(mesh):
    rows = P(("dp", "mp"), None)
    in_specs = (
        P("dp", None),
        P("dp"),
        P("dp", None),
        P("dp", None),
        P(),
        rows,
        rows,
        rows,
        P(None, None, "mp"),
        P("mp", None),
        P(None, "mp"),
        P("mp", None),
        P(),
        P(),
        P(),
        P(),
        rows,
    )
    out_specs = (
        P(),
        rows,
        P(None, None, "mp"),
        P("mp", None),
        P(None, "mp"),
        P("mp", None),
        P(),
        P(),
        P(),
        P(),
        rows,
        rows,
        rows,
    )
    return jax.shard_map(body, mesh=mesh, in_specs=in_specs, out_specs=out_specs, check_vma=False)
```

```python
import functools
from types import SimpleNamespace

import jax
import jax.numpy as jnp
from jax import lax
from jax.experimental import pallas as pl
from jax.experimental.pallas import tpu as pltpu
from jax.sharding import PartitionSpec as P

HEAD = 64
LONG_LEN = 128
SHORT_LEN = 32
BLOCK = 128
SLOTS = 16
NORM = -1
MESH = pl.DeviceIdType.MESH
bf16 = jnp.bfloat16
f32 = jnp.float32
i32 = jnp.int32

first_fix = 1.0 - 0.9**10
second_fix = 1.0 - 0.95**10


def nn(left, right):
    return lax.dot_general(left, right, (((1,), (0,)), ((), ())), preferred_element_type=f32)


def nt(left, right):
    return lax.dot_general(left, right, (((1,), (1,)), ((), ())), preferred_element_type=f32)


def tn(left, right):
    return lax.dot_general(left, right, (((0,), (0,)), ((), ())), preferred_element_type=f32)


def iota(shape, axis):
    return lax.broadcasted_iota(i32, shape, axis)


def column_of(row):
    count = row.shape[1]
    eye = iota((count, count), 0) == iota((count, count), 1)
    return jnp.sum(jnp.where(eye, row, 0.0), axis=1, keepdims=True)


def mean_of(values):
    return jnp.mean(values, axis=-1, keepdims=True)


def norm_forward(hidden):
    centered = hidden - mean_of(hidden)
    scale = lax.rsqrt(mean_of(centered * centered) + 1e-12)
    return centered * scale, scale


def norm_back(grad, normal, scale, gain):
    scaled = grad * gain
    return scale * (scaled - mean_of(scaled) - normal * mean_of(scaled * normal))


class Net:
    def __init__(self, send_sems, recv_sems):
        self.send_sems, self.recv_sems = send_sems, recv_sems
        self.open = [None] * send_sems.shape[0]
        self.count = 0
        self.names = {}

    def send(self, src, dst, device, name=None):
        slot = self.count % len(self.open)
        if self.open[slot] is not None:
            self.open[slot].wait_send()
        at = self.names.setdefault(self.count if name is None else name, len(self.names))
        self.count += 1
        copy = pltpu.make_async_remote_copy(
            src_ref=src,
            dst_ref=dst,
            send_sem=self.send_sems.at[slot],
            recv_sem=self.recv_sems.at[at],
            device_id=device,
            device_id_type=MESH,
        )
        copy.start()
        self.open[slot] = copy
        return copy

    def sent(self, copy):
        for slot, item in enumerate(self.open):
            if item is copy:
                copy.wait_send()
                self.open[slot] = None

    def drain(self):
        for copy in self.open:
            if copy is not None:
                copy.wait_send()
        self.open = [None] * len(self.open)


class Reduce:
    def __init__(self, net, part, whole, land, place, bits):
        self.net, self.part, self.whole, self.land = net, part, whole, land
        self.data_pos, self.model_pos = place
        self.bits = bits
        rows, width = part.shape
        self.half = width // 2
        self.row, self.len = 0, rows
        self.offset = 0
        self.stage = 0
        self.halved = []
        grows = sum(1 for stage in range(len(bits)) if self.halves(stage))
        self.todo = [self.add] * len(bits) + [self.grow] * grows

    def step(self):
        if self.todo:
            self.todo.pop(0)()

    def halves(self, stage):
        return stage == 0 or (self.part.shape[0] >> (stage - 1)) % 32 == 0

    def partner(self, bit):
        mine = lax.rem(lax.div(self.data_pos, 1 << bit), 2)
        return mine, (self.data_pos + (1 - 2 * mine) * (1 << bit), self.model_pos)

    def start(self):
        mine, device = self.partner(self.bits[self.stage])
        halved = self.halves(self.stage)
        count = self.len
        if self.stage == 0:
            away = pl.multiple_of((1 - mine) * self.half, 128)
            self.col = pl.multiple_of(mine * self.half, 128)
            src = self.part.at[:, pl.ds(away, self.half)]
        else:
            away = self.row
            if halved:
                count = self.len // 2
                away = pl.multiple_of(self.row + (1 - mine) * count, 16)
                self.row = pl.multiple_of(self.row + mine * count, 16)
                self.len = count
            src = self.part.at[pl.ds(away, count), pl.ds(self.col, self.half)]
        self.halved.append(halved)
        self.now = self.land.at[pl.ds(self.offset, count)]
        self.offset += count
        self.copy = self.net.send(src, self.now, device)

    def add(self):
        self.copy.wait_recv()
        last = self.stage == len(self.bits) - 1
        if not self.halved[-1]:
            self.net.sent(self.copy)
        target = self.whole if last else self.part
        cols = pl.ds(self.col, self.half)
        step = 48 if self.len % 48 == 0 else min(self.len, 64)
        now, row, part = self.now, self.row, self.part

        def tile(at, carry):
            here = pl.multiple_of(at * step, 16)
            there = pl.ds(pl.multiple_of(row + here, 16), step)
            total = part[there, cols].astype(f32) + now[pl.ds(here, step), :].astype(f32)
            target[there, cols] = total.astype(bf16)
            return carry

        lax.fori_loop(0, self.len // step, tile, 0)
        if last:
            self.spread()
        else:
            self.stage += 1
            self.start()

    def spread(self):
        while self.stage and not self.halved[self.stage]:
            self.stage -= 1
        _, device = self.partner(self.bits[self.stage])
        rows = pl.ds(self.row, self.len) if self.stage else slice(None)
        here = self.whole.at[rows, pl.ds(self.col, self.half)]
        self.copy = self.net.send(here, here, device)

    def grow(self):
        self.copy.wait_recv()
        if self.stage == 0:
            return
        mine, _ = self.partner(self.bits[self.stage])
        self.row = pl.multiple_of(self.row - mine * self.len, 16)
        self.len *= 2
        self.stage -= 1
        self.spread()


def layer_kernel(
    dims,
    owner_hbm,
    rowid_hbm,
    long_hbm,
    short_hbm,
    pairing_hbm,
    gain_one_hbm,
    shift_one_hbm,
    gain_two_hbm,
    shift_two_hbm,
    table_hbm,
    heads_hbm,
    mix_hbm,
    up_hbm,
    down_hbm,
    upper_hbm,
    first_hbm,
    second_hbm,
    block_out,
    norm_out,
    loss_out,
    *rest,
):
    resident = dims.resident
    if resident:
        sums, step_out, first_out, second_out, *scratch = rest
    else:
        weight_out, incoming_out, ids_hbm, *scratch = rest
    n_data, n_model = dims.n_data, dims.n_model
    s = SimpleNamespace(**dict(zip(dims.names, scratch, strict=True)))
    tok, width, cols, pad, ff = dims.tok, dims.width, dims.cols, dims.pad, dims.ff
    devices = n_data * n_model
    group = tok * n_model
    chunks = tok // BLOCK
    span = BLOCK * n_model
    slots = devices * SLOTS
    table_rows = table_hbm.shape[0]

    if resident:
        wide_a, wide_b = first_out, second_out
    else:
        wide_a, wide_b, sums = s.wide_a, s.wide_b, s.sums
    slope = wide_a.at[pl.ds(0, group)]
    partial = [wide_a.at[pl.ds(group + k * span, span)] for k in range(chunks)]
    s.normal_one, s.normed, s.normal_two, s.rows, s.grad_rows, s.second = [
        wide_b.at[pl.ds(i * tok, tok)] for i in range(6)
    ]
    s.gproj = s.table.at[pl.ds(0, group)]
    s.gp = s.table.at[pl.ds(group, group)]
    s.outgoing = s.found
    s.incoming = s.returned
    d = lax.axis_index("dp")
    m = lax.axis_index("mp")
    me = d * n_model + m
    core = lax.rem(m, 2)
    side = lax.div(m, 2)
    m1 = m + 1 - 2 * core
    m2 = m + 2 - 4 * side
    m3 = m1 + m2 - m
    by_core = (d, m1)
    by_side = (d, m2)
    net = Net(s.send_sems, s.recv_sems)

    def at_device(place):
        return (lax.div(place, n_model), lax.rem(place, n_model))

    def other(j):
        return lax.rem(me + j, devices)

    owner_ref, rowid_ref, long_ref, short_ref = s.owner, s.rowid, s.long, s.short
    pairing_ref = s.pairing
    small = [
        pltpu.make_async_copy(src, dst, s.small_sems.at[i])
        for i, (src, dst) in enumerate(
            (
                (owner_hbm, s.owner),
                (rowid_hbm, s.rowid),
                (long_hbm, s.long),
                (short_hbm, s.short),
                (pairing_hbm, s.pairing),
                (gain_one_hbm, s.gain_one),
                (shift_one_hbm, s.shift_one),
                (gain_two_hbm, s.gain_two),
                (shift_two_hbm, s.shift_two),
            )
        )
    ]
    for copy in small:
        copy.start()

    barrier = pltpu.get_barrier_semaphore()

    def greet(j, carry):
        pl.semaphore_signal(barrier, inc=1, device_id=at_device(other(j)), device_id_type=MESH)
        return carry

    lax.fori_loop(1, devices, greet, 0)

    stage_rows = table_rows // 4 if resident else span
    table_parts = table_rows // stage_rows

    def table_part(at):
        if resident:
            return step_out.at[pl.ds(at * stage_rows, stage_rows)]
        return partial[at % 2]

    def table_copy(at):
        return pltpu.make_async_copy(
            table_hbm.at[pl.ds(at * stage_rows, stage_rows)],
            table_part(at),
            s.table_sems.at[at],
        )

    ahead = table_parts if resident else 2
    for at in range(ahead):
        table_copy(at).start()
    loads = []

    def load(src, dst):
        copy = pltpu.make_async_copy(src, dst, s.load_sems.at[len(loads)])
        copy.start()
        loads.append(copy)

    wt, mixw, upw, downw = s.wt, s.mixw, s.upw, s.downw
    for part in range(3):
        load(heads_hbm.at[pl.ds(part * cols, cols)], wt.at[pl.ds(part * pad, cols)])
        wt[pl.ds(part * pad + cols, pad - cols), :] = jnp.zeros((pad - cols, width), bf16)
    load(mix_hbm, mixw.at[pl.ds(0, cols)])
    mixw[pl.ds(cols, pad - cols), :] = jnp.zeros((pad - cols, width), bf16)
    load(up_hbm, upw)
    load(down_hbm, downw)
    load(upper_hbm, s.upper)

    for copy in small:
        copy.wait()
    own_at = pl.multiple_of(m * tok, 128)
    owner_row = owner_ref[:, pl.ds(own_at, tok)]
    rowid_row = rowid_ref[:, pl.ds(own_at, tok)]
    owned = iota((devices, tok), 0) == owner_row
    before = (iota((tok, tok), 0) < iota((tok, tok), 1)).astype(f32).astype(bf16)
    counted = nn(owned.astype(f32).astype(bf16), before)
    rank_row = jnp.sum(jnp.where(owned, counted, 0.0), axis=0, keepdims=True)
    slot_row = owner_row.astype(f32) * SLOTS + rank_row
    slot_row_int = slot_row.astype(i32)
    wanted_row = (rowid_row + 1).astype(f32)
    step = min(slots, 256)

    def place_slots(at, carry):
        here = pl.ds(pl.multiple_of(at * step, step), step)
        placed = iota((step, tok), 0) + at * step == slot_row_int
        wanted = jnp.sum(jnp.where(placed, wanted_row, 0.0), axis=1, keepdims=True)
        high = jnp.floor(wanted * (1.0 / 64.0))
        low = wanted - 64.0 * high
        s.ask[here, :] = jnp.where(iota((step, 128), 1) < 64, high, low).astype(bf16)
        s.place[here, :] = placed.astype(f32).astype(bf16)
        return carry

    lax.fori_loop(0, slots // step, place_slots, 0)
    slot_col = column_of(slot_row).astype(i32)
    s.pick[...] = (iota((tok, slots), 1) == slot_col).astype(f32).astype(bf16)

    pl.semaphore_wait(barrier, devices - 1)

    def slot_rows(place):
        return pl.ds(pl.multiple_of(place * SLOTS, SLOTS), SLOTS)

    def swap_copy(src, dst, sems, to):
        return pltpu.make_async_remote_copy(
            src_ref=src.at[slot_rows(to)],
            dst_ref=dst.at[slot_rows(me)],
            send_sem=sems.at[0],
            recv_sem=sems.at[1],
            device_id=at_device(to),
            device_id_type=MESH,
        )

    def swap_some(src, dst, sems, first, last):
        def one(j, carry):
            swap_copy(src, dst, sems, other(j)).start()
            return carry

        lax.fori_loop(first, last, one, 0)

    def swap_start(src, dst, sems):
        swap_some(src, dst, sems, 1, devices)
        dst[slot_rows(me), :] = src[slot_rows(me), :]

    def swap_wait(dst, sem):
        blocks = dst.at[pl.ds(0, slots - SLOTS)]
        pltpu.make_async_copy(blocks, blocks, sem).wait()

    def swap_arrived(dst, sems):
        swap_wait(dst, sems.at[1])

    def swap_sent(dst, sems):
        swap_wait(dst, sems.at[0])

    ask_sems, row_sems, out_sems = s.ask_sems, s.row_sems, s.out_sems
    swap_start(s.ask, s.asked, ask_sems)
    for at in range(table_parts):
        table_copy(at).wait()
        s.table[pl.ds(at * stage_rows, stage_rows), :] = table_part(at)[...].astype(bf16)
        if at + ahead < table_parts:
            table_copy(at + ahead).start()
    swap_arrived(s.asked, ask_sems)

    per_block = BLOCK // SLOTS

    def look(at, carry):
        block = lax.rem(lax.div(me, per_block) + at, slots // BLOCK)
        rows = pl.ds(pl.multiple_of(block * BLOCK, BLOCK), BLOCK)
        asked = s.asked[rows, :].astype(f32)
        ident = asked[:, 0:1] * 64.0 + asked[:, 64:65] - 1.0
        eye = iota((BLOCK, BLOCK), 0) == iota((BLOCK, BLOCK), 1)
        ident_row = jnp.sum(jnp.where(eye, ident, 0.0), axis=0, keepdims=True)
        s.ids[:, rows] = jnp.broadcast_to(ident_row.astype(i32), (8, BLOCK))
        hot = (iota((BLOCK, table_rows), 1) == ident.astype(i32)).astype(f32).astype(bf16)
        s.found[rows, :] = nn(hot, s.table[...]).astype(bf16)

        def one(i, inner):
            to = block * per_block + lax.rem(lax.rem(me, per_block) + i, per_block)

            @pl.when(to != me)
            def _():
                swap_copy(s.found, s.returned, row_sems, to).start()

            return inner

        lax.fori_loop(0, per_block, one, 0)
        return carry

    lax.fori_loop(0, slots // BLOCK, look, 0)
    s.returned[slot_rows(me), :] = s.found[slot_rows(me), :]
    for copy in loads:
        copy.wait()
    swap_arrived(s.returned, row_sems)

    def rows_of(model, k):
        return pl.ds(pl.multiple_of(k * span + model * BLOCK, BLOCK), BLOCK)

    def own_rows(k):
        return pl.ds(k * BLOCK, BLOCK)

    class Gather:
        def __init__(self, buffer, k):
            self.buffer, self.k = buffer, k
            mine = buffer.at[rows_of(m, k)]
            self.far = net.send(mine, mine, by_side, (k, 0))
            self.near = net.send(mine, mine, by_core, (k, 1))

        def forward(self):
            self.far.wait_recv()
            there = self.buffer.at[rows_of(m2, self.k)]
            self.passed = net.send(there, there, by_core, (self.k, 2))

        def finish(self):
            self.near.wait_recv()
            self.passed.wait_recv()

    class Scatter:
        last = {}

        def __init__(self, k):
            self.k = k
            for copy in Scatter.last.get(k, []):
                net.sent(copy)
            part = partial[k]
            self.near = []
            for r, model in ((0, m3), (1, m1)):
                here = pl.ds(pl.multiple_of(model * BLOCK, BLOCK), BLOCK)
                s.near_send[k, r] = part[here, :].astype(bf16)
                self.near.append(
                    net.send(s.near_send.at[k, r], s.near_land.at[k, r], by_core, (k, 3 + r))
                )

        def middle(self):
            k = self.k
            self.near[0].wait_recv()
            here = pl.ds(pl.multiple_of(m2 * BLOCK, BLOCK), BLOCK)
            total = partial[k][here, :] + s.near_land[k, 0].astype(f32)
            s.far_send[k] = total.astype(bf16)
            self.far = net.send(s.far_send.at[k], s.far_land.at[k], by_side, (k, 5))
            Scatter.last[k] = self.near + [self.far]

        def end(self):
            k = self.k
            self.near[1].wait_recv()
            here = pl.ds(pl.multiple_of(m * BLOCK, BLOCK), BLOCK)
            total = partial[k][here, :] + s.near_land[k, 1].astype(f32)
            self.far.wait_recv()
            return total + s.far_land[k].astype(f32)

    def tiles(total, step, fn):
        def one(at, carry):
            fn(pl.multiple_of(at * step, step))
            return carry

        lax.fori_loop(0, total // step, one, 0)

    x, proj, att, probs = s.x, s.proj, s.att, s.probs
    gathers = []
    for k in range(chunks):
        own = nn(s.pick[own_rows(k), :], s.returned[...])
        x[rows_of(m, k), :] = own.astype(bf16)
        gathers.append(Gather(x, k))

    lane = iota((BLOCK, BLOCK), 1)
    sub = iota((BLOCK, BLOCK), 0)
    first_half = lane < HEAD
    head_masks = [
        (lane < HEAD).astype(f32).astype(bf16),
        (lane >= HEAD).astype(f32).astype(bf16),
    ]
    heads = cols // HEAD
    long_blocks = n_model // 2
    per_long = tok // LONG_LEN
    per_short = tok // SHORT_LEN
    short_in_block = BLOCK // SHORT_LEN

    def key_mask(model, k, is_long):
        if is_long:
            return sub < long_ref[0, model * per_long + k]
        keep = None
        for j in range(short_in_block):
            size = short_ref[0, (model - long_blocks) * per_short + k * short_in_block + j]
            start = j * SHORT_LEN
            ok = (sub >= start) & (sub < start + size) & (lane >= start) & (lane < start + SHORT_LEN)
            keep = ok if keep is None else keep | ok
        return keep

    def head_parts(source, rows, h, part):
        g = h // 2
        return source[rows, pl.ds(part * pad + g * BLOCK, BLOCK)]

    def attend(k):
        def project(at):
            rows = pl.ds(pl.multiple_of(k * span + at, 512), 512)
            proj[rows, :] = nt(x[rows, :], wt[...]).astype(bf16)

        tiles(span, 512, project)

        units = [(model, h) for model in range(n_model) for h in range(heads)]
        keeps = [key_mask(model, k, model < long_blocks) for model in range(n_model)]
        scores = []
        for model, h in units:
            rows = rows_of(model, k)
            query = head_parts(proj, rows, h, 0) * head_masks[h % 2]
            scores.append(nt(head_parts(proj, rows, h, 1), query))
        weights = []
        for (model, h), score in zip(units, scores, strict=True):
            score = jnp.where(keeps[model], score * 0.125, -1e30)
            part = jnp.exp(score - jnp.max(score, axis=0, keepdims=True))
            weights.append(part * (1.0 / jnp.sum(part, axis=0, keepdims=True)))
        outs = {}
        for unit, weight in zip(units, weights, strict=True):
            value = head_parts(proj, rows_of(unit[0], k), unit[1], 2)
            outs[unit] = tn(weight.astype(bf16), value)
        for unit, weight in zip(units, weights, strict=True):
            probs[(k, *unit)] = weight
        for model in range(n_model):
            for g in range(pad // BLOCK):
                second = outs.get((model, 2 * g + 1))
                if second is None:
                    second = jnp.zeros((BLOCK, BLOCK), f32)
                both = jnp.where(first_half, outs[model, 2 * g], second)
                att[rows_of(model, k), pl.ds(g * BLOCK, BLOCK)] = both.astype(bf16)

        def mix(at):
            rows = pl.ds(pl.multiple_of(k * span + at, 512), 512)
            partial[k][pl.ds(at, 512), :] = nn(att[rows, :], mixw[...])

        tiles(span, 512, mix)

    nothing = ((),) * chunks

    def pipeline(gathers, work, forward=nothing, middle=nothing, finish=nothing, also=None):
        scatters = []
        for k in range(chunks):
            if gathers:
                steps(*forward[k])
                gathers[k].forward()
            if k:
                steps(*middle[k - 1])
                scatters[k - 1].middle()
            if gathers:
                steps(*finish[k])
                gathers[k].finish()
            if also is not None and k == chunks - 1:
                also()
            work(k)
            scatters.append(Scatter(k))
        steps(*middle[-1])
        scatters[-1].middle()
        return scatters

    bits = tuple(range(n_data.bit_length() - 1))
    part_rows = [ff // 4] * 4 + [width // 4] * 4 + [cols] * 4
    part_at = [sum(part_rows[:i]) for i in range(len(part_rows))]
    reduces = [
        Reduce(
            net,
            s.grads.at[pl.ds(at, rows)],
            sums.at[pl.ds(at, rows)],
            s.sum_land.at[i],
            (d, m),
            bits if i else bits[1::-1] + bits[2:],
        )
        for i, (at, rows) in enumerate(zip(part_at, part_rows, strict=True))
    ]
    norm_sum = s.norm_sum
    norm_copies, norm_done = [], []
    stages = [by_core, by_side] + [reduces[0].partner(bit)[1] for bit in bits]

    def norm_send():
        at = len(norm_copies)
        if at < len(stages):
            norm_copies.append(net.send(norm_sum.at[at], s.norm_land.at[at], stages[at]))

    def norm_step():
        at = len(norm_copies) - 1
        norm_copies[at].wait_recv()
        norm_sum[at + 1] = norm_sum[at] + s.norm_land[at]
        norm_done.append(at)
        norm_send()

    def steps(*order):
        for at in order:
            if at == NORM:
                norm_step()
            else:
                reduces[at].step()

    scatters = pipeline(gathers, attend)

    gain_one, shift_one, gain_two, shift_two = [
        ref[...].reshape(1, width)
        for ref in (s.gain_one, s.shift_one, s.gain_two, s.shift_two)
    ]
    norm, act = s.norm, s.act
    gathers = []
    for k in range(chunks):
        hidden = x[rows_of(m, k), :].astype(f32) + scatters[k].end()
        normal, scale = norm_forward(hidden)
        s.normal_one[own_rows(k), :] = normal
        s.scale_one[own_rows(k), :] = jnp.broadcast_to(scale, (BLOCK, 128))
        normed = normal * gain_one + shift_one
        s.normed[own_rows(k), :] = normed
        norm[rows_of(m, k), :] = normed.astype(bf16)
        gathers.append(Gather(norm, k))

    def feed(k):
        def one(at):
            rows = pl.ds(pl.multiple_of(k * span + at, 512), 512)
            pre = nn(norm[rows, :], upw[...])
            cumulative = 0.5 * (1.0 + lax.erf(pre * 0.7071067811865476))
            act[rows, :] = (pre * cumulative).astype(bf16)
            slope[rows, :] = cumulative + pre * (0.3989422804014327 * jnp.exp(-0.5 * pre * pre))

        tiles(span, 512, one)

        def two(at):
            rows = pl.ds(pl.multiple_of(k * span + at, 512), 512)
            partial[k][pl.ds(at, 512), :] = nn(act[rows, :], downw[...])

        tiles(span, 512, two)

    scatters = pipeline(gathers, feed)

    gb, gp, gm, gproj = s.gb, s.gp, s.gm, s.gproj

    def second_back(k):
        rows = own_rows(k)
        return norm_back(
            s.grad_rows[rows, :], s.normal_two[rows, :], s.scale_two[rows, 0:1], gain_two
        )

    def early_gather(k):
        gb[rows_of(m, k), :] = second_back(k).astype(bf16)
        gathers.append(Gather(gb, k))

    s.grad_rows[...] = s.upper[...].astype(f32)
    gathers = []
    for k in range(chunks):
        hidden = s.normed[own_rows(k), :] + scatters[k].end()
        normal, scale = norm_forward(hidden)
        s.normal_two[own_rows(k), :] = normal
        s.scale_two[own_rows(k), :] = jnp.broadcast_to(scale, (BLOCK, 128))
        rows_now = normal * gain_two + shift_two
        s.rows[own_rows(k), :] = rows_now
        block_out[own_rows(k), :] = rows_now.astype(bf16)
        if k < chunks - 1:
            early_gather(k)

    pool = s.pool
    half = width // 2
    firsts = jnp.concatenate(
        [s.rows[pl.ds(i * SHORT_LEN, 1), :] for i in range(per_short)], axis=0
    )
    pool[d, m] = jnp.concatenate([firsts[:, :half], firsts[:, half:]], axis=0).astype(bf16)

    def pool_copy(j, model):
        return pltpu.make_async_remote_copy(
            src_ref=pool.at[d, m],
            dst_ref=pool.at[d, m],
            send_sem=s.pool_sems.at[0],
            recv_sem=s.pool_sems.at[1],
            device_id=(lax.rem(d + j, n_data), model),
            device_id_type=MESH,
        )

    def pool_start(j, carry):
        pool_copy(j, m).start()
        pool_copy(j, m2).start()
        return carry

    def pool_wait(at):
        blocks = pool.at[pl.ds(0, (2 * n_data - 1) // 3), pl.ds(0, 3)]
        pltpu.make_async_copy(blocks, blocks, s.pool_sems.at[at]).wait()

    lax.fori_loop(1, n_data, pool_start, 0)
    pool_copy(0, m2).start()
    early_gather(chunks - 1)
    pool_wait(1)
    near = net.send(pool.at[:, m], pool.at[:, m], by_core)
    passed = net.send(pool.at[:, m2], pool.at[:, m2], by_core)
    near.wait_recv()
    passed.wait_recv()

    count = devices * per_short
    sentences = dims.longs + dims.shorts
    pairs2 = pairing_ref.shape[1]

    def sentence_of(index):
        place = lax.div(index, per_short)
        slot = lax.rem(index, per_short)
        model = lax.rem(place, n_model)
        data = lax.div(place, n_model)
        ratio = LONG_LEN // SHORT_LEN
        is_long = model < long_blocks
        valid = jnp.logical_or(jnp.logical_not(is_long), lax.rem(slot, ratio) == 0)
        number = jnp.where(
            is_long,
            model * per_long + lax.div(slot, ratio),
            dims.longs + (model - long_blocks) * per_short + slot,
        )
        return jnp.where(valid, data * sentences + number, -1)

    group_rows_first = n_model * per_short

    def unfold(at, carry):
        part = pool[at].astype(f32)
        here = pl.ds(pl.multiple_of(at * group_rows_first, 16), group_rows_first)
        s.left[here, :] = part[:, :per_short, :].reshape(group_rows_first, half).astype(bf16)
        s.right[here, :] = part[:, per_short:, :].reshape(group_rows_first, half).astype(bf16)
        return carry

    lax.fori_loop(0, n_data, unfold, 0)
    gram, known = s.gram, s.known
    pair_col = column_of(pairing_ref[...].astype(f32)).astype(i32)
    step = 256 if count <= 256 else 128

    def measure(number, carry):
        at = number * step
        block = pl.ds(pl.multiple_of(at, 128), step)
        gram[:, block] = nt(s.left[...], s.left[block, :]) + nt(
            s.right[...], s.right[block, :]
        )
        sent = sentence_of(iota((1, step), 1) + at)
        place = jnp.sum(
            jnp.where(pair_col == sent, iota((pairs2, step), 0), 0).astype(f32),
            axis=0,
            keepdims=True,
        )
        place = jnp.where(sent >= 0, place, -2.0)
        pair = jnp.floor(place * 0.5)
        eye = iota((step, step), 0) == iota((step, step), 1)
        square = jnp.sum(jnp.where(eye, gram[block, block], 0.0), axis=0, keepdims=True)
        known[0:1, block] = lax.rsqrt(square + 1e-06)
        known[1:2, block] = pair
        known[2:3, block] = jnp.where(sent >= 0, place - 2.0 * pair, 5.0)
        for i in range(3):
            s.known_col[block, i : i + 1] = column_of(known[i : i + 1, block])
        return carry

    lax.fori_loop(0, count // step, measure, 0)

    def logits_of(part, block, inv_col, pair_col, side_col):
        inv_row, pair_row, side_row = known[0:1, block], known[1:2, block], known[2:3, block]
        facing = side_col + side_row == 1.0
        same = (pair_col == pair_row) & facing
        cosine = part * inv_col * inv_row
        return 40.0 * (cosine - jnp.where(same, 0.3, 0.0)), facing, same

    def lose(number, loss):
        block = pl.ds(pl.multiple_of(number * step, 128), step)
        logits, facing, same = logits_of(
            gram[:, block],
            block,
            s.known_col[:, 0:1],
            s.known_col[:, 1:2],
            s.known_col[:, 2:3],
        )
        masked = jnp.where(facing, logits, -1e30)
        top = jnp.max(masked, axis=0, keepdims=True)
        total = jnp.sum(jnp.where(facing, jnp.exp(masked - top), 0.0), axis=0, keepdims=True)
        valid = known[1:2, block] >= 0.0
        log_total = jnp.where(valid, top + jnp.log(jnp.where(valid, total, 1.0)), 0.0)
        known[3:4, block] = log_total
        matched = jnp.sum(jnp.where(same, logits, 0.0), axis=0, keepdims=True)
        return loss + jnp.sum(log_total - matched, axis=1, keepdims=True)

    loss = lax.fori_loop(0, count // step, lose, jnp.zeros((1, 1), f32))
    loss_out[...] = jnp.broadcast_to(loss * (2.0 / pairs2), loss_out.shape)

    own_first = pl.ds(pl.multiple_of(me * per_short, 8), per_short)
    mine_mask = iota((per_short, count), 1) == iota((per_short, count), 0) + me * per_short

    def own_col(row):
        return jnp.sum(jnp.where(mine_mask, row, 0.0), axis=1, keepdims=True)

    inv_row, log_row = known[0:1, :], known[3:4, :]
    inv_own, log_own = own_col(inv_row), own_col(log_row)
    logits, facing, same = logits_of(
        gram[own_first, :],
        slice(None),
        inv_own,
        own_col(known[1:2, :]),
        own_col(known[2:3, :]),
    )
    pull = jnp.exp(jnp.where(facing, logits - log_own, -1e30)) + jnp.exp(
        jnp.where(facing, logits - log_row, -1e30)
    )
    pull = 40.0 * (pull - jnp.where(same, 2.0, 0.0)) * inv_row
    pull_high = pull.astype(bf16)
    pull_low = (pull - pull_high.astype(f32)).astype(bf16)
    grad_unit = jnp.concatenate(
        [nn(pull_high, n[...]) + nn(pull_low, n[...]) for n in (s.left, s.right)], axis=1
    )
    unit = firsts * inv_own
    grad_firsts = inv_own * (
        grad_unit - unit * jnp.sum(unit * grad_unit, axis=1, keepdims=True)
    )
    grad_rows = s.grad_rows
    for i in range(per_short):
        at = pl.ds(i * SHORT_LEN, 1)
        grad_rows[at, :] = grad_rows[at, :] + grad_firsts[i : i + 1, :]


    norm_sum[0] = jnp.zeros((8, width), f32)
    for k in range(chunks):
        s.second[own_rows(k), :] = second_back(k)
    patch = s.patch
    firsts = jnp.concatenate(
        [s.second[pl.ds(i * SHORT_LEN, 1), :] for i in range(per_short)], axis=0
    )
    patch[m] = jnp.concatenate([firsts[:, :half], firsts[:, half:]], axis=0).astype(bf16)
    far = net.send(patch.at[m], patch.at[m], by_side)
    near = net.send(patch.at[m], patch.at[m], by_core)
    for k in range(chunks):
        grad = grad_rows[own_rows(k), :]
        normal = s.normal_two[own_rows(k), :]
        norm_sum[0, 2:3, :] = norm_sum[0, 2:3, :] + jnp.sum(grad * normal, axis=0, keepdims=True)
        norm_sum[0, 3:4, :] = norm_sum[0, 3:4, :] + jnp.sum(grad, axis=0, keepdims=True)
    for k in range(chunks):
        gathers[k].forward()
    far.wait_recv()
    passed = net.send(patch.at[m2], patch.at[m2], by_core)
    for k in range(chunks):
        gathers[k].finish()
        net.sent(gathers[k].far)
        net.sent(gathers[k].near)
        net.sent(gathers[k].passed)
    near.wait_recv()
    passed.wait_recv()
    top_row = iota((16, width), 0) == 0
    per_chunk = BLOCK // SHORT_LEN

    def mend(model, carry):
        fresh = patch[model].astype(f32)
        for i in range(per_short):
            at = (i // per_chunk) * span + model * BLOCK + (i % per_chunk) * SHORT_LEN
            rows = pl.ds(pl.multiple_of(at, 16), 16)
            new = jnp.concatenate(
                [fresh[i : i + 1], fresh[per_short + i : per_short + i + 1]], axis=1
            )
            gb[rows, :] = jnp.where(top_row, new, gb[rows, :].astype(f32)).astype(bf16)
        return carry

    lax.fori_loop(0, n_model, mend, 0)

    def feed_back(k):
        def one(at):
            rows = pl.ds(pl.multiple_of(k * span + at, 512), 512)
            gp[rows, :] = (nt(gb[rows, :], downw[...]) * slope[rows, :]).astype(bf16)

        tiles(span, 512, one)

        def two(at):
            rows = pl.ds(pl.multiple_of(k * span + at, 512), 512)
            partial[k][pl.ds(at, 512), :] = nt(gp[rows, :], upw[...])

        tiles(span, 512, two)

    def weight_grad(target, base, rows, left, right, left_at=0):
        step = 64

        def one(at):
            part = tn(left[:, pl.ds(pl.multiple_of(left_at + at, 64), step)], right[...])
            target[pl.ds(pl.multiple_of(base + at, 16), step), :] = part.astype(bf16)

        tiles(rows, step, one)

    def begin(first, last, left, right, keep=None):
        base = made = part_at[first]
        for at in range(0, left.shape[1], 256):
            part = tn(left[:, at : at + 256], right[...]).astype(bf16)
            count = 256 if keep is None else keep
            s.grads[pl.ds(made, count), :] = part[:count]
            made += count
            while first < last and part_at[first] + part_rows[first] <= made:
                reduces[first].start()
                first += 1

    begin(0, 4, act, gb)
    scatters = pipeline([], feed_back, middle=((), (0, 1)))
    begin(4, 8, norm, gp)
    before_end = ((2, 1), (3, 2, 0, 1))
    gathers = []
    for k in range(chunks):
        steps(*before_end[k])
        grad = s.second[own_rows(k), :] + scatters[k].end()
        normal = s.normal_one[own_rows(k), :]
        norm_sum[0, 0:1, :] = norm_sum[0, 0:1, :] + jnp.sum(grad * normal, axis=0, keepdims=True)
        norm_sum[0, 1:2, :] = norm_sum[0, 1:2, :] + jnp.sum(grad, axis=0, keepdims=True)
        back = norm_back(grad, normal, s.scale_one[own_rows(k), 0:1], gain_one)
        s.second[own_rows(k), :] = back
        gm[rows_of(m, k), :] = back.astype(bf16)
        gathers.append(Gather(gm, k))
    norm_send()
    steps(3, 4, 2, NORM, 0)

    def attend_back(k):
        def unmix(at):
            rows = pl.ds(pl.multiple_of(k * span + at, 512), 512)
            s.gatt[rows, :] = nt(gm[rows, :], mixw[...]).astype(bf16)

        tiles(span, 512, unmix)

        units = [(model, h) for model in range(n_model) for h in range(heads)]
        grads_out, grads_probs = [], []
        for model, h in units:
            rows = rows_of(model, k)
            grad_out = s.gatt[rows, pl.ds((h // 2) * BLOCK, BLOCK)] * head_masks[h % 2]
            grads_out.append(grad_out)
            grads_probs.append(nt(head_parts(proj, rows, h, 2), grad_out))
        lows, grads_scores = [], []
        for unit, grad_probs in zip(units, grads_probs, strict=True):
            weight = probs[(k, *unit)]
            inner = jnp.sum(weight * grad_probs, axis=0, keepdims=True)
            lows.append(weight.astype(bf16))
            grads_scores.append((weight * (grad_probs - inner)).astype(bf16))
        outs = {}
        for i, (model, h) in enumerate(units):
            rows = rows_of(model, k)
            outs[0, model, h] = tn(grads_scores[i], head_parts(proj, rows, h, 1)) * 0.125
            outs[1, model, h] = nn(grads_scores[i], head_parts(proj, rows, h, 0)) * 0.125
            outs[2, model, h] = nn(lows[i], grads_out[i])
        for model in range(n_model):
            for part in range(3):
                for g in range(pad // BLOCK):
                    second = outs.get((part, model, 2 * g + 1))
                    if second is None:
                        second = jnp.zeros((BLOCK, BLOCK), f32)
                    both = jnp.where(first_half, outs[part, model, 2 * g], second)
                    gproj[rows_of(model, k), pl.ds(part * pad + g * BLOCK, BLOCK)] = both.astype(
                        bf16
                    )

        def one(at):
            rows = pl.ds(pl.multiple_of(k * span + at, 512), 512)
            partial[k][pl.ds(at, 512), :] = nn(gproj[rows, :], wt[...])

        tiles(span, 512, one)

    scatters = pipeline(
        gathers,
        attend_back,
        forward=((), (3, 6, 2, 5, NORM, 0, 1, 7, 4, NORM)),
        middle=((), (2, 5, 1, 7)),
        finish=((5, 1, 4), (3, 6, 0)),
        also=lambda: begin(8, 9, att, gm, cols),
    )
    begin(9, 12, gproj, x, cols)
    steps(4, NORM, 8, 3)
    before_end = ((), (6, NORM, 2))
    swap_sent(s.returned, row_sems)
    for k in range(chunks):
        steps(*before_end[k])
        grad = s.second[own_rows(k), :] + scatters[k].end()
        s.grad_in[own_rows(k), :] = grad.astype(bf16)

    def pack(at):
        rows = pl.ds(at, 256)
        s.outgoing[rows, :] = nn(s.place[rows, :], s.grad_in[...]).astype(bf16)

    tiles(slots, 256, pack)
    batch = devices // 2
    swap_some(s.outgoing, s.incoming, out_sems, 1, batch)
    s.incoming[slot_rows(me), :] = s.outgoing[slot_rows(me), :]

    tail = [0, 5, 9, 7, 4, 8, 10, 6, 11, 3, 5, 9, 7]
    rest_of_tail = [4, 8, 10, 6, 5, 11, 9, 7, 6, 8, 10, 11]
    rest_of_tail += [9, 8, 7, 10, 11, 9, 10, 8, 11, 9, 10, 11]
    if resident:
        moments = [
            pltpu.make_async_copy(first_hbm, first_out, s.load_sems.at[0]),
            pltpu.make_async_copy(second_hbm, second_out, s.load_sems.at[1]),
        ]
        for copy in moments:
            copy.start()
    for at in range(1, 2):
        steps(*tail[: 5])
        tail = tail[5 :]
        swap_some(s.outgoing, s.incoming, out_sems, at * batch, (at + 1) * batch)
    steps(*tail)
    swap_arrived(s.incoming, out_sems)
    if resident:
        for copy in moments:
            copy.wait()
        rows = table_rows // 8
        for at in range(8):
            here = pl.ds(at * rows, rows)
            first_new, second_new, step = table_update(
                s.ids[0:1, :],
                s.incoming[...],
                first_out[here, :],
                second_out[here, :],
                step_out[here, :],
                at * rows,
            )
            first_out[here, :] = first_new
            second_out[here, :] = second_new
            step_out[here, :] = step
            steps(*rest_of_tail[2 * at : 2 * at + 2])
        rest_of_tail = rest_of_tail[16:]
    steps(*rest_of_tail)
    while any(item.todo for item in reduces):
        steps(*(i for i, item in enumerate(reduces) if item.todo))
    while len(norm_done) < len(stages):
        norm_step()
    norm_out[...] = norm_sum[len(stages)]
    if not resident:
        outs = [
            pltpu.make_async_copy(sums, weight_out, s.load_sems.at[0]),
            pltpu.make_async_copy(s.incoming, incoming_out, s.load_sems.at[1]),
            pltpu.make_async_copy(s.ids, ids_hbm, s.load_sems.at[2]),
        ]
        for copy in outs:
            copy.start()
        for copy in outs:
            copy.wait()
    net.drain()
    pool_wait(0)
    swap_sent(s.asked, ask_sems)
    swap_sent(s.incoming, out_sems)


def table_update(ids, incoming, first, second, table, base):
    rows, slots = first.shape[0], incoming.shape[0]
    hot = (iota((rows, slots), 0) + base == ids).astype(f32)
    uses = jnp.sum(hot, axis=1, keepdims=True)
    row_grad = nn(hot.astype(bf16), incoming) * (1.0 / jnp.maximum(uses, 1.0))
    first_new = 0.9 * first + 0.1 * row_grad
    second_new = 0.95 * second + 0.05 * row_grad * row_grad
    scale = jnp.sqrt(second_new * (1.0 / second_fix)) + 1e-08
    return first_new, second_new, first_new * (1.0 / first_fix) / scale + 0.01 * table


def finish_kernel(
    cols,
    block_ref,
    norm_ref,
    loss_ref,
    low,
    step_ref,
    first_ref,
    second_ref,
    step_hbm,
    first_out,
    second_out,
    down_out,
    up_out,
    mix_out,
    heads_out,
    loss_out,
    *rest,
):
    norm_outs, block_out = rest[:4], rest[4]
    wide, state_sems, wide_sems = rest[5:]
    width = low.shape[1]
    states = [
        pltpu.make_async_copy(src, dst, state_sems.at[i])
        for i, (src, dst) in enumerate(
            (
                (step_ref, step_hbm),
                (first_ref, first_out),
                (second_ref, second_out),
                (block_ref, block_out),
            )
        )
    ]
    for copy in states:
        copy.start()
    loss_out[...] = loss_ref[0:1, 0:1]
    for i, out in enumerate(norm_outs):
        out[...] = norm_ref[i, :]
    starts = (0, width, 2 * width, 2 * width + cols, 3 * width)
    wides = []
    for i, out in enumerate((down_out, up_out, mix_out, heads_out)):
        count = starts[i + 1] - starts[i]
        here = pl.ds(starts[i], count)
        step = 96

        def one(at, carry, base=starts[i]):
            rows = pl.ds(pl.multiple_of(base + at * step, 16), step)
            wide[rows, :] = low[rows, :].astype(f32)
            return carry

        lax.fori_loop(0, count // step, one, 0)
        wides.append(pltpu.make_async_copy(wide.at[here], out, wide_sems.at[i]))
        wides[-1].start()
    for copy in states + wides:
        copy.wait()


def table_kernel(
    cols,
    ids_ref,
    norm_ref,
    loss_ref,
    incoming_hbm,
    weights_hbm,
    table_hbm,
    first_hbm,
    second_hbm,
    step_hbm,
    first_out,
    second_out,
    down_out,
    up_out,
    mix_out,
    heads_out,
    loss_out,
    *rest,
):
    norm_outs = rest[:4]
    incoming, low, wide, state, in_sems, out_sems, low_sems, wide_sems = rest[4:]
    slots, width = incoming.shape
    parts = in_sems.shape[1]
    rows = state.shape[1] // parts

    def tile(at):
        return pl.ds(pl.multiple_of(at * rows, 8), rows)

    def load(i, at):
        src = (first_hbm, second_hbm, table_hbm)[i]
        return pltpu.make_async_copy(
            src.at[tile(at)], state.at[i, tile(at)], in_sems.at[i, at]
        )

    def store(i, at):
        dst = (first_out, second_out, step_hbm)[i]
        return pltpu.make_async_copy(
            state.at[i, tile(at)], dst.at[tile(at)], out_sems.at[i, at]
        )

    def each_part(step):
        def one(at, carry):
            for i in range(3):
                step(i, at)
            return carry

        lax.fori_loop(0, parts, one, 0)

    named = pltpu.make_async_copy(incoming_hbm, incoming, low_sems.at[0])
    named.start()
    lows = []
    for i in range(3):
        here = pl.ds(i * width, width)
        lows.append(
            pltpu.make_async_copy(weights_hbm.at[here], low.at[here], low_sems.at[1 + i])
        )
    for copy in lows[:1]:
        copy.start()
    each_part(lambda i, at: load(i, at).start())
    for copy in lows[1:]:
        copy.start()
    loss_out[...] = loss_ref[0:1, 0:1]
    for i, out in enumerate(norm_outs):
        out[...] = norm_ref[i, :]
    named.wait()

    wides = []
    starts = (0, width, 2 * width, 2 * width + cols, 3 * width)
    for i, out in enumerate((down_out, up_out, mix_out, heads_out)):
        here = pl.ds(starts[i], starts[i + 1] - starts[i])
        wides.append(pltpu.make_async_copy(wide.at[here], out, wide_sems.at[i]))

    def widen(i):
        lows[i].wait()
        step = 96

        def one(at, carry):
            here = pl.ds(pl.multiple_of(i * width + at * step, 16), step)
            wide[here, :] = low[here, :].astype(f32)
            return carry

        lax.fori_loop(0, width // step, one, 0)
        for copy in wides[i : i + 1] if i < 2 else wides[2:]:
            copy.start()

    widen(0)

    def update(at, carry):
        for i in range(3):
            load(i, at).wait()
        here = tile(at)
        first_new, second_new, step = table_update(
            ids_ref[0:1, :],
            incoming[...],
            state[0, here, :],
            state[1, here, :],
            state[2, here, :],
            at * rows,
        )
        state[0, here, :] = first_new
        state[1, here, :] = second_new
        state[2, here, :] = step
        for i in range(3):
            store(i, at).start()
        return carry

    lax.fori_loop(0, parts, update, 0)
    widen(1)
    widen(2)
    each_part(lambda i, at: store(i, at).wait())
    for copy in wides:
        copy.wait()


def body(
    token_owner,
    token_row,
    long_len,
    short_len,
    pairing,
    embed_table,
    first_moment,
    second_moment,
    heads_weight,
    mix_weight,
    up_weight,
    down_weight,
    first_gain,
    first_shift,
    second_gain,
    second_shift,
    upper_grad,
):
    tok, width = upper_grad.shape
    n_model, n_data = lax.axis_size("mp"), lax.axis_size("dp")
    devices = n_model * n_data
    group = tok * n_model
    cols = heads_weight.shape[2]
    pad = -(-cols // BLOCK) * BLOCK
    ff = up_weight.shape[1]
    slots = devices * SLOTS
    chunks = tok // BLOCK
    span = BLOCK * n_model
    per_short = tok // SHORT_LEN
    firsts = devices * per_short
    table_rows = embed_table.shape[0]
    bits = n_data.bit_length() - 1
    vmem = pltpu.VMEM
    dma = pltpu.SemaphoreType.DMA
    shapes = dict(
        table=vmem((table_rows, width), bf16),
        wt=vmem((3 * pad, width), bf16),
        mixw=vmem((pad, width), bf16),
        upw=vmem((width, ff), bf16),
        downw=vmem((ff, width), bf16),
        upper=vmem((tok, width), bf16),
        ask=vmem((slots, 128), bf16),
        asked=vmem((slots, 128), bf16),
        place=vmem((slots, tok), bf16),
        pick=vmem((tok, slots), bf16),
        found=vmem((slots, width), bf16),
        returned=vmem((slots, width), bf16),
        x=vmem((group, width), bf16),
        proj=vmem((group, 3 * pad), bf16),
        att=vmem((group, pad), bf16),
        gatt=vmem((group, pad), bf16),
        probs=vmem((chunks, n_model, cols // HEAD, BLOCK, BLOCK), f32),
        near_send=vmem((chunks, 2, BLOCK, width), bf16),
        near_land=vmem((chunks, 2, BLOCK, width), bf16),
        far_send=vmem((chunks, BLOCK, width), bf16),
        far_land=vmem((chunks, BLOCK, width), bf16),
        scale_one=vmem((tok, 128), f32),
        norm=vmem((group, width), bf16),
        act=vmem((group, ff), bf16),
        scale_two=vmem((tok, 128), f32),
        patch=vmem((n_model, 2 * per_short, width // 2), bf16),
        pool=vmem((n_data, n_model, 2 * per_short, width // 2), bf16),
        left=vmem((firsts, width // 2), bf16),
        right=vmem((firsts, width // 2), bf16),
        gram=vmem((firsts, firsts), f32),
        known=vmem((8, firsts), f32),
        known_col=vmem((firsts, 128), f32),
        gb=vmem((group, width), bf16),
        gm=vmem((group, width), bf16),
        grad_in=vmem((tok, width), bf16),
        norm_sum=vmem((3 + bits, 8, width), f32),
        norm_land=vmem((2 + bits, 8, width), f32),
        grads=vmem((3 * width, width), bf16),
        sum_land=vmem((12, 2 * cols + 64, width // 2), bf16),
        send_sems=dma((32,)),
        recv_sems=dma((20 + 25 * bits,)),
        owner=vmem((1, group), i32),
        rowid=vmem((1, group), i32),
        long=pltpu.SMEM(long_len.shape, i32),
        short=pltpu.SMEM(short_len.shape, i32),
        pairing=vmem((1, pairing.shape[0]), i32),
        gain_one=vmem((width,), f32),
        shift_one=vmem((width,), f32),
        gain_two=vmem((width,), f32),
        shift_two=vmem((width,), f32),
        small_sems=dma((9,)),
        load_sems=dma((8,)),
        table_sems=dma((max(4, table_rows // span),)),
        ids=vmem((8, slots), i32),
        ask_sems=dma((2,)),
        row_sems=dma((2,)),
        out_sems=dma((2,)),
        pool_sems=dma((2,)),
    )
    resident = devices <= 32
    if not resident:
        shapes.update(
            wide_a=vmem((2 * group, width), f32),
            wide_b=vmem((6 * tok, width), f32),
            sums=vmem((3 * width, width), bf16),
        )
    dims = SimpleNamespace(
        resident=resident,
        n_data=n_data,
        n_model=n_model,
        names=tuple(shapes),
        tok=tok,
        width=width,
        cols=cols,
        pad=pad,
        ff=ff,
        longs=long_len.shape[1],
        shorts=short_len.shape[1],
    )
    in_vmem = pl.BlockSpec(memory_space=pltpu.VMEM)
    in_hbm = pl.BlockSpec(memory_space=pl.ANY)
    heads_rows = jnp.transpose(heads_weight, (1, 2, 0)).reshape(3 * cols, width)
    whole = jax.ShapeDtypeStruct((table_rows, width), f32)
    out_shape = (
        jax.ShapeDtypeStruct((tok, width), bf16),
        jax.ShapeDtypeStruct((8, width), f32),
        jax.ShapeDtypeStruct((8, 128), f32),
    )
    if resident:
        out_shape = (vmem((tok, width), bf16), vmem((8, width), f32), vmem((8, 128), f32))
        out_shape += (vmem((3 * width, width), bf16),) + (vmem((table_rows, width), f32),) * 3
        out_specs = (in_vmem,) * 7
    else:
        out_shape += (
            jax.ShapeDtypeStruct((3 * width, width), bf16),
            jax.ShapeDtypeStruct((slots, width), bf16),
            jax.ShapeDtypeStruct((8, slots), i32),
        )
        out_specs = (in_vmem,) * 3 + (in_hbm,) * 3
    block_out, norms, loss, *more = pl.pallas_call(
        functools.partial(layer_kernel, dims),
        out_shape=out_shape,
        in_specs=[in_hbm] * 17,
        out_specs=out_specs,
        scratch_shapes=list(shapes.values()),
        compiler_params=pltpu.CompilerParams(
            collective_id=0,
            has_side_effects=True,
            vmem_limit_bytes=(40 if resident else 63) * 2**20,
        ),
    )(
        token_owner.reshape(1, group),
        token_row.reshape(1, group),
        long_len,
        short_len,
        pairing.reshape(1, -1),
        first_gain,
        first_shift,
        second_gain,
        second_shift,
        embed_table,
        heads_rows,
        mix_weight,
        up_weight,
        down_weight,
        upper_grad,
        first_moment,
        second_moment,
    )
    out_shape = (
        (whole, whole, whole)
        + tuple(jax.ShapeDtypeStruct((rows, width), f32) for rows in (ff, width, cols, 3 * cols))
        + (jax.ShapeDtypeStruct((1, 1), f32),)
        + (jax.ShapeDtypeStruct((width,), f32),) * 4
    )
    out_specs = (in_hbm,) * 7 + (in_vmem,) * 5
    if resident:
        finished = pl.pallas_call(
            functools.partial(finish_kernel, cols),
            out_shape=out_shape + (jax.ShapeDtypeStruct((tok, width), bf16),),
            in_specs=[in_vmem] * 7,
            out_specs=out_specs + (in_hbm,),
            scratch_shapes=[vmem((3 * width, width), f32), dma((4,)), dma((4,))],
            compiler_params=pltpu.CompilerParams(vmem_limit_bytes=20 * 2**20),
        )(block_out, norms, loss, *more)
        *finished, block_out = finished
    else:
        weights, incoming, ids = more
        parts = 8
        finished = pl.pallas_call(
            functools.partial(table_kernel, cols),
            out_shape=out_shape,
            in_specs=[in_vmem] * 3 + [in_hbm] * 5,
            out_specs=out_specs,
            scratch_shapes=[
                vmem((slots, width), bf16),
                vmem((3 * width, width), bf16),
                vmem((3 * width, width), f32),
                vmem((3, table_rows, width), f32),
                dma((3, parts)),
                dma((3, parts)),
                dma((4,)),
                dma((4,)),
            ],
            compiler_params=pltpu.CompilerParams(vmem_limit_bytes=63 * 2**20),
        )(ids, norms, loss, incoming, weights, embed_table, first_moment, second_moment)
    table_step, first_new, second_new, down_grad, up_grad, mix_grad, heads_grad, loss = finished[:8]
    norm_grads = finished[8:]
    return (
        loss.reshape(()),
        block_out,
        jnp.transpose(heads_grad.reshape(3, cols, width), (2, 0, 1)),
        mix_grad,
        up_grad,
        down_grad,
        *norm_grads,
        table_step,
        first_new,
        second_new,
    )


def solution(mesh):
    rows = P(("dp", "mp"), None)
    in_specs = (
        P("dp", None),
        P("dp"),
        P("dp", None),
        P("dp", None),
        P(),
        rows,
        rows,
        rows,
        P(None, None, "mp"),
        P("mp", None),
        P(None, "mp"),
        P("mp", None),
        P(),
        P(),
        P(),
        P(),
        rows,
    )
    out_specs = (
        P(),
        rows,
        P(None, None, "mp"),
        P("mp", None),
        P(None, "mp"),
        P("mp", None),
        P(),
        P(),
        P(),
        P(),
        rows,
        rows,
        rows,
    )
    return jax.shard_map(body, mesh=mesh, in_specs=in_specs, out_specs=out_specs, check_vma=False)
```
